32 devices in a mesh: wide: 8 (over z, x), narrow: 4 (over y, core).
Axes of the slice: x: 2, y: 2, z: 4, core: 2. Of those that a mesh axis runs over, the one named last changes fastest.
Arguments:
- tokens: bfloat16 [32768, 512], P(('wide', 'narrow')), may hold values from -11 to 11
- cotangent: float32 [32768, 512], P(('wide', 'narrow')), may hold values from -6 to 6
- cells: int32 [32, 1024], P(('wide', 'narrow')), may hold values from 0 to 3, never falling along the last dimension, each value on 1 to 512 neighbouring positions
- present: int32 [32, 1024], P(('wide', 'narrow')), may hold values 0 or 1
- generate: int32 [32, 1024], P(('wide', 'narrow')), may hold values 0 or 1
- w_qkv: float32 [512, 1536], P('narrow'), may hold values from -0.25 to 0.25
- w_out: float32 [512, 512], P('narrow'), may hold values from -1 to 1
- w_up: float32 [512, 512], P('narrow'), may hold values from -0.25 to 0.25
- w_down: float32 [512, 512], P('narrow'), may hold values from -0.25 to 0.25
- vectors: float32 [9, 512], P(None, 'narrow'), may hold values from -1.5 to 3.2
- m_qkv: float32 [512, 1536], P('narrow'), may hold values from -2 to 2
- m_out: float32 [512, 512], P('narrow'), may hold values from -2 to 2
- m_up: float32 [512, 512], P('narrow'), may hold values from -2 to 2
- m_down: float32 [512, 512], P('narrow'), may hold values from -2 to 2
- m_vec: float32 [9, 512], P(None, 'narrow'), may hold values from -4 to 4
- v_qkv: float32 [512, 1536], P('narrow'), may hold values from 0.010386238 to 0.1661798
- v_out: float32 [512, 512], P('narrow'), may hold values from 0.010386238 to 0.1661798
- v_up: float32 [512, 512], P('narrow'), may hold values from 0.010386238 to 0.1661798
- v_down: float32 [512, 512], P('narrow'), may hold values from 0.010386238 to 0.1661798
- v_vec: float32 [9, 512], P(None, 'narrow'), may hold values from 0.09347615 to 1.4956183
Outputs:
- mixed: bfloat16 [32768, 512], P(('wide', 'narrow'))
- input_grad: float32 [32768, 512], P(('wide', 'narrow'))
- grad_norm: float32 [], replicated
- new_qkv: float32 [512, 1536], P('narrow')
- new_out: float32 [512, 512], P('narrow')
- new_up: float32 [512, 512], P('narrow')
- new_down: float32 [512, 512], P('narrow')
- new_vectors: float32 [9, 512], P(None, 'narrow')
- first_qkv: float32 [512, 1536], P('narrow')
- first_out: float32 [512, 512], P('narrow')
- first_up: float32 [512, 512], P('narrow')
- first_down: float32 [512, 512], P('narrow')
- first_vec: float32 [9, 512], P(None, 'narrow')
- second_qkv: float32 [512, 1536], P('narrow')
- second_out: float32 [512, 512], P('narrow')
- second_up: float32 [512, 512], P('narrow')
- second_down: float32 [512, 512], P('narrow')
- second_vec: float32 [9, 512], P(None, 'narrow')
- copy_qkv: bfloat16 [512, 1536], P('narrow')
- copy_out: bfloat16 [512, 512], P('narrow')
- copy_up: bfloat16 [512, 512], P('narrow')
- copy_down: bfloat16 [512, 512], P('narrow')
- copy_vec: bfloat16 [9, 512], P(None, 'narrow')
The draws below stay inside these ranges and needn't reach their ends.
Inputs may be any that keep to these rules, and one draw needn't show every extreme that they name: `cells`: within a row cell numbers never fall; each cell holds 1 to 512 tokens, one exactly that many.
All inputs are finite; a program needn't handle non-finite values. No bound on the sum of `present` or of `generate` on one device may be relied on, other than what follows from the above.
Results may differ from the reference program's by a relative error of at most 0.012.
Values may be sent and summed in bfloat16 or wider, within the bound.
No kernel may reach another device: no remote copies, remote signals or barrier semaphores. Data moves between devices by JAX's collectives and lax.ppermute only.
A program may use at most 192 MiB of HBM per device.

```python
import math
import jax
import jax.numpy as jnp
import numpy as np
from jax import lax

D = 512
FF = 512
HEADS = 8
HEAD_DIM = 64
TOK_DEV = 1024
CELLS = 4
STEP = 10
ROWS = 32
TOKENS = 32768
PARAMS = 1577472


def draw_tokens(key, part):
    key = jax.random.fold_in(key, 11)
    column = jnp.arange(D, dtype=jnp.float32) / (D - 1)
    base = jnp.clip(jax.random.normal(key, (TOKENS, D), jnp.float32), -6.0, 6.0)
    return (base * 0.6 * 3.0 ** column).astype(jnp.bfloat16)


def draw_vectors(key, part):
    key = jax.random.fold_in(key, 23)
    first_key, second_key = jax.random.split(key)
    column = jnp.arange(D, dtype=jnp.float32) / (D - 1)
    rising = 0.6 * 3.0 ** column
    biases = jnp.clip(0.3 * jax.random.normal(first_key, (9, D), jnp.float32), -1.5, 1.5)
    factor = jax.random.uniform(second_key, (9, D), jnp.float32, 0.8, 1.25)
    row = jnp.arange(9, dtype=jnp.int32)[:, None]
    is_gain = (row == 5) | (row == 7)
    return jnp.where(is_gain, rising[None, :] * factor, biases).astype(jnp.float32)


def plant(values, key, low, high):
    extent = values.shape
    place = [jax.random.randint(jax.random.fold_in(key, axis), (), 0, extent[axis]) for axis in range(len(extent))]
    values = values.at[tuple(place)].set(low)
    longest = extent.index(max(extent))
    place[longest] = (place[longest] + 1) % extent[longest]
    return values.at[tuple(place)].set(high)


def shard_levels(stream_key, extent, shards, smallest, top_value):
    factor_of = 1.0
    for position, blocks in shards:
        heights = jax.random.uniform(jax.random.fold_in(jax.random.fold_in(stream_key, 6), position), (blocks,), jnp.float32, smallest / len(shards), top_value / len(shards))
        factor_of = factor_of * jnp.repeat(jnp.exp(heights), extent[position] // blocks).reshape((-1,) + (1,) * (len(extent) - 1 - position))
    return factor_of


def profile(number_of, total, reach, skew):
    loads = [(1 << 20) // math.isqrt(rank ** skew) + 1 for rank in range(2, number_of + 1)]
    rest, counts = total - reach - (number_of - 1), [1] * (number_of - 1)
    while rest > 0:
        candidates = [i for i in range(number_of - 1) if counts[i] < reach]
        whole, remaining = sum([loads[i] for i in candidates]), rest
        for i in candidates:
            more = min(reach - counts[i], max(1, remaining * loads[i] // whole), rest)
            counts[i] = counts[i] + more
            rest = rest - more
    return np.array([reach] + counts)


def uneven(own_key, number_of, total, reach, slope):
    if number_of == 2:
        one = jax.random.randint(own_key, (), max(1, total - reach), min(reach, total - 1) + 1)
        return jnp.stack([one, total - one])
    lengths = jnp.asarray(profile(number_of, total, reach, slope), jnp.int32)
    couples = (number_of - 1) // 2
    donor, sink = lengths[1:1 + 2 * couples:2], lengths[2:2 + 2 * couples:2]
    room = jnp.minimum(donor - 1, reach - sink)
    shifted = jax.random.randint(jax.random.fold_in(own_key, 1), (couples,), 0, 1 << 20) % (room + 1)
    lengths = lengths.at[1:1 + 2 * couples:2].set(donor - shifted).at[2:2 + 2 * couples:2].set(sink + shifted)
    return lengths[jax.random.permutation(jax.random.fold_in(own_key, 2), number_of)]


def gaussian(stream_key, extent, scale, reach, cuts=(), held_as=jnp.bfloat16):
    factor_of = shard_levels(stream_key, extent, cuts, -0.22, 0.18) if cuts else 1.0
    values = jax.random.normal(stream_key, extent, jnp.float32) * scale * factor_of
    return jnp.minimum(jnp.maximum(values, -reach), reach).astype(held_as)


def setup_inputs(seed: int = 0) -> dict:
    key_of = jax.random.split(jax.random.key(seed), 21)
    tokens = draw_tokens(jax.random.fold_in(key_of[20], 71), 0)
    cotangent = gaussian(key_of[1], (TOKENS, D), 1.0, 6.0, ((0, 32),), jnp.float32)
    cells = jax.vmap(lambda own: jnp.searchsorted(jnp.cumsum(uneven(own, CELLS, TOK_DEV, TOK_DEV // 2, 0)), jnp.arange(TOK_DEV), side="right"))(jax.random.split(key_of[2], ROWS)).reshape((ROWS, TOK_DEV)).astype(jnp.int32)
    present = plant((jax.random.randint(key_of[3], (ROWS, TOK_DEV), 0, 25) < 24).astype(jnp.int32), jax.random.fold_in(key_of[3], 1), 0, 1)
    generate = plant((jax.random.randint(key_of[4], (ROWS, TOK_DEV), 0, 4) < 1).astype(jnp.int32), jax.random.fold_in(key_of[4], 1), 0, 1)
    w_qkv = gaussian(key_of[5], (D, 3 * D), D ** -0.5, 0.25, ((0, 4),), jnp.float32)
    w_out = gaussian(key_of[6], (D, D), (D // 16) ** -0.5, 1.0, ((0, 4),), jnp.float32)
    w_up = gaussian(key_of[7], (D, FF), D ** -0.5, 0.25, ((0, 4),), jnp.float32)
    w_down = gaussian(key_of[8], (FF, D), FF ** -0.5, 0.25, ((0, 4),), jnp.float32)
    vectors = draw_vectors(jax.random.fold_in(key_of[20], 71), 0)
    m_qkv = gaussian(key_of[10], (D, 3 * D), ((TOKENS / PARAMS) ** 0.5), 2.0, ((0, 4),), jnp.float32)
    m_out = gaussian(key_of[11], (D, D), ((TOKENS / PARAMS) ** 0.5), 2.0, ((0, 4),), jnp.float32)
    m_up = gaussian(key_of[12], (D, FF), ((TOKENS / PARAMS) ** 0.5), 2.0, ((0, 4),), jnp.float32)
    m_down = gaussian(key_of[13], (FF, D), ((TOKENS / PARAMS) ** 0.5), 2.0, ((0, 4),), jnp.float32)
    m_vec = gaussian(key_of[14], (9, D), (3 * (TOKENS / PARAMS) ** 0.5), 4.0, ((1, 4),), jnp.float32)
    v_qkv = jnp.clip(jnp.exp(math.log(0.1661798) - 2.7725887 * jax.random.uniform(key_of[15], (D, 3 * D), jnp.float32) ** shard_levels(key_of[15], (D, 3 * D), ((0, 4),), -0.2, 0.2)), 0.010386238, 0.1661798)
    v_out = jnp.clip(jnp.exp(math.log(0.1661798) - 2.7725887 * jax.random.uniform(key_of[16], (D, D), jnp.float32) ** shard_levels(key_of[16], (D, D), ((0, 4),), -0.2, 0.2)), 0.010386238, 0.1661798)
    v_up = jnp.clip(jnp.exp(math.log(0.1661798) - 2.7725887 * jax.random.uniform(key_of[17], (D, FF), jnp.float32) ** shard_levels(key_of[17], (D, FF), ((0, 4),), -0.2, 0.2)), 0.010386238, 0.1661798)
    v_down = jnp.clip(jnp.exp(math.log(0.1661798) - 2.7725887 * jax.random.uniform(key_of[18], (FF, D), jnp.float32) ** shard_levels(key_of[18], (FF, D), ((0, 4),), -0.2, 0.2)), 0.010386238, 0.1661798)
    v_vec = jnp.clip(jnp.exp(math.log(1.4956183) - 2.7725887 * jax.random.uniform(key_of[19], (9, D), jnp.float32) ** shard_levels(key_of[19], (9, D), ((1, 4),), -0.2, 0.2)), 0.09347615, 1.4956183)
    return dict(tokens=tokens, cotangent=cotangent, cells=cells, present=present, generate=generate, w_qkv=w_qkv, w_out=w_out, w_up=w_up, w_down=w_down, vectors=vectors, m_qkv=m_qkv, m_out=m_out, m_up=m_up, m_down=m_down, m_vec=m_vec, v_qkv=v_qkv, v_out=v_out, v_up=v_up, v_down=v_down, v_vec=v_vec)


@jax.custom_vjp
def low(v):
    return lax.optimization_barrier(v.astype(jnp.bfloat16)).astype(jnp.float32)

@jax.custom_vjp
def low_back(v):
    return v

def low_keep(v):
    return (low(v), None)

def low_pass(kept, grad):
    return (grad,)

def back_keep(v):
    return (v, None)

def back_low(kept, grad):
    return (low(grad),)
low.defvjp(low_keep, low_pass)
low_back.defvjp(back_keep, back_low)
HIGH = lax.Precision.HIGHEST
NORM_EPS = 1e-05
ADAM_EPS = 1e-08

def layer_norm(value, gain, shift):
    center = value - lax.optimization_barrier(jnp.mean(value, -1, keepdims=True))
    spread = lax.optimization_barrier(jnp.mean(center * center, -1, keepdims=True))
    return center * lax.rsqrt(spread + NORM_EPS) * gain + shift

def attend_block(q_block, index_block, cell_block, keys, values, cell_row, keep_key):
    positions = jnp.arange(cell_row.shape[0], dtype=jnp.int32)
    allowed = (index_block[:, None] == positions[None, :]) | (cell_block[:, None] == cell_row[None, :]) & keep_key[None, :]
    scores = jnp.einsum('bhe,khe->hbk', q_block, keys, precision=HIGH) * HEAD_DIM ** (-0.5)
    scores = low_back(scores)
    scores = jnp.where(allowed[None], scores, -1e+30)
    top = lax.optimization_barrier(jnp.max(scores, -1, keepdims=True))
    expo = jnp.exp(scores - top)
    prob = low(expo / lax.optimization_barrier(jnp.sum(expo, -1, keepdims=True)))
    return jnp.einsum('hbk,khe->bhe', prob, values, precision=HIGH)

def row_layer(x_row, params, cell_row, keep_key):
    w_qkv, w_out, w_up, w_down, vectors = [low(p) for p in params]
    length = x_row.shape[0]
    bias = jnp.concatenate([vectors[0], jnp.zeros_like(vectors[0]), vectors[1]])
    query_key_value = low_back(low(jnp.dot(x_row, w_qkv, precision=HIGH) + bias))
    queries = query_key_value[:, :D].reshape(length, HEADS, HEAD_DIM)
    keys = query_key_value[:, D:2 * D].reshape(length, HEADS, HEAD_DIM)
    values = query_key_value[:, 2 * D:].reshape(length, HEADS, HEAD_DIM)
    block = min(512, length)
    count = length // block
    index = jnp.arange(length, dtype=jnp.int32).reshape(count, block)

    def one_block(args):
        return attend_block(args[0], args[1], args[2], keys, values, cell_row, keep_key)
    attention_result = lax.map(jax.checkpoint(one_block), (queries.reshape(count, block, HEADS, HEAD_DIM), index, cell_row.reshape(count, block)))
    attention_result = low_back(low(attention_result.reshape(length, D)))
    residual_branch = low_back(jnp.dot(attention_result, w_out, precision=HIGH) + vectors[2])
    first_moment = layer_norm(x_row + residual_branch, vectors[5], vectors[6])
    preactivation = low_back(jnp.dot(low(first_moment), w_up, precision=HIGH) + vectors[3])
    hidden_activation = low(jax.nn.gelu(preactivation, approximate=False))
    down_projection_output = low_back(jnp.dot(hidden_activation, w_down, precision=HIGH) + vectors[4])
    return layer_norm(first_moment + down_projection_output, vectors[7], vectors[8])

def adamw(weight, grad, first_moment, second, rate, decay):
    first_moment = 0.5 * first_moment + 0.5 * grad
    second = 0.5 * second + 0.5 * grad * grad
    fix = 1.0 - 0.5 ** STEP
    update = first_moment / fix / (jnp.sqrt(second / fix) + ADAM_EPS)
    return (weight - rate * (update + decay * weight), first_moment, second)

def reference(tokens, cotangent, cells, present, generate, w_qkv, w_out, w_up, w_down, vectors, m_qkv, m_out, m_up, m_down, m_vec, v_qkv, v_out, v_up, v_down, v_vec):
    params = (w_qkv, w_out, w_up, w_down, vectors)
    x_rows = tokens.astype(jnp.float32).reshape(ROWS, TOK_DEV, D)
    c_rows = cotangent.reshape(ROWS, TOK_DEV, D)

    def row_step(total, inputs):
        x_row, c_row, cell_row, pres_row, gen_row = inputs
        keep_key = (pres_row == 1) & (gen_row == 0)

        def forward(xv, pv):
            return row_layer(xv, pv, cell_row, keep_key)
        out, pull = jax.vjp(forward, x_row, params)
        dx_row, dparams = pull(c_row)
        total = jax.tree.map(lambda a, b: a + b, total, dparams)
        return (total, (out.astype(jnp.bfloat16), dx_row))
    zeros = jax.tree.map(jnp.zeros_like, params)
    grads, (outs, dxs) = lax.scan(row_step, zeros, (x_rows, c_rows, cells, present, generate))
    squares = jnp.float32(0.0)
    for grad in grads:
        squares = squares + jnp.sum(grad * grad)
    grad_norm = jnp.sqrt(squares)
    limit = math.sqrt(TOKENS)
    factor = limit / jnp.maximum(grad_norm, limit)
    clipped = [g * factor for g in grads]
    firsts = (m_qkv, m_out, m_up, m_down, m_vec)
    seconds = (v_qkv, v_out, v_up, v_down, v_vec)
    news, new_firsts, new_seconds = ([], [], [])
    for number in range(5):
        rate = 0.5 if number == 4 else 0.1
        decay = 0.0 if number == 4 else 0.01
        neww, newm, newv = adamw(params[number], clipped[number], firsts[number], seconds[number], rate, decay)
        news.append(neww)
        new_firsts.append(newm)
        new_seconds.append(newv)
    return (outs.reshape(TOKENS, D), dxs.reshape(TOKENS, D), grad_norm, news[0], news[1], news[2], news[3], news[4], new_firsts[0], new_firsts[1], new_firsts[2], new_firsts[3], new_firsts[4], new_seconds[0], new_seconds[1], new_seconds[2], new_seconds[3], new_seconds[4], news[0].astype(jnp.bfloat16), news[1].astype(jnp.bfloat16), news[2].astype(jnp.bfloat16), news[3].astype(jnp.bfloat16), news[4].astype(jnp.bfloat16))
```

```python
import functools
import math

import jax
import jax.numpy as jnp
from jax import lax
from jax.experimental import pallas as pl
from jax.experimental.pallas import tpu as pltpu
from jax.sharding import PartitionSpec as P

D = 512
HEADS = 8
HEAD_DIM = 64
PAIR = 2 * HEAD_DIM
PAIRS = HEADS // 2
TRIO = 3 * PAIR
TOK_DEV = 1024
QT = 256
HALF = TOK_DEV // 2
TILES = 1
MT = 512
STEP = 10
NORM_EPS = 1e-05
ADAM_EPS = 1e-08
MASKED = -1e30
BF = jnp.bfloat16
F32 = jnp.float32
MIB = 1024 * 1024
GROUP = 2
HW = GROUP * TRIO
FORWARD_MIB, MIDDLE_MIB, BACKWARD_MIB = 16, 20, 24

NN = (((1,), (0,)), ((), ()))
NT = (((1,), (1,)), ((), ()))
TN = (((0,), (0,)), ((), ()))
TT = (((0,), (1,)), ((), ()))


def dot(a, b, dims):
    return lax.dot_general(a, b, dims, preferred_element_type=F32)


def params(mib=20):
    return pltpu.CompilerParams(vmem_limit_bytes=mib * MIB)


def sds(shape, dtype):
    return jax.ShapeDtypeStruct(shape, dtype)


SMEM = pl.BlockSpec(memory_space=pltpu.SMEM)
VM = pl.BlockSpec(memory_space=pltpu.VMEM)
ANY = pl.BlockSpec(memory_space=pl.ANY)
HBM = pl.BlockSpec(memory_space=pltpu.HBM)


def whole(shape):
    return pl.BlockSpec(shape, lambda i: (0,) * len(shape))


def cost(flops, moved, exps=0):
    return pl.CostEstimate(flops=int(flops), bytes_accessed=int(moved), transcendentals=int(exps))


def fetch(pairs, sems):
    copies = [
        pltpu.make_async_copy(source, target, sems.at[number])
        for number, (source, target) in enumerate(pairs)
    ]
    for copy in copies:
        copy.start()
    return copies


def trio_columns(base):
    return [
        (local * TRIO + t * PAIR, t * D + (base + local) * PAIR)
        for local in range(GROUP)
        for t in range(3)
    ]


def pack_first_kernel(w_hbm, vec_hbm, out_ref, w_ref, vec_ref, sems):
    rows, vec_cols = w_hbm.shape[0], vec_hbm.shape[1]
    width = GROUP * PAIR
    copies = fetch(
        [(w_hbm.at[:, t * D : t * D + width], w_ref.at[t]) for t in range(3)] + [(vec_hbm, vec_ref)], sems
    )
    for copy in copies:
        copy.wait()
    for local in range(GROUP):
        for t in range(3):
            target = local * TRIO + t * PAIR
            out_ref[:rows, target : target + PAIR] = w_ref[t, :, local * PAIR : (local + 1) * PAIR].astype(BF)
    out_ref[rows:, :] = jnp.zeros((16, HW), BF)
    vec = jnp.concatenate([vec_ref[...], jnp.zeros((7, vec_cols), F32)], 0)
    out_ref[rows:, :vec_cols] = vec.astype(BF)


def pack_first(w_qkv, vectors):
    rows = w_qkv.shape[0]
    return pl.pallas_call(
        pack_first_kernel,
        in_specs=[HBM, HBM],
        out_specs=VM,
        out_shape=sds((rows + 16, HW), BF),
        scratch_shapes=[
            pltpu.VMEM((3, rows, GROUP * PAIR), F32),
            pltpu.VMEM(vectors.shape, F32),
            pltpu.SemaphoreType.DMA((4,)),
        ],
        compiler_params=params(60),
        name="pack_first",
    )(w_qkv, vectors)


def pack_second_kernel(w_ref, w_out_ref, w_up_ref, w_down_ref, *refs):
    second_ref, rest_ref = refs[-2:]
    for target, source in trio_columns(GROUP):
        second_ref[:, target : target + PAIR] = w_ref[:, source : source + PAIR].astype(BF)
    rest_ref[:, :D] = w_out_ref[...].astype(BF)
    rest_ref[:, D : 2 * D] = w_up_ref[...].astype(BF)
    rest_ref[:, 2 * D :] = w_down_ref[...].astype(BF)


def pick(piece, lead, rows):
    return piece[rows, :] if lead is None else piece[lead, rows, :]


def assemble(order, pieces, place, w_full):
    rows = D // len(order)
    for number, (piece, lead, mask) in enumerate(order):
        at = number if mask is None else jnp.bitwise_xor(place[0], mask)
        w_full[pl.ds(pl.multiple_of(at * rows, rows), rows), :] = pick(
            pieces[piece], lead, slice(0, rows)
        )


def turn_rows(source, start, write):
    blocks = source.shape[0] // 8
    whole_blocks, rest = start >> 3, start & 7
    inside = lax.broadcasted_iota(jnp.int32, (8, source.shape[1]), 0) < 8 - rest

    def rolled(block):
        at = pl.multiple_of(((block + whole_blocks) & (blocks - 1)) * 8, 8)
        return pltpu.roll(source[pl.ds(at, 8), :], (8 - rest) & 7, 0)

    def step(i, first):
        second, third = rolled(2 * i + 1), rolled(2 * i + 2)
        write(i, jnp.where(inside, first, second), jnp.where(inside, second, third))
        return third

    lax.fori_loop(0, blocks // 2, step, rolled(0), unroll=8)


def write_into(out):
    def write(i, upper, lower):
        at = pl.multiple_of(i * 16, 16)
        out[pl.ds(at, 16), :] = jnp.concatenate([upper, lower], 0).astype(out.dtype)

    return write


def turn_tokens_kernel(tokens, both, *refs):
    tokens_out, turned_out, cells_out, start_out, wide_tokens = refs[-5:]
    cell = both[0:1, :]
    start = jnp.int32(TOK_DEV)
    for c in range(4):
        size = jnp.sum((cell == c).astype(jnp.int32))
        first = jnp.sum((cell < c).astype(jnp.int32))
        start = jnp.where(size == HALF, jnp.minimum(start, first), start)
    start_out[0] = start
    shift = jnp.where(start == 0, 0, TOK_DEV - start)
    row = lax.broadcasted_iota(jnp.int32, (8, TOK_DEV), 0)
    cells_out[...] = pltpu.roll(jnp.where(row == 0, cell, both[1:2, :]), shift, 1)
    wide_tokens[...] = tokens[...].astype(F32)
    turn_rows(wide_tokens, start, write_into(tokens_out))
    turned_out[...] = tokens_out[...].T


def turn_tokens(tokens, both, later):
    return pl.pallas_call(
        turn_tokens_kernel,
        in_specs=[VM, VM] + [ANY] * len(later),
        out_specs=[VM] * 3 + [SMEM],
        out_shape=[
            sds((TOK_DEV, D), BF),
            sds((D, TOK_DEV), BF),
            sds((8, TOK_DEV), jnp.int32),
            sds((1,), jnp.int32),
        ],
        scratch_shapes=[pltpu.VMEM((TOK_DEV, D), F32)],
        compiler_params=params(16),
        cost_estimate=cost(1e7, 3e6),
        name="turn_tokens",
    )(tokens, both, *later)


def turn_cotangent_kernel(start, cot_ref, *refs):
    turn_rows(cot_ref, start[0], write_into(refs[-1]))


def turn_cotangent(start, cot, later):
    return pl.pallas_call(
        turn_cotangent_kernel,
        in_specs=[SMEM, VM] + [ANY] * len(later),
        out_specs=VM,
        out_shape=sds((TOK_DEV, D), F32),
        compiler_params=params(16),
        cost_estimate=cost(1e7, 4e6),
        name="turn_cotangent",
    )(start, cot, *later)


def turn_back_kernel(start, grad_ref, mixed_ref, *refs):
    grad_out, mixed_out, wide_mixed = refs[-3:]
    back = (TOK_DEV - start[0]) & (TOK_DEV - 1)
    wide_mixed[...] = mixed_ref[...].astype(F32)
    turn_rows(wide_mixed, back, write_into(mixed_out))
    turn_rows(grad_ref, back, write_into(grad_out))


def turn_back(start, grad, mixed, later):
    return pl.pallas_call(
        turn_back_kernel,
        in_specs=[SMEM, VM, VM] + [ANY] * len(later),
        out_specs=[VM, VM],
        out_shape=[sds(grad.shape, F32), sds(mixed.shape, BF)],
        scratch_shapes=[pltpu.VMEM(mixed.shape, F32)],
        compiler_params=params(),
        cost_estimate=cost(1, 1),
        name="turn_back",
    )(start, grad, mixed, *later)


def make_bias(cells_ref, bias):
    for half in range(2):
        mine = slice(half * HALF, (half + 1) * HALF)
        number = lax.broadcasted_iota(jnp.int32, (16, HALF), 0)
        of_key = jnp.where(cells_ref[1:2, mine] == number, 1.0, 0.0).astype(BF)
        of_query = jnp.where(cells_ref[0:1, mine] == number, 1.0, 0.0).astype(BF)
        keys = lax.broadcasted_iota(jnp.int32, (HALF, HALF), 0)
        queries = lax.broadcasted_iota(jnp.int32, (HALF, HALF), 1)
        seen = (dot(of_key, of_query, TN) > 0.5) | (keys == queries)
        bias[mine, :] = jnp.where(seen, 0.0, MASKED)


def column_of(row):
    eye = lax.broadcasted_iota(jnp.int32, (PAIR, PAIR), 0) == lax.broadcasted_iota(
        jnp.int32, (PAIR, PAIR), 1
    )
    return jnp.sum(jnp.where(eye, row, 0.0), 1, keepdims=True)


def both_heads(pair_t):
    zero = jnp.zeros((HEAD_DIM, pair_t.shape[1]), pair_t.dtype)
    return jnp.concatenate(
        [
            jnp.concatenate([pair_t[:HEAD_DIM], zero], 0),
            jnp.concatenate([zero, pair_t[HEAD_DIM:]], 0),
        ],
        1,
    )


def forward_kernel(order, n_pieces, base, *refs):
    place, tokens, cells_ref, vec_in = refs[:4]
    pieces = refs[4 : 4 + n_pieces]
    att_out, lse_out, krow_out, vrow_out, qt_out, kt_out, w_full, vec_full, bias = refs[4 + n_pieces :]
    assemble(order, pieces, place, w_full)
    if vec_in.shape[1] == D:
        vec_full[...] = vec_in[...].astype(F32)
    else:
        rows = D // len(order)
        for piece, lead, mask in order:
            at = pl.multiple_of(jnp.bitwise_xor(place[0], mask) * rows, rows)
            vec_full[:, pl.ds(at, rows)] = pick(pieces[piece], lead, slice(rows, rows + 16))[
                :, :rows
            ].astype(F32)
    make_bias(cells_ref, bias)
    x = tokens[...]
    halves = [slice(0, HALF), slice(HALF, TOK_DEV)]
    chains = []
    for local in range(GROUP):
        lane = slice((base + local) * PAIR, (base + local + 1) * PAIR)
        w = w_full[:, local * TRIO : (local + 1) * TRIO]
        b_q = vec_full[0:1, lane]
        b_v = vec_full[1:2, lane]
        trio = dot(w, x, TT)
        rows = dot(x, w[:, PAIR:], NN)
        here = slice(local * PAIR, (local + 1) * PAIR)
        q_t = ((trio[:PAIR] + column_of(b_q)) * (HEAD_DIM**-0.5)).astype(BF)
        v_t = (trio[2 * PAIR :] + column_of(b_v)).astype(BF)
        k_row = rows[:, :PAIR].astype(BF)
        krow_out[local] = k_row
        vrow_out[local] = (rows[:, PAIR:] + b_v).astype(BF)
        qt_out[here, :] = q_t
        kt_out[here, :] = trio[PAIR : 2 * PAIR].astype(BF)
        for mine in halves:
            chains.append((local, mine, v_t, dot(k_row[mine], both_heads(q_t[:, mine]), NN)))
    for local, mine, v_t, s in chains:
        mask = bias[mine, :]
        s = s + jnp.concatenate([mask, mask], 1)
        top = jnp.max(s, 0, keepdims=True)
        e = jnp.exp(s - top)
        total = jnp.sum(e, 0, keepdims=True)
        lse = top + jnp.log(total)
        e_low = e.astype(BF)
        for h in range(2):
            cols = slice(h * HALF, (h + 1) * HALF)
            head = slice(h * HEAD_DIM, (h + 1) * HEAD_DIM)
            o = dot(v_t[head, mine], e_low[:, cols], NN)
            at = local * PAIR + h * HEAD_DIM
            att_out[at : at + HEAD_DIM, mine] = (o / total[:, cols]).astype(BF)
            lse_out[local, h : h + 1, mine] = lse[:, cols]


def forward_attention(base, place, tokens, cells, vec, pieces, order):
    wide_t, tall = sds((GROUP * PAIR, TOK_DEV), BF), sds((GROUP, TOK_DEV, PAIR), BF)
    return pl.pallas_call(
        functools.partial(forward_kernel, order, len(pieces), base),
        in_specs=[SMEM] + [VM] * (3 + len(pieces)),
        out_specs=[VM] * 8,
        out_shape=[
            wide_t, sds((GROUP, 8, TOK_DEV), F32), tall, tall, wide_t, wide_t, sds((D, HW), BF), sds((16, D), F32)
        ],
        scratch_shapes=[pltpu.VMEM((TOK_DEV, HALF), F32)],
        compiler_params=params(FORWARD_MIB),
        cost_estimate=cost(6e9, 8e6, 2**21),
        name="forward_attention",
    )(place, tokens, cells, vec, *pieces)


def normalize(value):
    center = value - jnp.mean(value, -1, keepdims=True)
    inverse = lax.rsqrt(jnp.mean(center * center, -1, keepdims=True) + NORM_EPS)
    return center * inverse, inverse


def normalize_back(grad, normal, inverse):
    return inverse * (
        grad
        - jnp.mean(grad, -1, keepdims=True)
        - normal * jnp.mean(grad * normal, -1, keepdims=True)
    )


def column_sum(value):
    return jnp.sum(value, 0, keepdims=True)


def row_sources(place, n_shards, stages):
    if not stages:
        return [(0, 0, D)]
    rows = D // n_shards
    piece = D >> len(stages)
    found = []
    for block in range(1 << len(stages)):
        masks = {"narrow": 0, "wide": 0}
        for number, (axis, mask) in enumerate(stages):
            if block >> (len(stages) - 1 - number) & 1:
                masks[axis] |= mask
        source = jnp.bitwise_xor(place[0], masks["narrow"]) * rows
        if piece < rows:
            source = source + jnp.bitwise_xor(place[1], masks["wide"]) * piece
        found.append((block * piece, pl.multiple_of(source, piece), piece))
    return found


def store_rows(outs, place, n_shards, stages, matrix, cols):
    height = outs[0].shape[0]
    for target, source, rows in row_sources(place, n_shards, stages):
        out = outs[target // height]
        at = target % height
        out[at : at + rows, cols] = matrix[pl.ds(source, rows), :].astype(BF)


def gelu_parts(value):
    density = jnp.exp(-0.5 * value * value)
    t = 1.0 / (1.0 + (0.3275911 / math.sqrt(2.0)) * jnp.abs(value))
    poly = 1.061405429
    for factor in (-1.453152027, 1.421413741, -0.284496736, 0.254829592):
        poly = poly * t + factor
    tail = 0.5 * poly * t * density
    return jnp.where(value >= 0.0, 1.0 - tail, tail), value * density * (1.0 / math.sqrt(2.0 * math.pi))


def middle_kernel(order, n_pieces, n_shards, stages, *refs):
    n_g = 2 if stages else 1
    place, tokens, cot_ref, att_a, att_b, vec_ref = refs[:6]
    pieces = refs[6 : 6 + n_pieces]
    mixed_out, dh1_out, datt_out, vec_out = refs[6 + n_pieces : 10 + n_pieces]
    g_outs = refs[10 + n_pieces : 10 + n_pieces + n_g]
    w_full, att_all, first_all, hidden_all, branch_all, pre_all, down_all, dw, sums = refs[
        10 + n_pieces + n_g :
    ]
    step = pl.program_id(0)

    @pl.when(step == 0)
    def _():
        assemble(order, pieces, place, w_full)
        sums[...] = jnp.zeros_like(sums)

    w_out, w_up, w_down = w_full[:, :D], w_full[:, D : 2 * D], w_full[:, 2 * D :]

    def vec(row):
        return vec_ref[row : row + 1, :]

    def tile(number):
        at = pl.ds(pl.multiple_of(step * (TILES * MT) + number * MT, MT), MT)
        att_t = jnp.concatenate([att_a[:, at], att_b[:, at]], 0)
        att_all[:, at] = att_t
        branch = dot(att_t, w_out, TN)
        yield
        normal_1, inverse_1 = normalize(tokens[at, :].astype(F32) + (branch + vec(2)))
        first = normal_1 * vec(5) + vec(6)
        first_low = first.astype(BF)
        first_all[at, :] = first_low
        pre = dot(first_low, w_up, NN)
        yield
        pre = pre + vec(3)
        cdf, bump = gelu_parts(pre)
        hidden = (pre * cdf).astype(BF)
        hidden_all[at, :] = hidden
        slope = cdf + bump
        down = dot(hidden, w_down, NN)
        yield
        normal_2, inverse_2 = normalize(first + (down + vec(4)))
        mixed_out[at, :] = (normal_2 * vec(7) + vec(8)).astype(BF)
        cot = cot_ref[at, :]
        d_h2 = normalize_back(cot * vec(7), normal_2, inverse_2)
        d_down = d_h2.astype(BF)
        down_all[at, :] = d_down
        d_hidden = dot(d_down, w_down, NT)
        yield
        sums[7:8, :] += column_sum(cot * normal_2)
        sums[8:9, :] += column_sum(cot)
        d_pre = (d_hidden * slope).astype(BF)
        pre_all[at, :] = d_pre
        d_up = dot(d_pre, w_up, NT)
        yield
        d_first = d_h2 + d_up
        d_h1 = normalize_back(d_first * vec(5), normal_1, inverse_1)
        dh1_out[at, :] = d_h1
        d_branch = d_h1.astype(BF)
        branch_all[at, :] = d_branch
        datt_out[:, at] = dot(w_out, d_branch, NT).astype(BF)
        yield
        sums[5:6, :] += column_sum(d_first * normal_1)
        sums[6:7, :] += column_sum(d_first)

    tiles = [tile(number) for number in range(TILES)]
    while tiles:
        tiles = [one for one in tiles if next(one, True) is None]

    @pl.when(step == pl.num_programs(0) - 1)
    def _():
        ones = jnp.ones((16, TOK_DEV), BF)
        sums[2:3, :] = dot(ones, branch_all[...], NN)[:1]
        sums[3:4, :] = dot(ones, pre_all[...], NN)[:1]
        sums[4:5, :] = dot(ones, down_all[...], NN)[:1]
        vec_out[...] = sums[...]
        dw[0] = dot(att_all[...], branch_all[...], NN)
        dw[1] = dot(first_all[...], pre_all[...], TN)
        dw[2] = dot(hidden_all[...], down_all[...], TN)
        for number in range(3):
            store_rows(
                g_outs, place, n_shards, stages, dw.at[number], slice(number * D, (number + 1) * D)
            )


def middle(place, tokens, cot, atts, vec, pieces, order, stages):
    height = TILES * MT
    g_shapes = [(D // 2, 3 * D)] * 2 if stages else [(D, 3 * D)]
    return pl.pallas_call(
        functools.partial(middle_kernel, order, len(pieces), len(order), stages),
        grid=(TOK_DEV // height,),
        in_specs=[SMEM] + [VM] * (5 + len(pieces)),
        out_specs=[VM] * (4 + len(g_shapes)),
        out_shape=[
            sds((TOK_DEV, D), BF),
            sds((TOK_DEV, D), F32),
            sds((D, TOK_DEV), BF),
            sds((16, D), F32),
        ]
        + [sds(shape, BF) for shape in g_shapes],
        scratch_shapes=[pltpu.VMEM((D, 3 * D), BF), pltpu.VMEM((D, TOK_DEV), BF)]
        + [pltpu.VMEM((TOK_DEV, D), BF)] * 5
        + [pltpu.VMEM((3, D, D), F32), pltpu.VMEM((16, D), F32)],
        compiler_params=params(MIDDLE_MIB),
        cost_estimate=cost(1e10, 1.2e7, 2**20),
        name="middle",
    )(place, tokens, cot, *atts, vec, *pieces)


def backward_kernel(n_shards, stages, base, n_before, place, cells_ref, tokens_t, vec_ref, att_ref, lse_ref,
                    krow_ref, vrow_ref, qt_ref, kt_ref, datt_ref, *refs):
    before = refs[:n_before]
    bias, dw = refs[-2:]
    n_g = 2 if stages else 1
    d_out, vec = refs[-4 - n_g : -2 - n_g]
    g_outs = refs[-2 - n_g : -2]
    make_bias(cells_ref, bias)
    vec[...] = vec_ref[...]
    halves = [slice(0, HALF), slice(HALF, TOK_DEV)]
    chains = []
    for local in range(GROUP):
        here = slice(local * PAIR, (local + 1) * PAIR)
        q_t, k_t = qt_ref[here, :], kt_ref[here, :]
        d_t = datt_ref[(base + local) * PAIR : (base + local + 1) * PAIR, :]
        k_row, v_row = krow_ref[local], vrow_ref[local]
        product = d_t.astype(F32) * att_ref[here, :].astype(F32)
        for mine in halves:
            s = dot(k_row[mine], both_heads(q_t[:, mine]), NN)
            d_prob = dot(v_row[mine], both_heads(d_t[:, mine]), NN)
            chains.append((local, mine, q_t, k_t, d_t, product, s, d_prob))
    for local, mine, q_t, k_t, d_t, product, s, d_prob in chains:
        mask = bias[mine, :]
        lse = jnp.concatenate([lse_ref[local, 0:1, mine], lse_ref[local, 1:2, mine]], 1)
        delta = jnp.concatenate(
            [column_sum(product[:HEAD_DIM, mine]), column_sum(product[HEAD_DIM:, mine])], 1
        )
        prob = jnp.exp(s + jnp.concatenate([mask, mask], 1) - lse)
        d_s = (prob * (d_prob - delta)).astype(BF)
        prob_low = prob.astype(BF)
        for h in range(2):
            cols = slice(h * HALF, (h + 1) * HALF)
            head = slice(h * HEAD_DIM, (h + 1) * HEAD_DIM)
            d_q = dot(k_t[head, mine], d_s[:, cols], NN) * (HEAD_DIM**-0.5)
            d_k = dot(q_t[head, mine], d_s[:, cols], NT)
            d_v = dot(d_t[head, mine], prob_low[:, cols], NT)
            for t, value in enumerate((d_q, d_k, d_v)):
                at = t * PAIR + h * HEAD_DIM
                d_out[local, at : at + HEAD_DIM, mine] = value.astype(BF)
    ones = jnp.ones((16, TOK_DEV), BF)
    for out, ref in zip(g_outs, before):
        out[:, : ref.shape[1]] = ref[...]
    first = before[0].shape[1] if before else 0
    for local in range(GROUP):
        pair = base + local
        trio = d_out[local]
        dw[local] = dot(tokens_t[...], trio, NT)
        at = first + local * TRIO
        store_rows(g_outs, place, n_shards, stages, dw.at[local], slice(at, at + TRIO))
        total = dot(ones, trio, NT)
        lanes = slice(pair * PAIR, (pair + 1) * PAIR)
        vec[0:1, lanes] = total[:1, :PAIR]
        vec[1:2, lanes] = total[:1, 2 * PAIR :]
    if stages and base + GROUP == PAIRS:
        height = g_outs[0].shape[0]
        rows = D // n_shards
        for target, source, count in row_sources(place, n_shards, stages):
            at = pl.multiple_of(source // rows * rows, rows)
            g_outs[target // height][target % height : target % height + count, HW:] = vec[
                :, pl.ds(at, rows)
            ].astype(BF)


def backward_attention(base, place, cells, tokens_t, vec_sums, saved, d_t, before, n_shards, stages, later):
    width = HW + (before[0].shape[1] if before else 0)
    if stages:
        width += PAIR if base + GROUP == PAIRS else 0
        shapes = [sds((D // 2, width), BF)] * 2
    else:
        shapes = [sds((D, width), BF)]
    return pl.pallas_call(
        functools.partial(backward_kernel, n_shards, stages, base, len(before)),
        in_specs=[SMEM] + [VM] * (10 + len(before)) + [ANY] * len(later),
        out_specs=[VM] * (2 + len(shapes)),
        out_shape=[sds((GROUP, TRIO, TOK_DEV), BF), sds((16, D), F32)] + shapes,
        scratch_shapes=[pltpu.VMEM((TOK_DEV, HALF), F32), pltpu.VMEM((GROUP, D, TRIO), F32)],
        compiler_params=params(BACKWARD_MIB),
        cost_estimate=cost(1e10, 8e6, 2**21),
        name="backward_attention",
    )(place, cells, tokens_t, vec_sums, *saved, d_t, *before, *later)


def input_grad_kernel(w_a, w_b, dh1_ref, trio_a, trio_b, *refs):
    out = refs[-1]
    for part in range(TOK_DEV // QT):
        here = slice(part * QT, (part + 1) * QT)
        total = None
        for w_ref, trio in ((w_a, trio_a), (w_b, trio_b)):
            term = dot(w_ref[...], jnp.concatenate([trio[0, :, here], trio[1, :, here]], 0), NN)
            total = term if total is None else total + term
        out[here, :] = dh1_ref[here, :] + total.T


def input_gradient(weights, d_h1, trios, later):
    return pl.pallas_call(
        input_grad_kernel,
        in_specs=[VM] * 5 + [ANY] * len(later),
        out_specs=VM,
        out_shape=sds((TOK_DEV, D), F32),
        compiler_params=params(24),
        cost_estimate=cost(1, 1),
        name="input_gradient",
    )(*weights, d_h1, *trios, *later)


def adam(weight, grad, first, second, rate, decay):
    first = 0.5 * first + 0.5 * grad
    second = 0.5 * second + 0.5 * grad * grad
    fix = 1.0 - 0.5**STEP
    update = first * (1.0 / fix) / (jnp.sqrt(second * (1.0 / fix)) + ADAM_EPS)
    return weight - rate * (update + decay * weight), first, second


def pair_parts(first, base):
    return [
        (slice(first + target, first + target + PAIR), 0, source) for target, source in trio_columns(base)
    ]


EARLY_PARTS = [(slice(i * D, (i + 1) * D), i + 1, 0) for i in range(3)] + pair_parts(3 * D, 0)
LATE_PARTS = pair_parts(0, GROUP)


def adam_kernel(quick, limit, place, square_ref, *refs):
    n_grads = 4 if quick else 2
    grads = refs[:n_grads]
    vec_ref = refs[n_grads]
    states = refs[n_grads + 1 : n_grads + 16]
    outs = refs[n_grads + 16 : n_grads + 36]
    norm_out = refs[-1]
    step = pl.program_id(0)
    norm = jnp.sqrt(square_ref[0:1, 0:1])
    factor = limit / jnp.maximum(norm, limit)

    def write(number, where, grad, rate, decay):
        new, first, second = adam(
            states[number][where], grad * factor, states[5 + number][where],
            states[10 + number][where], rate, decay,
        )
        outs[number][where] = new
        outs[5 + number][where] = first
        outs[10 + number][where] = second
        outs[15 + number][where] = new.astype(BF)

    height = states[0].shape[0]
    pieces = height // 16 if quick else 1
    rows = height // pieces
    for piece in range(pieces):
        if quick:
            mask = jnp.bitwise_xor(place[1], step * pieces + piece)
            at = pl.multiple_of(((mask >> 2) & 1) * 16 + ((mask >> 1) & 1) * 32, 16)
            odd = (mask & 1) == 1
        else:
            at = pl.multiple_of(step * rows, rows)
        for group, parts in enumerate((EARLY_PARTS, LATE_PARTS)):
            for cols, number, target in parts:
                if quick:
                    low, high = grads[2 * group], grads[2 * group + 1]
                    grad = jnp.where(odd, high[pl.ds(at, rows), cols], low[pl.ds(at, rows), cols])
                else:
                    grad = grads[group][pl.ds(at, rows), cols]
                where = (
                    slice(piece * rows, (piece + 1) * rows),
                    slice(target, target + cols.stop - cols.start),
                )
                write(number, where, grad.astype(F32), 0.1, 0.01)

    @pl.when(step == 0)
    def _():
        norm_out[0, 0] = norm[0, 0]
        vec_cols = states[4].shape[1]
        write(4, (slice(0, 9), slice(0, vec_cols)), vec_ref[0:9, :vec_cols].astype(F32), 0.5, 0.0)


def adam_step(place, squares, limit, grads, vec_grad, weights, firsts, seconds, quick):
    steps = 4

    def spec(value):
        if value.shape[0] == 9:
            return whole(value.shape)
        return pl.BlockSpec((value.shape[0] // steps, value.shape[1]), lambda i: (i, 0))

    state = [spec(w) for w in weights]
    shapes = [sds(w.shape, F32) for w in weights]
    return pl.pallas_call(
        functools.partial(adam_kernel, quick, limit),
        grid=(steps,),
        in_specs=[SMEM] + [VM] * (2 + len(grads)) + state * 3,
        out_specs=state * 4 + [SMEM],
        out_shape=shapes * 3 + [sds(w.shape, BF) for w in weights] + [sds((1, 1), F32)],
        compiler_params=params(),
        name="adam",
    )(place, squares, *grads, vec_grad, *weights, *firsts, *seconds)


def swap(value, axis, mask):
    size = lax.axis_size(axis)
    return lax.ppermute(value, axis, [(i, i ^ mask) for i in range(size)])


def add_low(a, b):
    return (a.astype(F32) + b.astype(F32)).astype(BF)


def after(value, *others):
    return lax.optimization_barrier((value, others))[0]


def fold(keep, arrived):
    rows = keep.shape[0] // 2
    send = add_low(keep[rows:], arrived[rows:])
    return add_low(keep[:rows], arrived[:rows]), send


def finish_kernel(place, early_ref, keep, arrived, piece_out, vec_out, square_out):
    late = add_low(keep[:, :HW], arrived[:, :HW])
    vec = keep[:, HW:].astype(F32) + arrived[:, HW:].astype(F32)
    piece_out[...] = late
    vec_out[...] = vec
    early, late = early_ref[...].astype(F32), late.astype(F32)
    total = jnp.sum(early * early) + jnp.sum(late * late)
    total = total + jnp.where(place[1] == 0, jnp.sum(vec * vec), 0.0)
    square_out[...] = jnp.full(square_out.shape, total, F32)


def finish(place, early, keep, arrived):
    return pl.pallas_call(
        finish_kernel,
        in_specs=[SMEM] + [VM] * 3,
        out_specs=[VM] * 3,
        out_shape=[sds((16, HW), BF), sds((16, PAIR), F32), sds((8, PAIR), F32)],
        compiler_params=params(),
        name="finish",
    )(place, early, keep, arrived)


def directly(value, axis, masks):
    return [swap(value, axis, mask) for mask in masks]


def four(value, others):
    return (value + others[0]) + (others[1] + others[2])


def join(held, arrived):
    return jnp.concatenate([held, arrived], 0)


def squares_of(value):
    value = value.astype(F32)
    return jnp.sum(value * value)


STAGES = (("narrow", 1), ("narrow", 2), ("wide", 1), ("wide", 2), ("wide", 4))


def body(
    tokens, cotangent, cells, present, generate,
    w_qkv, w_out, w_up, w_down, vectors,
    m_qkv, m_out, m_up, m_down, m_vec,
    v_qkv, v_out, v_up, v_down, v_vec,
):
    narrow, wide = lax.axis_size("narrow"), lax.axis_size("wide")
    quick = narrow == 4 and wide == 8
    stages = STAGES if quick else ()
    place = jnp.stack([lax.axis_index("narrow"), lax.axis_index("wide")]).astype(jnp.int32)
    shard = w_qkv.shape[0]

    low_a = pack_first(w_qkv, vectors)
    keys = jnp.where((present == 1) & (generate == 0), cells, -1)
    tokens, tokens_t, cells, start = turn_tokens(
        tokens, after(jnp.concatenate([cells, keys], 0), low_a), []
    )
    low_b, low_rest = pl.pallas_call(
        pack_second_kernel,
        in_specs=[VM] * 4 + [ANY],
        out_specs=[VM, VM],
        out_shape=[sds((shard, HW), BF), sds((shard, 3 * D), BF)],
        compiler_params=params(),
        name="pack_second",
    )(w_qkv, w_out, w_up, w_down, cells)
    if quick:
        y_a = after(swap(low_a, "narrow", 2), (tokens, low_b))
        pieces_a = [low_a, swap(low_a, "narrow", 1), y_a, swap(y_a, "narrow", 1)]
        y_b = swap(after(low_b, y_a), "narrow", 2)
        c_b = swap(low_b, "narrow", 1)
        order = [(j, None, j) for j in range(4)]
        vec = jnp.zeros((8, PAIR), BF)
    else:
        pieces_a, pieces_b = [lax.all_gather(low_a, "narrow")], [lax.all_gather(low_b, "narrow")]
        pieces_rest = [lax.all_gather(low_rest, "narrow")]
        order = [(0, j, None) for j in range(narrow)]
        vec = lax.all_gather(vectors.astype(BF), "narrow", axis=1, tiled=True)
        vec = jnp.pad(vec, ((0, 7), (0, 0)))

    *saved_a, w_a, vec_full = forward_attention(0, place, tokens, cells, vec, pieces_a, order)
    if quick:
        y_b, c_b = after(y_b, saved_a), after(c_b, saved_a)
        pieces_b = [low_b, c_b, y_b, swap(y_b, "narrow", 1)]
        y_rest = swap(after(low_rest, y_b), "narrow", 2)
        c_rest = swap(low_rest, "narrow", 1)
    *saved_b, w_b, vec_full = forward_attention(GROUP, place, tokens, cells, vec_full, pieces_b, order)
    cotangent = turn_cotangent(start, cotangent, [saved_b[0]])
    if quick:
        y_rest, c_rest = after(y_rest, (saved_b, cotangent)), after(c_rest, saved_b)
        pieces_rest = [low_rest, c_rest, y_rest, swap(y_rest, "narrow", 1)]
    mixed, d_h1, d_t, vec_sums, *g_rest = middle(
        place, tokens, cotangent, (saved_a[0], saved_b[0]), vec_full, pieces_rest, order, stages
    )
    trio_a, vec_sums, *early = backward_attention(
        0, place, cells, tokens_t, vec_sums, saved_a, d_t, g_rest, narrow, stages, []
    )
    later = []
    if quick:
        e_keep, e_send = early
        e_keep, e_send = fold(e_keep, swap(e_send, "narrow", 1))
        e_arrived = swap(e_send, "narrow", 2)
        later = [e_send]
    trio_b, vec_sums, *late = backward_attention(
        GROUP, place, cells, tokens_t, vec_sums, saved_b, d_t, [], narrow, stages, later
    )
    weights, trios = (w_a, w_b), (trio_a, trio_b)

    if quick:
        b_keep, b_send = late
        b_arrived = swap(b_send, "narrow", 1)
        e_keep, e_send = fold(e_keep, after(e_arrived, trio_b))
        e_arrived = swap(e_send, "wide", 1)
        b_keep, b_send = fold(b_keep, after(b_arrived, e_send))
        b_arrived = swap(b_send, "narrow", 2)
        turned_grad = input_gradient(weights, d_h1, trios, [b_send])
        input_grad, mixed = turn_back(start, turned_grad, mixed, [])
        b_keep, b_send = fold(b_keep, after(b_arrived, input_grad))
        b_arrived = swap(b_send, "wide", 1)
        e_keep, e_send = fold(e_keep, after(e_arrived, b_send))
        e_arrived = swap(e_send, "wide", 2)
        b_keep, b_send = fold(b_keep, after(b_arrived, e_send))
        b_arrived = swap(b_send, "wide", 2)
        e_keep, e_send = fold(e_keep, after(e_arrived, b_send))
        e_arrived = swap(e_send, "wide", 4)
        b_keep, b_send = fold(b_keep, after(b_arrived, e_send))
        b_arrived = swap(b_send, "wide", 4)
        e_low = add_low(e_keep, after(e_arrived, b_send))
        e_arrived = swap(e_low, "wide", 4)
        b_low, vec_total, squares = finish(place, e_low, b_keep, b_arrived)
        b_arrived = swap(b_low, "wide", 4)
        squares = four(squares, directly(squares, "narrow", (1, 2, 3)))
        e_low = join(e_low, after(e_arrived, squares))
        e_arrived, square = swap(e_low, "wide", 2), swap(squares, "wide", 1)
        b_low = join(b_low, after(b_arrived, e_low))
        b_arrived = swap(b_low, "wide", 2)
        squares = squares + after(square, b_low)
        e_low = join(e_low, after(e_arrived, squares))
        e_arrived, others = swap(e_low, "wide", 1), directly(squares, "wide", (2, 4, 6))
        b_low = join(b_low, after(b_arrived, e_low))
        b_arrived = swap(b_low, "wide", 1)
        squares = four(squares, after(others, b_low))
        grads = [e_low, after(e_arrived, squares), b_low, after(b_arrived, squares)]
    else:
        turned_grad = input_gradient(weights, d_h1, trios, [])
        input_grad, mixed = turn_back(start, turned_grad, mixed, [])
        vec_total = lax.psum_scatter(vec_sums, "narrow", scatter_dimension=1, tiled=True)
        vec_total = lax.psum(vec_total, "wide")
        grads = []
        for every in (early[0], late[0]):
            total = lax.psum_scatter(every, "narrow", scatter_dimension=0, tiled=True)
            grads.append(lax.psum(total.astype(F32), "wide"))
        squares = lax.psum(sum(squares_of(v) for v in grads + [vec_total]), "narrow")
        squares = jnp.full((8, PAIR), squares, F32)
    *updated, grad_norm = adam_step(
        place, squares, math.sqrt(TOK_DEV * wide * narrow), grads, vec_total,
        (w_qkv, w_out, w_up, w_down, vectors),
        (m_qkv, m_out, m_up, m_down, m_vec),
        (v_qkv, v_out, v_up, v_down, v_vec),
        quick,
    )
    return (mixed, input_grad, grad_norm[0, 0], *updated)


def solution(mesh):
    split = P(("wide", "narrow"), None)
    state = (P("narrow", None),) * 4 + (P(None, "narrow"),)
    return jax.shard_map(
        body,
        mesh=mesh,
        in_specs=(split,) * 5 + state * 3,
        out_specs=(split, split, P()) + state * 4,
        check_vma=False,
    )
```

```python
import functools
import math

import jax
import jax.numpy as jnp
from jax import lax
from jax.experimental import pallas as pl
from jax.experimental.pallas import tpu as pltpu
from jax.sharding import PartitionSpec as P

D = 512
HEADS = 8
HEAD_DIM = 64
PAIR = 2 * HEAD_DIM
PAIRS = HEADS // 2
TRIO = 3 * PAIR
TOK_DEV = 1024
QT = 256
HALF = TOK_DEV // 2
TILES = 1
MT = 512
STEP = 10
NORM_EPS = 1e-05
ADAM_EPS = 1e-08
MASKED = -1e30
HIDDEN = 16
BF = jnp.bfloat16
F32 = jnp.float32
MIB = 1024 * 1024
GROUP = 2
HW = GROUP * TRIO
FIRST = 1
LATE = (PAIRS - FIRST) * TRIO
FORWARD_MIB, MIDDLE_MIB, BACKWARD_MIB = 12, 20, 22

NN = (((1,), (0,)), ((), ()))
NT = (((1,), (1,)), ((), ()))
TN = (((0,), (0,)), ((), ()))
TT = (((0,), (1,)), ((), ()))


def dot(a, b, dims):
    return lax.dot_general(a, b, dims, preferred_element_type=F32)


def params(mib=8):
    return pltpu.CompilerParams(vmem_limit_bytes=mib * MIB)


def sds(shape, dtype):
    return jax.ShapeDtypeStruct(shape, dtype)


SMEM = pl.BlockSpec(memory_space=pltpu.SMEM)
VM = pl.BlockSpec(memory_space=pltpu.VMEM)
ANY = pl.BlockSpec(memory_space=pl.ANY)
HBM = pl.BlockSpec(memory_space=pltpu.HBM)


def whole(shape):
    return pl.BlockSpec(shape, lambda i: (0,) * len(shape))


def cost(flops, moved, exps=0):
    return pl.CostEstimate(flops=int(flops), bytes_accessed=int(moved), transcendentals=int(exps))


def fetch(pairs, sems):
    copies = [
        pltpu.make_async_copy(source, target, sems.at[number])
        for number, (source, target) in enumerate(pairs)
    ]
    for copy in copies:
        copy.start()
    return copies


def trio_columns(base):
    return [
        (local * TRIO + t * PAIR, t * D + (base + local) * PAIR)
        for local in range(GROUP)
        for t in range(3)
    ]


def pack_first_kernel(w_hbm, vec_hbm, out_ref, w_ref, vec_ref, sems):
    rows, vec_cols = w_hbm.shape[0], vec_hbm.shape[1]
    width = GROUP * PAIR
    copies = fetch(
        [(w_hbm.at[:, t * D : t * D + width], w_ref.at[t]) for t in range(3)] + [(vec_hbm, vec_ref)], sems
    )
    for copy in copies:
        copy.wait()
    for local in range(GROUP):
        for t in range(3):
            target = local * TRIO + t * PAIR
            out_ref[:rows, target : target + PAIR] = w_ref[t, :, local * PAIR : (local + 1) * PAIR].astype(BF)
    out_ref[rows:, :] = jnp.zeros((16, HW), BF)
    vec = jnp.concatenate([vec_ref[...], jnp.zeros((7, vec_cols), F32)], 0)
    out_ref[rows:, :vec_cols] = vec.astype(BF)


def pack_first(w_qkv, vectors):
    rows = w_qkv.shape[0]
    return pl.pallas_call(
        pack_first_kernel,
        in_specs=[HBM, HBM],
        out_specs=VM,
        out_shape=sds((rows + 16, HW), BF),
        scratch_shapes=[
            pltpu.VMEM((3, rows, GROUP * PAIR), F32),
            pltpu.VMEM(vectors.shape, F32),
            pltpu.SemaphoreType.DMA((4,)),
        ],
        compiler_params=params(60),
        name="pack_first",
    )(w_qkv, vectors)


def pack_second_kernel(w_ref, w_out_ref, w_up_ref, w_down_ref, *refs):
    second_ref, rest_ref = refs[-2:]
    for target, source in trio_columns(GROUP):
        second_ref[:, target : target + PAIR] = w_ref[:, source : source + PAIR].astype(BF)
    rest_ref[:, :D] = w_out_ref[...].astype(BF)
    rest_ref[:, D : 2 * D] = w_up_ref[...].astype(BF)
    rest_ref[:, 2 * D :] = w_down_ref[...].astype(BF)


def pick(piece, lead, rows):
    return piece[rows, :] if lead is None else piece[lead, rows, :]


def assemble(order, pieces, place, w_full):
    rows = D // len(order)
    for number, (piece, lead, mask) in enumerate(order):
        at = number if mask is None else jnp.bitwise_xor(place[0], mask)
        w_full[pl.ds(pl.multiple_of(at * rows, rows), rows), :] = pick(
            pieces[piece], lead, slice(0, rows)
        )


def turn_rows(source, start, write):
    blocks = source.shape[0] // 8
    whole_blocks, rest = start >> 3, start & 7
    inside = lax.broadcasted_iota(jnp.int32, (8, source.shape[1]), 0) < 8 - rest

    def rolled(block):
        at = pl.multiple_of(((block + whole_blocks) & (blocks - 1)) * 8, 8)
        return pltpu.roll(source[pl.ds(at, 8), :], (8 - rest) & 7, 0)

    def step(i, first):
        second, third = rolled(2 * i + 1), rolled(2 * i + 2)
        write(i, jnp.where(inside, first, second), jnp.where(inside, second, third))
        return third

    lax.fori_loop(0, blocks // 2, step, rolled(0), unroll=8)


def write_into(out):
    def write(i, upper, lower):
        at = pl.multiple_of(i * 16, 16)
        out[pl.ds(at, 16), :] = jnp.concatenate([upper, lower], 0).astype(out.dtype)

    return write


def turn_tokens_kernel(tokens, coded, *refs):
    tokens_out, turned_out, cells_out, start_out, wide_tokens = refs[-5:]
    seen = coded[...] < HIDDEN
    cell = jnp.where(seen, coded[...], coded[...] - HIDDEN)
    start = jnp.int32(TOK_DEV)
    for c in range(4):
        size = jnp.sum((cell == c).astype(jnp.int32))
        first = jnp.sum((cell < c).astype(jnp.int32))
        start = jnp.where(size == HALF, jnp.minimum(start, first), start)
    start_out[0] = start
    shift = jnp.where(start == 0, 0, TOK_DEV - start)
    row = lax.broadcasted_iota(jnp.int32, (8, TOK_DEV), 0)
    cells_out[...] = pltpu.roll(jnp.where((row == 0) | seen, cell, -1), shift, 1)
    wide_tokens[...] = tokens[...].astype(F32)
    turn_rows(wide_tokens, start, write_into(tokens_out))
    turned_out[...] = tokens_out[...].T


def turn_tokens(tokens, coded):
    return pl.pallas_call(
        turn_tokens_kernel,
        in_specs=[VM, VM],
        out_specs=[VM] * 3 + [SMEM],
        out_shape=[
            sds((TOK_DEV, D), BF),
            sds((D, TOK_DEV), BF),
            sds((8, TOK_DEV), jnp.int32),
            sds((1,), jnp.int32),
        ],
        scratch_shapes=[pltpu.VMEM((TOK_DEV, D), F32)],
        compiler_params=params(),
        cost_estimate=cost(1e7, 3e6),
        name="turn_tokens",
    )(tokens, coded)


def turn_cotangent_kernel(start, cot_ref, *refs):
    turn_rows(cot_ref, start[0], write_into(refs[-1]))


def turn_cotangent(start, cot, later):
    return pl.pallas_call(
        turn_cotangent_kernel,
        in_specs=[SMEM, VM] + [ANY] * len(later),
        out_specs=VM,
        out_shape=sds((TOK_DEV, D), F32),
        compiler_params=params(),
        cost_estimate=cost(1e7, 4e6),
        name="turn_cotangent",
    )(start, cot, *later)


def turn_back_kernel(start, grad_ref, mixed_ref, *refs):
    grad_out, mixed_out, wide_mixed = refs[-3:]
    back = (TOK_DEV - start[0]) & (TOK_DEV - 1)
    wide_mixed[...] = mixed_ref[...].astype(F32)
    turn_rows(wide_mixed, back, write_into(mixed_out))
    turn_rows(grad_ref, back, write_into(grad_out))


def turn_back(start, grad, mixed, later):
    return pl.pallas_call(
        turn_back_kernel,
        in_specs=[SMEM, VM, VM] + [ANY] * len(later),
        out_specs=[VM, VM],
        out_shape=[sds(grad.shape, F32), sds(mixed.shape, BF)],
        scratch_shapes=[pltpu.VMEM(mixed.shape, F32)],
        compiler_params=params(),
        cost_estimate=cost(1, 1),
        name="turn_back",
    )(start, grad, mixed, *later)


def make_bias(cells_ref, bias):
    for half in range(2):
        mine = slice(half * HALF, (half + 1) * HALF)
        number = lax.broadcasted_iota(jnp.int32, (16, HALF), 0)
        of_key = jnp.where(cells_ref[1:2, mine] == number, 1.0, 0.0).astype(BF)
        of_query = jnp.where(cells_ref[0:1, mine] == number, 1.0, 0.0).astype(BF)
        keys = lax.broadcasted_iota(jnp.int32, (HALF, HALF), 0)
        queries = lax.broadcasted_iota(jnp.int32, (HALF, HALF), 1)
        seen = (dot(of_key, of_query, TN) > 0.5) | (keys == queries)
        bias[mine, :] = jnp.where(seen, 0.0, MASKED)


def column_of(row):
    eye = lax.broadcasted_iota(jnp.int32, (PAIR, PAIR), 0) == lax.broadcasted_iota(
        jnp.int32, (PAIR, PAIR), 1
    )
    return jnp.sum(jnp.where(eye, row, 0.0), 1, keepdims=True)


def both_heads(pair_t):
    zero = jnp.zeros((HEAD_DIM, pair_t.shape[1]), pair_t.dtype)
    return jnp.concatenate(
        [
            jnp.concatenate([pair_t[:HEAD_DIM], zero], 0),
            jnp.concatenate([zero, pair_t[HEAD_DIM:]], 0),
        ],
        1,
    )


def forward_kernel(order, n_pieces, base, *refs):
    place, tokens, cells_ref, vec_in = refs[:4]
    pieces = refs[4 : 4 + n_pieces]
    att_out, lse_out, krow_out, vrow_out, qt_out, kt_out, w_full, vec_full, bias = refs[4 + n_pieces :]
    assemble(order, pieces, place, w_full)
    if vec_in.shape[1] == D:
        vec_full[...] = vec_in[...].astype(F32)
    else:
        rows = D // len(order)
        for piece, lead, mask in order:
            at = pl.multiple_of(jnp.bitwise_xor(place[0], mask) * rows, rows)
            vec_full[:, pl.ds(at, rows)] = pick(pieces[piece], lead, slice(rows, rows + 16))[
                :, :rows
            ].astype(F32)
    make_bias(cells_ref, bias)
    x = tokens[...]
    halves = [slice(0, HALF), slice(HALF, TOK_DEV)]
    chains = []
    for local in range(GROUP):
        lane = slice((base + local) * PAIR, (base + local + 1) * PAIR)
        w = w_full[:, local * TRIO : (local + 1) * TRIO]
        b_q = vec_full[0:1, lane]
        b_v = vec_full[1:2, lane]
        trio = dot(w, x, TT)
        rows = dot(x, w[:, PAIR:], NN)
        here = slice(local * PAIR, (local + 1) * PAIR)
        q_t = ((trio[:PAIR] + column_of(b_q)) * (HEAD_DIM**-0.5)).astype(BF)
        v_t = (trio[2 * PAIR :] + column_of(b_v)).astype(BF)
        k_row = rows[:, :PAIR].astype(BF)
        krow_out[local] = k_row
        vrow_out[local] = (rows[:, PAIR:] + b_v).astype(BF)
        qt_out[here, :] = q_t
        kt_out[here, :] = trio[PAIR : 2 * PAIR].astype(BF)
        for mine in halves:
            chains.append((local, mine, v_t, dot(k_row[mine], both_heads(q_t[:, mine]), NN)))
    for local, mine, v_t, s in chains:
        mask = bias[mine, :]
        s = s + jnp.concatenate([mask, mask], 1)
        top = jnp.max(s, 0, keepdims=True)
        e = jnp.exp(s - top)
        total = jnp.sum(e, 0, keepdims=True)
        lse = top + jnp.log(total)
        e_low = e.astype(BF)
        for h in range(2):
            cols = slice(h * HALF, (h + 1) * HALF)
            head = slice(h * HEAD_DIM, (h + 1) * HEAD_DIM)
            o = dot(v_t[head, mine], e_low[:, cols], NN)
            at = local * PAIR + h * HEAD_DIM
            att_out[at : at + HEAD_DIM, mine] = (o / total[:, cols]).astype(BF)
            lse_out[local, h : h + 1, mine] = lse[:, cols]


def forward_attention(base, place, tokens, cells, vec, pieces, order):
    wide_t, tall = sds((GROUP * PAIR, TOK_DEV), BF), sds((GROUP, TOK_DEV, PAIR), BF)
    return pl.pallas_call(
        functools.partial(forward_kernel, order, len(pieces), base),
        in_specs=[SMEM] + [VM] * (3 + len(pieces)),
        out_specs=[VM] * 8,
        out_shape=[
            wide_t, sds((GROUP, 8, TOK_DEV), F32), tall, tall, wide_t, wide_t, sds((D, HW), BF), sds((16, D), F32)
        ],
        scratch_shapes=[pltpu.VMEM((TOK_DEV, HALF), F32)],
        compiler_params=params(FORWARD_MIB),
        cost_estimate=cost(6e9, 8e6, 2**21),
        name="forward_attention",
    )(place, tokens, cells, vec, *pieces)


def normalize(value):
    center = value - jnp.mean(value, -1, keepdims=True)
    inverse = lax.rsqrt(jnp.mean(center * center, -1, keepdims=True) + NORM_EPS)
    return center * inverse, inverse


def normalize_back(grad, normal, inverse):
    return inverse * (
        grad
        - jnp.mean(grad, -1, keepdims=True)
        - normal * jnp.mean(grad * normal, -1, keepdims=True)
    )


def column_sum(value):
    return jnp.sum(value, 0, keepdims=True)


def row_sources(place, n_shards, stages):
    if not stages:
        return [(0, 0, D)]
    rows = D // n_shards
    piece = D >> len(stages)
    found = []
    for block in range(1 << len(stages)):
        masks = {"narrow": 0, "wide": 0}
        for number, (axis, mask) in enumerate(stages):
            if block >> (len(stages) - 1 - number) & 1:
                masks[axis] |= mask
        source = jnp.bitwise_xor(place[0], masks["narrow"]) * rows
        if piece < rows:
            source = source + jnp.bitwise_xor(place[1], masks["wide"]) * piece
        found.append((block * piece, pl.multiple_of(source, piece), piece))
    return found


def store_rows(outs, place, n_shards, stages, matrix, cols):
    height = outs[0].shape[0]
    for target, source, rows in row_sources(place, n_shards, stages):
        out = outs[target // height]
        at = target % height
        out[at : at + rows, cols] = matrix[pl.ds(source, rows), :].astype(BF)


def gelu_parts(value):
    density = jnp.exp(-0.5 * value * value)
    t = 1.0 / (1.0 + (0.3275911 / math.sqrt(2.0)) * jnp.abs(value))
    poly = 1.061405429
    for factor in (-1.453152027, 1.421413741, -0.284496736, 0.254829592):
        poly = poly * t + factor
    tail = 0.5 * poly * t * density
    return jnp.where(value >= 0.0, 1.0 - tail, tail), value * density * (1.0 / math.sqrt(2.0 * math.pi))


def middle_kernel(order, n_pieces, n_shards, stages, *refs):
    n_g = 2 if stages else 1
    place, tokens, cot_ref, att_a, att_b, vec_ref = refs[:6]
    pieces = refs[6 : 6 + n_pieces]
    mixed_out, dh1_out, datt_out, vec_out = refs[6 + n_pieces : 10 + n_pieces]
    g_outs = refs[10 + n_pieces : 10 + n_pieces + n_g]
    w_full, att_all, first_all, hidden_all, branch_all, pre_all, down_all, dw, sums = refs[
        10 + n_pieces + n_g :
    ]
    step = pl.program_id(0)

    @pl.when(step == 0)
    def _():
        assemble(order, pieces, place, w_full)
        sums[...] = jnp.zeros_like(sums)

    w_out, w_up, w_down = w_full[:, :D], w_full[:, D : 2 * D], w_full[:, 2 * D :]

    def vec(row):
        return vec_ref[row : row + 1, :]

    def tile(number):
        at = pl.ds(pl.multiple_of(step * (TILES * MT) + number * MT, MT), MT)
        att_t = jnp.concatenate([att_a[:, at], att_b[:, at]], 0)
        att_all[:, at] = att_t
        branch = dot(att_t, w_out, TN)
        yield
        normal_1, inverse_1 = normalize(tokens[at, :].astype(F32) + (branch + vec(2)))
        first = normal_1 * vec(5) + vec(6)
        first_low = first.astype(BF)
        first_all[at, :] = first_low
        pre = dot(first_low, w_up, NN)
        yield
        pre = pre + vec(3)
        cdf, bump = gelu_parts(pre)
        hidden = (pre * cdf).astype(BF)
        hidden_all[at, :] = hidden
        slope = cdf + bump
        down = dot(hidden, w_down, NN)
        yield
        normal_2, inverse_2 = normalize(first + (down + vec(4)))
        mixed_out[at, :] = (normal_2 * vec(7) + vec(8)).astype(BF)
        cot = cot_ref[at, :]
        d_h2 = normalize_back(cot * vec(7), normal_2, inverse_2)
        d_down = d_h2.astype(BF)
        down_all[at, :] = d_down
        d_hidden = dot(d_down, w_down, NT)
        yield
        sums[7:8, :] += column_sum(cot * normal_2)
        sums[8:9, :] += column_sum(cot)
        d_pre = (d_hidden * slope).astype(BF)
        pre_all[at, :] = d_pre
        d_up = dot(d_pre, w_up, NT)
        yield
        d_first = d_h2 + d_up
        d_h1 = normalize_back(d_first * vec(5), normal_1, inverse_1)
        dh1_out[at, :] = d_h1
        d_branch = d_h1.astype(BF)
        branch_all[at, :] = d_branch
        datt_out[:, at] = dot(w_out, d_branch, NT).astype(BF)
        yield
        sums[5:6, :] += column_sum(d_first * normal_1)
        sums[6:7, :] += column_sum(d_first)

    tiles = [tile(number) for number in range(TILES)]
    while tiles:
        tiles = [one for one in tiles if next(one, True) is None]

    @pl.when(step == pl.num_programs(0) - 1)
    def _():
        ones = jnp.ones((16, TOK_DEV), BF)
        sums[2:3, :] = dot(ones, branch_all[...], NN)[:1]
        sums[3:4, :] = dot(ones, pre_all[...], NN)[:1]
        sums[4:5, :] = dot(ones, down_all[...], NN)[:1]
        vec_out[...] = sums[...]
        dw[0] = dot(att_all[...], branch_all[...], NN)
        dw[1] = dot(first_all[...], pre_all[...], TN)
        dw[2] = dot(hidden_all[...], down_all[...], TN)
        for number in range(3):
            store_rows(
                g_outs, place, n_shards, stages, dw.at[number], slice(number * D, (number + 1) * D)
            )


def middle(place, tokens, cot, atts, vec, pieces, order, stages):
    height = TILES * MT
    g_shapes = [(D // 2, 3 * D)] * 2 if stages else [(D, 3 * D)]
    return pl.pallas_call(
        functools.partial(middle_kernel, order, len(pieces), len(order), stages),
        grid=(TOK_DEV // height,),
        in_specs=[SMEM] + [VM] * (5 + len(pieces)),
        out_specs=[VM] * (4 + len(g_shapes)),
        out_shape=[
            sds((TOK_DEV, D), BF),
            sds((TOK_DEV, D), F32),
            sds((D, TOK_DEV), BF),
            sds((16, D), F32),
        ]
        + [sds(shape, BF) for shape in g_shapes],
        scratch_shapes=[pltpu.VMEM((D, 3 * D), BF), pltpu.VMEM((D, TOK_DEV), BF)]
        + [pltpu.VMEM((TOK_DEV, D), BF)] * 5
        + [pltpu.VMEM((3, D, D), F32), pltpu.VMEM((16, D), F32)],
        compiler_params=params(MIDDLE_MIB),
        cost_estimate=cost(1e10, 1.2e7, 2**20),
        name="middle",
    )(place, tokens, cot, *atts, vec, *pieces)


def backward_kernel(n_shards, stages, plan, n_sets, n_before, last, place, cells_ref, tokens_t, vec_ref,
                    datt_ref, *refs):
    sets = [refs[6 * number : 6 * (number + 1)] for number in range(n_sets)]
    before = refs[6 * n_sets : 6 * n_sets + n_before]
    bias, dw = refs[-2:]
    n_g = 2 if stages else 1
    d_out, vec = refs[-4 - n_g : -2 - n_g]
    g_outs = refs[-2 - n_g : -2]
    make_bias(cells_ref, bias)
    vec[...] = vec_ref[...]
    halves = [slice(0, HALF), slice(HALF, TOK_DEV)]
    chains = []
    for place_out, (number, local, pair) in enumerate(plan):
        att_ref, lse_ref, krow_ref, vrow_ref, qt_ref, kt_ref = sets[number]
        here = slice(local * PAIR, (local + 1) * PAIR)
        q_t, k_t = qt_ref[here, :], kt_ref[here, :]
        d_t = datt_ref[pair * PAIR : (pair + 1) * PAIR, :]
        k_row, v_row = krow_ref[local], vrow_ref[local]
        product = d_t.astype(F32) * att_ref[here, :].astype(F32)
        for mine in halves:
            s = dot(k_row[mine], both_heads(q_t[:, mine]), NN)
            d_prob = dot(v_row[mine], both_heads(d_t[:, mine]), NN)
            lse = jnp.concatenate([lse_ref[local, 0:1, mine], lse_ref[local, 1:2, mine]], 1)
            chains.append((place_out, mine, q_t, k_t, d_t, product, s, d_prob, lse))
    for place_out, mine, q_t, k_t, d_t, product, s, d_prob, lse in chains:
        mask = bias[mine, :]
        delta = jnp.concatenate(
            [column_sum(product[:HEAD_DIM, mine]), column_sum(product[HEAD_DIM:, mine])], 1
        )
        prob = jnp.exp(s + jnp.concatenate([mask, mask], 1) - lse)
        d_s = (prob * (d_prob - delta)).astype(BF)
        prob_low = prob.astype(BF)
        for h in range(2):
            cols = slice(h * HALF, (h + 1) * HALF)
            head = slice(h * HEAD_DIM, (h + 1) * HEAD_DIM)
            d_q = dot(k_t[head, mine], d_s[:, cols], NN) * (HEAD_DIM**-0.5)
            d_k = dot(q_t[head, mine], d_s[:, cols], NT)
            d_v = dot(d_t[head, mine], prob_low[:, cols], NT)
            for t, value in enumerate((d_q, d_k, d_v)):
                at = t * PAIR + h * HEAD_DIM
                d_out[place_out, at : at + HEAD_DIM, mine] = value.astype(BF)
    ones = jnp.ones((16, TOK_DEV), BF)
    for out, ref in zip(g_outs, before):
        out[:, : ref.shape[1]] = ref[...]
    first = before[0].shape[1] if before else 0
    for place_out, (number, local, pair) in enumerate(plan):
        trio = d_out[place_out]
        dw[place_out] = dot(tokens_t[...], trio, NT)
        at = first + place_out * TRIO
        store_rows(g_outs, place, n_shards, stages, dw.at[place_out], slice(at, at + TRIO))
        total = dot(ones, trio, NT)
        lanes = slice(pair * PAIR, (pair + 1) * PAIR)
        vec[0:1, lanes] = total[:1, :PAIR]
        vec[1:2, lanes] = total[:1, 2 * PAIR :]
    if stages and last:
        height = g_outs[0].shape[0]
        rows = D // n_shards
        for target, source, count in row_sources(place, n_shards, stages):
            at = pl.multiple_of(source // rows * rows, rows)
            g_outs[target // height][target % height : target % height + count, LATE:] = vec[
                :, pl.ds(at, rows)
            ].astype(BF)


def backward_attention(plan, last, place, cells, tokens_t, vec_sums, sets, d_t, before, n_shards, stages, later):
    width = len(plan) * TRIO + (before[0].shape[1] if before else 0)
    if stages:
        shapes = [sds((D // 2, width + (PAIR if last else 0)), BF)] * 2
    else:
        shapes = [sds((D, width), BF)]
    flat = [value for saved in sets for value in saved]
    return pl.pallas_call(
        functools.partial(backward_kernel, n_shards, stages, plan, len(sets), len(before), last),
        in_specs=[SMEM] + [VM] * (4 + len(flat) + len(before)) + [ANY] * len(later),
        out_specs=[VM] * (2 + len(shapes)),
        out_shape=[sds((len(plan), TRIO, TOK_DEV), BF), sds((16, D), F32)] + shapes,
        scratch_shapes=[pltpu.VMEM((TOK_DEV, HALF), F32), pltpu.VMEM((len(plan), D, TRIO), F32)],
        compiler_params=params(BACKWARD_MIB),
        cost_estimate=cost(5e9 * len(plan), 8e6, 2**21),
        name="backward_attention",
    )(place, cells, tokens_t, vec_sums, d_t, *flat, *before, *later)


def input_grad_kernel(w_a, w_b, dh1_ref, trio_a, trio_b, *refs):
    out = refs[-1]
    trios = [ref.at[number] for ref in (trio_a, trio_b) for number in range(ref.shape[0])]
    for tile in range(TOK_DEV // QT):
        here = slice(tile * QT, (tile + 1) * QT)
        total = None
        for w_ref, trio in ((w_a, trios[:GROUP]), (w_b, trios[GROUP:])):
            term = dot(w_ref[...], jnp.concatenate([part[:, here] for part in trio], 0), NN)
            total = term if total is None else total + term
        out[here, :] = dh1_ref[here, :] + total.T


def input_gradient(weights, d_h1, trios, later):
    return pl.pallas_call(
        input_grad_kernel,
        in_specs=[VM] * 5 + [ANY] * len(later),
        out_specs=VM,
        out_shape=sds((TOK_DEV, D), F32),
        compiler_params=params(),
        cost_estimate=cost(1, 1),
        name="input_gradient",
    )(*weights, d_h1, *trios, *later)


def adam(weight, grad, first, second, rate, decay):
    first = 0.5 * first + 0.5 * grad
    second = 0.5 * second + 0.5 * grad * grad
    fix = 1.0 - 0.5**STEP
    update = first * (1.0 / fix) / (jnp.sqrt(second * (1.0 / fix)) + ADAM_EPS)
    return weight - rate * (update + decay * weight), first, second


def pair_parts(first, pairs):
    return [
        (slice(at, at + PAIR), 0, t * D + pair * PAIR)
        for number, pair in enumerate(pairs)
        for t in range(3)
        for at in [first + number * TRIO + t * PAIR]
    ]


EARLY_PARTS = [(slice(i * D, (i + 1) * D), i + 1, 0) for i in range(3)] + pair_parts(3 * D, range(FIRST))
LATE_PARTS = pair_parts(0, range(FIRST, PAIRS))


def adam_kernel(quick, limit, place, square_ref, *refs):
    n_grads = 4 if quick else 2
    grads = refs[:n_grads]
    vec_ref = refs[n_grads]
    states = refs[n_grads + 1 : n_grads + 16]
    outs = refs[n_grads + 16 : n_grads + 36]
    norm_out = refs[-1]
    step = pl.program_id(0)
    norm = jnp.sqrt(square_ref[0:1, 0:1])
    factor = limit / jnp.maximum(norm, limit)

    def write(number, where, grad, rate, decay):
        new, first, second = adam(
            states[number][where], grad * factor, states[5 + number][where],
            states[10 + number][where], rate, decay,
        )
        outs[number][where] = new
        outs[5 + number][where] = first
        outs[10 + number][where] = second
        outs[15 + number][where] = new.astype(BF)

    height = states[0].shape[0]
    pieces = height // 16 if quick else 1
    rows = height // pieces
    for piece in range(pieces):
        if quick:
            mask = jnp.bitwise_xor(place[1], step * pieces + piece)
            at = pl.multiple_of(((mask >> 2) & 1) * 16 + ((mask >> 1) & 1) * 32, 16)
            odd = (mask & 1) == 1
        else:
            at = pl.multiple_of(step * rows, rows)
        for group, parts in enumerate((EARLY_PARTS, LATE_PARTS)):
            for cols, number, target in parts:
                if quick:
                    low, high = grads[2 * group], grads[2 * group + 1]
                    grad = jnp.where(odd, high[pl.ds(at, rows), cols], low[pl.ds(at, rows), cols])
                else:
                    grad = grads[group][pl.ds(at, rows), cols]
                where = (
                    slice(piece * rows, (piece + 1) * rows),
                    slice(target, target + cols.stop - cols.start),
                )
                write(number, where, grad.astype(F32), 0.1, 0.01)

    @pl.when(step == 0)
    def _():
        norm_out[0, 0] = norm[0, 0]
        vec_cols = states[4].shape[1]
        write(4, (slice(0, 9), slice(0, vec_cols)), vec_ref[0:9, :vec_cols].astype(F32), 0.5, 0.0)


def adam_step(place, squares, limit, grads, vec_grad, weights, firsts, seconds, quick):
    steps = 4

    def spec(value):
        if value.shape[0] == 9:
            return whole(value.shape)
        return pl.BlockSpec((value.shape[0] // steps, value.shape[1]), lambda i: (i, 0))

    state = [spec(w) for w in weights]
    shapes = [sds(w.shape, F32) for w in weights]
    return pl.pallas_call(
        functools.partial(adam_kernel, quick, limit),
        grid=(steps,),
        in_specs=[SMEM] + [VM] * (2 + len(grads)) + state * 3,
        out_specs=state * 4 + [SMEM],
        out_shape=shapes * 3 + [sds(w.shape, BF) for w in weights] + [sds((1, 1), F32)],
        compiler_params=params(),
        name="adam",
    )(place, squares, *grads, vec_grad, *weights, *firsts, *seconds)


def swap(value, axis, mask):
    size = lax.axis_size(axis)
    return lax.ppermute(value, axis, [(i, i ^ mask) for i in range(size)])


def add_low(a, b):
    return (a.astype(F32) + b.astype(F32)).astype(BF)


def after(value, *others):
    return lax.optimization_barrier((value, others))[0]


def fold(keep, arrived):
    rows = keep.shape[0] // 2
    send = add_low(keep[rows:], arrived[rows:])
    return add_low(keep[:rows], arrived[:rows]), send


def squares_kernel(place, early, late, vec, out):
    total = []
    for piece in range(4):
        rows = slice(16 * piece, 16 * (piece + 1))
        first, second = early[rows, :].astype(F32), late[rows, :].astype(F32)
        total.append(jnp.sum(first * first) + jnp.sum(second * second))
    total = (total[0] + total[1]) + (total[2] + total[3])
    total = total + jnp.where((place[1] & 1) == 0, jnp.sum(vec[...] * vec[...]), 0.0)
    out[...] = jnp.full(out.shape, total, F32)


def half_squares(place, early, late, vec):
    return pl.pallas_call(
        squares_kernel,
        in_specs=[SMEM] + [VM] * 3,
        out_specs=VM,
        out_shape=sds((8, PAIR), F32),
        compiler_params=params(),
        cost_estimate=cost(1, 1),
        name="half_squares",
    )(place, early, late, vec)


def directly(value, axis, masks):
    return [swap(value, axis, mask) for mask in masks]


def four(value, others):
    return (value + others[0]) + (others[1] + others[2])


def join(held, arrived):
    return jnp.concatenate([held, arrived], 0)


def squares_of(value):
    value = value.astype(F32)
    return jnp.sum(value * value)


STAGES = (("narrow", 1), ("narrow", 2), ("wide", 1), ("wide", 2), ("wide", 4))


def body(
    tokens, cotangent, cells, present, generate,
    w_qkv, w_out, w_up, w_down, vectors,
    m_qkv, m_out, m_up, m_down, m_vec,
    v_qkv, v_out, v_up, v_down, v_vec,
):
    narrow, wide = lax.axis_size("narrow"), lax.axis_size("wide")
    quick = narrow == 4 and wide == 8
    stages = STAGES if quick else ()
    place = jnp.stack([lax.axis_index("narrow"), lax.axis_index("wide")]).astype(jnp.int32)
    shard = w_qkv.shape[0]

    low_a = pack_first(w_qkv, vectors)
    coded = jnp.where((present == 1) & (generate == 0), cells, cells + HIDDEN)
    tokens, tokens_t, cells, start = turn_tokens(tokens, after(coded, low_a))
    low_b, low_rest = pl.pallas_call(
        pack_second_kernel,
        in_specs=[VM] * 4 + [ANY],
        out_specs=[VM, VM],
        out_shape=[sds((shard, HW), BF), sds((shard, 3 * D), BF)],
        compiler_params=params(),
        name="pack_second",
    )(w_qkv, w_out, w_up, w_down, cells)
    if quick:
        y_a = after(swap(low_a, "narrow", 2), (tokens, low_b))
        pieces_a = [low_a, swap(low_a, "narrow", 1), y_a, swap(y_a, "narrow", 1)]
        y_b = swap(after(low_b, y_a), "narrow", 2)
        c_b = swap(low_b, "narrow", 1)
        order = [(j, None, j) for j in range(4)]
        vec = jnp.zeros((8, PAIR), BF)
    else:
        pieces_a, pieces_b = [lax.all_gather(low_a, "narrow")], [lax.all_gather(low_b, "narrow")]
        pieces_rest = [lax.all_gather(low_rest, "narrow")]
        order = [(0, j, None) for j in range(narrow)]
        vec = lax.all_gather(vectors.astype(BF), "narrow", axis=1, tiled=True)
        vec = jnp.pad(vec, ((0, 7), (0, 0)))

    *saved_a, w_a, vec_full = forward_attention(0, place, tokens, cells, vec, pieces_a, order)
    if quick:
        y_b, c_b = after(y_b, saved_a), after(c_b, saved_a)
        pieces_b = [low_b, c_b, y_b, swap(y_b, "narrow", 1)]
        y_rest = swap(after(low_rest, y_b), "narrow", 2)
        c_rest = swap(low_rest, "narrow", 1)
    *saved_b, w_b, vec_full = forward_attention(GROUP, place, tokens, cells, vec_full, pieces_b, order)
    cotangent = turn_cotangent(start, cotangent, [saved_b[0]])
    if quick:
        y_rest, c_rest = after(y_rest, (saved_b, cotangent)), after(c_rest, saved_b)
        pieces_rest = [low_rest, c_rest, y_rest, swap(y_rest, "narrow", 1)]
    mixed, d_h1, d_t, vec_sums, *g_rest = middle(
        place, tokens, cotangent, (saved_a[0], saved_b[0]), vec_full, pieces_rest, order, stages
    )
    sets = [saved_a, saved_b]
    plan = [(pair // GROUP, pair % GROUP, pair) for pair in range(PAIRS)]
    trio_a, vec_sums, *early = backward_attention(
        plan[:FIRST], False, place, cells, tokens_t, vec_sums, sets, d_t, g_rest, narrow, stages, []
    )
    later = []
    if quick:
        e_keep, e_send = early
        e_keep, e_send = fold(e_keep, swap(e_send, "narrow", 1))
        e_arrived = swap(e_send, "narrow", 2)
        later = [e_send]
    trio_b, vec_sums, *late = backward_attention(
        plan[FIRST:], True, place, cells, tokens_t, vec_sums, sets, d_t, [], narrow, stages, later
    )
    weights, trios = (w_a, w_b), (trio_a, trio_b)

    if quick:
        b_keep, b_send = late
        b_arrived = swap(b_send, "narrow", 1)
        turned_grad = input_gradient(weights, d_h1, trios, [])
        e_keep, e_send = fold(e_keep, after(e_arrived, turned_grad))
        e_arrived = swap(e_send, "wide", 1)
        b_keep, b_send = fold(b_keep, after(b_arrived, e_send))
        b_arrived = swap(b_send, "narrow", 2)
        input_grad, mixed = turn_back(start, turned_grad, mixed, [b_send])
        e_keep, e_send = fold(e_keep, after(e_arrived, input_grad))
        e_arrived = swap(e_send, "wide", 2)
        b_keep, b_send = fold(b_keep, after(b_arrived, e_send))
        b_arrived = swap(b_send, "wide", 1)
        e_keep, e_send = fold(e_keep, after(e_arrived, b_send))
        e_arrived = swap(e_send, "wide", 4)
        b_keep, b_send = fold(b_keep, after(b_arrived, e_send))
        b_arrived = swap(b_send, "wide", 2)
        e_low = add_low(e_keep, after(e_arrived, b_send))
        e_arrived = swap(e_low, "wide", 4)
        b_keep, b_send = fold(b_keep, after(b_arrived, e_low))
        b_arrived = swap(b_send, "wide", 4)
        e_low = join(e_low, after(e_arrived, b_send))
        e_arrived = swap(e_low, "wide", 2)
        b_arrived = after(b_arrived, e_low)
        vec_total = b_keep[:, LATE:].astype(F32) + b_arrived[:, LATE:].astype(F32)
        b_low = add_low(b_keep[:, :LATE], b_arrived[:, :LATE])
        b_arrived = swap(b_low, "wide", 4)
        e_low = join(e_low, after(e_arrived, b_low))
        b_low = join(b_low, after(b_arrived, e_low))
        b_low = join(b_low, swap(b_low, "wide", 2))
        e_arrived, b_arrived = swap(e_low, "wide", 1), swap(b_low, "wide", 1)
        squares = half_squares(place, e_low, b_low, vec_total)
        squares = four(squares, directly(squares, "narrow", (1, 2, 3)))
        squares = squares + swap(squares, "wide", 1)
        grads = [e_low, after(e_arrived, squares), b_low, after(b_arrived, squares)]
    else:
        turned_grad = input_gradient(weights, d_h1, trios, [])
        input_grad, mixed = turn_back(start, turned_grad, mixed, [])
        vec_total = lax.psum_scatter(vec_sums, "narrow", scatter_dimension=1, tiled=True)
        vec_total = lax.psum(vec_total, "wide")
        grads = []
        for every in (early[0], late[0]):
            total = lax.psum_scatter(every, "narrow", scatter_dimension=0, tiled=True)
            grads.append(lax.psum(total.astype(F32), "wide"))
        squares = lax.psum(sum(squares_of(v) for v in grads + [vec_total]), "narrow")
        squares = jnp.full((8, PAIR), squares, F32)
    *updated, grad_norm = adam_step(
        place, squares, math.sqrt(TOK_DEV * wide * narrow), grads, vec_total,
        (w_qkv, w_out, w_up, w_down, vectors),
        (m_qkv, m_out, m_up, m_down, m_vec),
        (v_qkv, v_out, v_up, v_down, v_vec),
        quick,
    )
    return (mixed, input_grad, grad_norm[0, 0], *updated)


def solution(mesh):
    split = P(("wide", "narrow"), None)
    state = (P("narrow", None),) * 4 + (P(None, "narrow"),)
    return jax.shard_map(
        body,
        mesh=mesh,
        in_specs=(split,) * 5 + state * 3,
        out_specs=(split, split, P()) + state * 4,
        check_vma=False,
    )
```

```python
import functools
import math

import jax
import jax.numpy as jnp
from jax import lax
from jax.experimental import pallas as pl
from jax.experimental.pallas import tpu as pltpu
from jax.sharding import PartitionSpec as P

D = 512
HEADS = 8
HEAD_DIM = 64
PAIR = 2 * HEAD_DIM
PAIRS = HEADS // 2
TRIO = 3 * PAIR
TOK_DEV = 1024
QT = 256
HALF = TOK_DEV // 2
TILES = 1
MT = 512
STEP = 10
NORM_EPS = 1e-05
ADAM_EPS = 1e-08
MASKED = -1e30
HIDDEN = 16
BF = jnp.bfloat16
F32 = jnp.float32
MIB = 1024 * 1024
GROUP = 2
HW = GROUP * TRIO
FIRST = 1
LATE = (PAIRS - FIRST) * TRIO
FORWARD_MIB, MIDDLE_MIB, BACKWARD_MIB = 12, 20, 22

NN = (((1,), (0,)), ((), ()))
NT = (((1,), (1,)), ((), ()))
TN = (((0,), (0,)), ((), ()))


def dot(a, b, dims):
    return lax.dot_general(a, b, dims, preferred_element_type=F32)


def params(mib=8):
    return pltpu.CompilerParams(vmem_limit_bytes=mib * MIB)


def sds(shape, dtype):
    return jax.ShapeDtypeStruct(shape, dtype)


SMEM = pl.BlockSpec(memory_space=pltpu.SMEM)
VM = pl.BlockSpec(memory_space=pltpu.VMEM)
ANY = pl.BlockSpec(memory_space=pl.ANY)
HBM = pl.BlockSpec(memory_space=pltpu.HBM)


def whole(shape):
    return pl.BlockSpec(shape, lambda i: (0,) * len(shape))


def cost(flops, moved, exps=0):
    return pl.CostEstimate(flops=int(flops), bytes_accessed=int(moved), transcendentals=int(exps))


def fetch(pairs, sems):
    copies = [
        pltpu.make_async_copy(source, target, sems.at[number])
        for number, (source, target) in enumerate(pairs)
    ]
    for copy in copies:
        copy.start()
    return copies


def trio_columns(base):
    return [
        (local * TRIO + t * PAIR, t * D + (base + local) * PAIR)
        for local in range(GROUP)
        for t in range(3)
    ]


def pack_first_kernel(w_hbm, vec_hbm, out_ref, w_ref, vec_ref, sems):
    rows, vec_cols = w_hbm.shape[0], vec_hbm.shape[1]
    width = GROUP * PAIR
    copies = fetch(
        [(w_hbm.at[:, t * D : t * D + width], w_ref.at[t]) for t in range(3)] + [(vec_hbm, vec_ref)], sems
    )
    for copy in copies:
        copy.wait()
    for local in range(GROUP):
        for t in range(3):
            target = local * TRIO + t * PAIR
            out_ref[:rows, target : target + PAIR] = w_ref[t, :, local * PAIR : (local + 1) * PAIR].astype(BF)
    out_ref[rows:, :] = jnp.zeros((16, HW), BF)
    vec = jnp.concatenate([vec_ref[...], jnp.zeros((7, vec_cols), F32)], 0)
    out_ref[rows:, :vec_cols] = vec.astype(BF)


def pack_first(w_qkv, vectors):
    rows = w_qkv.shape[0]
    return pl.pallas_call(
        pack_first_kernel,
        in_specs=[HBM, HBM],
        out_specs=VM,
        out_shape=sds((rows + 16, HW), BF),
        scratch_shapes=[
            pltpu.VMEM((3, rows, GROUP * PAIR), F32),
            pltpu.VMEM(vectors.shape, F32),
            pltpu.SemaphoreType.DMA((4,)),
        ],
        compiler_params=params(60),
        name="pack_first",
    )(w_qkv, vectors)


def pack_second_kernel(w_ref, w_out_ref, w_up_ref, w_down_ref, *refs):
    second_ref, rest_ref = refs[-2:]
    for target, source in trio_columns(GROUP):
        second_ref[:, target : target + PAIR] = w_ref[:, source : source + PAIR].astype(BF)
    rest_ref[:, :D] = w_out_ref[...].astype(BF)
    rest_ref[:, D : 2 * D] = w_up_ref[...].astype(BF)
    rest_ref[:, 2 * D :] = w_down_ref[...].astype(BF)


def pick(piece, lead, rows):
    return piece[rows, :] if lead is None else piece[lead, rows, :]


def assemble(order, pieces, place, w_full):
    rows = D // len(order)
    for number, (piece, lead, mask) in enumerate(order):
        at = number if mask is None else jnp.bitwise_xor(place[0], mask)
        w_full[pl.ds(pl.multiple_of(at * rows, rows), rows), :] = pick(
            pieces[piece], lead, slice(0, rows)
        )


def turn_rows(source, start, write):
    blocks = source.shape[0] // 8
    whole_blocks, rest = start >> 3, start & 7
    inside = lax.broadcasted_iota(jnp.int32, (8, source.shape[1]), 0) < 8 - rest

    def rolled(block):
        at = pl.multiple_of(((block + whole_blocks) & (blocks - 1)) * 8, 8)
        return pltpu.roll(source[pl.ds(at, 8), :], (8 - rest) & 7, 0)

    def step(i, first):
        second, third = rolled(2 * i + 1), rolled(2 * i + 2)
        write(i, jnp.where(inside, first, second), jnp.where(inside, second, third))
        return third

    lax.fori_loop(0, blocks // 2, step, rolled(0), unroll=8)


def write_into(out):
    def write(i, upper, lower):
        at = pl.multiple_of(i * 16, 16)
        out[pl.ds(at, 16), :] = jnp.concatenate([upper, lower], 0).astype(out.dtype)

    return write


def turn_tokens_kernel(tokens, coded, *refs):
    tokens_out, turned_out, cells_out, start_out, wide_tokens = refs[-5:]
    seen = coded[...] < HIDDEN
    cell = jnp.where(seen, coded[...], coded[...] - HIDDEN)
    start = jnp.int32(TOK_DEV)
    for c in range(4):
        size = jnp.sum((cell == c).astype(jnp.int32))
        first = jnp.sum((cell < c).astype(jnp.int32))
        start = jnp.where(size == HALF, jnp.minimum(start, first), start)
    start_out[0] = start
    shift = jnp.where(start == 0, 0, TOK_DEV - start)
    row = lax.broadcasted_iota(jnp.int32, (8, TOK_DEV), 0)
    cells_out[...] = pltpu.roll(jnp.where((row == 0) | seen, cell, -1), shift, 1)
    wide_tokens[...] = tokens[...].astype(F32)
    turn_rows(wide_tokens, start, write_into(tokens_out))
    turned_out[...] = tokens_out[...].T


def turn_tokens(tokens, coded):
    return pl.pallas_call(
        turn_tokens_kernel,
        in_specs=[VM, VM],
        out_specs=[VM] * 3 + [SMEM],
        out_shape=[
            sds((TOK_DEV, D), BF),
            sds((D, TOK_DEV), BF),
            sds((8, TOK_DEV), jnp.int32),
            sds((1,), jnp.int32),
        ],
        scratch_shapes=[pltpu.VMEM((TOK_DEV, D), F32)],
        compiler_params=params(),
        cost_estimate=cost(1e7, 3e6),
        name="turn_tokens",
    )(tokens, coded)


def turn_cotangent_kernel(start, cot_ref, *refs):
    turn_rows(cot_ref, start[0], write_into(refs[-1]))


def turn_cotangent(start, cot, later):
    return pl.pallas_call(
        turn_cotangent_kernel,
        in_specs=[SMEM, VM] + [ANY] * len(later),
        out_specs=VM,
        out_shape=sds((TOK_DEV, D), F32),
        compiler_params=params(),
        cost_estimate=cost(1e7, 4e6),
        name="turn_cotangent",
    )(start, cot, *later)


def turn_back_kernel(start, source, *refs):
    turned, wide_source = refs[-2:]
    back = (TOK_DEV - start[0]) & (TOK_DEV - 1)
    if source.dtype == F32:
        turn_rows(source, back, write_into(turned))
    else:
        wide_source[...] = source[...].astype(F32)
        turn_rows(wide_source, back, write_into(turned))


def turn_back(start, value, later):
    scratch = (8, PAIR) if value.dtype == F32 else value.shape
    return pl.pallas_call(
        turn_back_kernel,
        in_specs=[SMEM, VM] + [ANY] * len(later),
        out_specs=VM,
        out_shape=sds(value.shape, value.dtype),
        scratch_shapes=[pltpu.VMEM(scratch, F32)],
        compiler_params=params(),
        cost_estimate=cost(1, 1),
        name="turn_back",
    )(start, value, *later)


def make_bias(cells_ref, bias):
    for half in range(2):
        mine = slice(half * HALF, (half + 1) * HALF)
        number = lax.broadcasted_iota(jnp.int32, (16, HALF), 0)
        of_key = jnp.where(cells_ref[1:2, mine] == number, 1.0, 0.0).astype(BF)
        of_query = jnp.where(cells_ref[0:1, mine] == number, 1.0, 0.0).astype(BF)
        keys = lax.broadcasted_iota(jnp.int32, (HALF, HALF), 0)
        queries = lax.broadcasted_iota(jnp.int32, (HALF, HALF), 1)
        seen = (dot(of_key, of_query, TN) > 0.5) | (keys == queries)
        bias[mine, :] = jnp.where(seen, 0.0, MASKED)


def column_of(row):
    eye = lax.broadcasted_iota(jnp.int32, (PAIR, PAIR), 0) == lax.broadcasted_iota(
        jnp.int32, (PAIR, PAIR), 1
    )
    return jnp.sum(jnp.where(eye, row, 0.0), 1, keepdims=True)


def both_heads(pair_t):
    zero = jnp.zeros((HEAD_DIM, pair_t.shape[1]), pair_t.dtype)
    return jnp.concatenate(
        [
            jnp.concatenate([pair_t[:HEAD_DIM], zero], 0),
            jnp.concatenate([zero, pair_t[HEAD_DIM:]], 0),
        ],
        1,
    )


def forward_kernel(order, n_pieces, base, *refs):
    place, tokens, tokens_t, cells_ref, vec_in = refs[:5]
    pieces = refs[5 : 5 + n_pieces]
    att_out, lse_out, krow_out, vrow_out, qt_out, kt_out, w_full, vec_full, tokens_out, bias = refs[
        5 + n_pieces :
    ]
    assemble(order, pieces, place, w_full)
    if vec_in.shape[1] == D:
        vec_full[...] = vec_in[...].astype(F32)
    else:
        rows = D // len(order)
        for piece, lead, mask in order:
            at = pl.multiple_of(jnp.bitwise_xor(place[0], mask) * rows, rows)
            vec_full[:, pl.ds(at, rows)] = pick(pieces[piece], lead, slice(rows, rows + 16))[
                :, :rows
            ].astype(F32)
    make_bias(cells_ref, bias)
    x = tokens[...]
    tokens_out[...] = x
    halves = [slice(0, HALF), slice(HALF, TOK_DEV)]
    chains = []
    for local in range(GROUP):
        lane = slice((base + local) * PAIR, (base + local + 1) * PAIR)
        w = w_full[:, local * TRIO : (local + 1) * TRIO]
        b_q = vec_full[0:1, lane]
        b_v = vec_full[1:2, lane]
        trio = dot(w, tokens_t[...], TN)
        rows = dot(x, w[:, PAIR:], NN)
        here = slice(local * PAIR, (local + 1) * PAIR)
        q_t = ((trio[:PAIR] + column_of(b_q)) * (HEAD_DIM**-0.5)).astype(BF)
        v_t = (trio[2 * PAIR :] + column_of(b_v)).astype(BF)
        k_row = rows[:, :PAIR].astype(BF)
        krow_out[local] = k_row
        vrow_out[local] = (rows[:, PAIR:] + b_v).astype(BF)
        qt_out[here, :] = q_t
        kt_out[here, :] = trio[PAIR : 2 * PAIR].astype(BF)
        for mine in halves:
            chains.append((local, mine, v_t, dot(k_row[mine], both_heads(q_t[:, mine]), NN)))
    for local, mine, v_t, s in chains:
        mask = bias[mine, :]
        s = s + jnp.concatenate([mask, mask], 1)
        top = jnp.max(s, 0, keepdims=True)
        e = jnp.exp(s - top)
        total = jnp.sum(e, 0, keepdims=True)
        lse = top + jnp.log(total)
        e_low = e.astype(BF)
        for h in range(2):
            cols = slice(h * HALF, (h + 1) * HALF)
            head = slice(h * HEAD_DIM, (h + 1) * HEAD_DIM)
            o = dot(v_t[head, mine], e_low[:, cols], NN)
            at = local * PAIR + h * HEAD_DIM
            att_out[at : at + HEAD_DIM, mine] = (o / total[:, cols]).astype(BF)
            lse_out[local, h : h + 1, mine] = lse[:, cols]


def forward_attention(base, place, tokens, tokens_t, cells, vec, pieces, order):
    wide_t, tall = sds((GROUP * PAIR, TOK_DEV), BF), sds((GROUP, TOK_DEV, PAIR), BF)
    return pl.pallas_call(
        functools.partial(forward_kernel, order, len(pieces), base),
        in_specs=[SMEM] + [VM] * (4 + len(pieces)),
        out_specs=[VM] * 9,
        out_shape=[
            wide_t, sds((GROUP, 8, TOK_DEV), F32), tall, tall, wide_t, wide_t, sds((D, HW), BF), sds((16, D), F32),
            sds((TOK_DEV, D), BF),
        ],
        scratch_shapes=[pltpu.VMEM((TOK_DEV, HALF), F32)],
        compiler_params=params(FORWARD_MIB),
        cost_estimate=cost(6e9, 8e6, 2**21),
        name="forward_attention",
    )(place, tokens, tokens_t, cells, vec, *pieces)


def normalize(value):
    center = value - jnp.mean(value, -1, keepdims=True)
    inverse = lax.rsqrt(jnp.mean(center * center, -1, keepdims=True) + NORM_EPS)
    return center * inverse, inverse


def normalize_back(grad, normal, inverse):
    return inverse * (
        grad
        - jnp.mean(grad, -1, keepdims=True)
        - normal * jnp.mean(grad * normal, -1, keepdims=True)
    )


def column_sum(value):
    return jnp.sum(value, 0, keepdims=True)


def row_sources(place, n_shards, stages):
    if not stages:
        return [(0, 0, D)]
    rows = D // n_shards
    piece = D >> len(stages)
    found = []
    for block in range(1 << len(stages)):
        masks = {"narrow": 0, "wide": 0}
        for number, (axis, mask) in enumerate(stages):
            if block >> (len(stages) - 1 - number) & 1:
                masks[axis] |= mask
        source = jnp.bitwise_xor(place[0], masks["narrow"]) * rows
        if piece < rows:
            source = source + jnp.bitwise_xor(place[1], masks["wide"]) * piece
        found.append((block * piece, pl.multiple_of(source, piece), piece))
    return found


def store_rows(outs, place, n_shards, stages, matrix, cols):
    height = outs[0].shape[0]
    for target, source, rows in row_sources(place, n_shards, stages):
        out = outs[target // height]
        at = target % height
        out[at : at + rows, cols] = matrix[pl.ds(source, rows), :].astype(BF)


def gelu_parts(value):
    density = jnp.exp(-0.5 * value * value)
    t = 1.0 / (1.0 + (0.3275911 / math.sqrt(2.0)) * jnp.abs(value))
    poly = 1.061405429
    for factor in (-1.453152027, 1.421413741, -0.284496736, 0.254829592):
        poly = poly * t + factor
    tail = 0.5 * poly * t * density
    return jnp.where(value >= 0.0, 1.0 - tail, tail), value * density * (1.0 / math.sqrt(2.0 * math.pi))


def middle_kernel(order, n_pieces, n_shards, stages, *refs):
    n_g = 2 if stages else 1
    place, tokens, cot_ref, att_a, att_b, vec_ref = refs[:6]
    pieces = refs[6 : 6 + n_pieces]
    mixed_out, dh1_out, datt_out, vec_out = refs[6 + n_pieces : 10 + n_pieces]
    g_outs = refs[10 + n_pieces : 10 + n_pieces + n_g]
    w_full, att_all, first_all, hidden_all, branch_all, pre_all, down_all, dw, sums = refs[
        10 + n_pieces + n_g :
    ]
    step = pl.program_id(0)

    @pl.when(step == 0)
    def _():
        assemble(order, pieces, place, w_full)
        sums[...] = jnp.zeros_like(sums)

    w_out, w_up, w_down = w_full[:, :D], w_full[:, D : 2 * D], w_full[:, 2 * D :]

    def vec(row):
        return vec_ref[row : row + 1, :]

    def tile(number):
        at = pl.ds(pl.multiple_of(step * (TILES * MT) + number * MT, MT), MT)
        att_t = jnp.concatenate([att_a[:, at], att_b[:, at]], 0)
        att_all[:, at] = att_t
        branch = dot(att_t, w_out, TN)
        yield
        normal_1, inverse_1 = normalize(tokens[at, :].astype(F32) + (branch + vec(2)))
        first = normal_1 * vec(5) + vec(6)
        first_low = first.astype(BF)
        first_all[at, :] = first_low
        pre = dot(first_low, w_up, NN)
        yield
        pre = pre + vec(3)
        cdf, bump = gelu_parts(pre)
        hidden = (pre * cdf).astype(BF)
        hidden_all[at, :] = hidden
        slope = cdf + bump
        down = dot(hidden, w_down, NN)
        yield
        normal_2, inverse_2 = normalize(first + (down + vec(4)))
        mixed_out[at, :] = (normal_2 * vec(7) + vec(8)).astype(BF)
        cot = cot_ref[at, :]
        d_h2 = normalize_back(cot * vec(7), normal_2, inverse_2)
        d_down = d_h2.astype(BF)
        down_all[at, :] = d_down
        d_hidden = dot(d_down, w_down, NT)
        yield
        sums[7:8, :] += column_sum(cot * normal_2)
        sums[8:9, :] += column_sum(cot)
        d_pre = (d_hidden * slope).astype(BF)
        pre_all[at, :] = d_pre
        d_up = dot(d_pre, w_up, NT)
        yield
        d_first = d_h2 + d_up
        d_h1 = normalize_back(d_first * vec(5), normal_1, inverse_1)
        dh1_out[at, :] = d_h1
        d_branch = d_h1.astype(BF)
        branch_all[at, :] = d_branch
        datt_out[:, at] = dot(w_out, d_branch, NT).astype(BF)
        yield
        sums[5:6, :] += column_sum(d_first * normal_1)
        sums[6:7, :] += column_sum(d_first)

    tiles = [tile(number) for number in range(TILES)]
    while tiles:
        tiles = [one for one in tiles if next(one, True) is None]

    @pl.when(step == pl.num_programs(0) - 1)
    def _():
        ones = jnp.ones((16, TOK_DEV), BF)
        sums[2:3, :] = dot(ones, branch_all[...], NN)[:1]
        sums[3:4, :] = dot(ones, pre_all[...], NN)[:1]
        sums[4:5, :] = dot(ones, down_all[...], NN)[:1]
        vec_out[...] = sums[...]
        dw[0] = dot(att_all[...], branch_all[...], NN)
        dw[1] = dot(first_all[...], pre_all[...], TN)
        dw[2] = dot(hidden_all[...], down_all[...], TN)
        for number in range(3):
            store_rows(
                g_outs, place, n_shards, stages, dw.at[number], slice(number * D, (number + 1) * D)
            )


def middle(place, tokens, cot, atts, vec, pieces, order, stages):
    height = TILES * MT
    g_shapes = [(D // 2, 3 * D)] * 2 if stages else [(D, 3 * D)]
    return pl.pallas_call(
        functools.partial(middle_kernel, order, len(pieces), len(order), stages),
        grid=(TOK_DEV // height,),
        in_specs=[SMEM] + [VM] * (5 + len(pieces)),
        out_specs=[VM] * (4 + len(g_shapes)),
        out_shape=[
            sds((TOK_DEV, D), BF),
            sds((TOK_DEV, D), F32),
            sds((D, TOK_DEV), BF),
            sds((16, D), F32),
        ]
        + [sds(shape, BF) for shape in g_shapes],
        scratch_shapes=[pltpu.VMEM((D, 3 * D), BF), pltpu.VMEM((D, TOK_DEV), BF)]
        + [pltpu.VMEM((TOK_DEV, D), BF)] * 5
        + [pltpu.VMEM((3, D, D), F32), pltpu.VMEM((16, D), F32)],
        compiler_params=params(MIDDLE_MIB),
        cost_estimate=cost(1e10, 1.2e7, 2**20),
        name="middle",
    )(place, tokens, cot, *atts, vec, *pieces)


def backward_kernel(n_shards, stages, plan, n_sets, n_before, last, place, cells_ref, tokens_t, vec_ref,
                    datt_ref, *refs):
    sets = [refs[6 * number : 6 * (number + 1)] for number in range(n_sets)]
    before = refs[6 * n_sets : 6 * n_sets + n_before]
    bias, dw = refs[-2:]
    n_g = 2 if stages else 1
    d_out, vec = refs[-4 - n_g : -2 - n_g]
    g_outs = refs[-2 - n_g : -2]
    make_bias(cells_ref, bias)
    vec[...] = vec_ref[...]
    halves = [slice(0, HALF), slice(HALF, TOK_DEV)]
    chains = []
    for place_out, (number, local, pair) in enumerate(plan):
        att_ref, lse_ref, krow_ref, vrow_ref, qt_ref, kt_ref = sets[number]
        here = slice(local * PAIR, (local + 1) * PAIR)
        q_t, k_t = qt_ref[here, :], kt_ref[here, :]
        d_t = datt_ref[pair * PAIR : (pair + 1) * PAIR, :]
        k_row, v_row = krow_ref[local], vrow_ref[local]
        product = d_t.astype(F32) * att_ref[here, :].astype(F32)
        for mine in halves:
            s = dot(k_row[mine], both_heads(q_t[:, mine]), NN)
            d_prob = dot(v_row[mine], both_heads(d_t[:, mine]), NN)
            lse = jnp.concatenate([lse_ref[local, 0:1, mine], lse_ref[local, 1:2, mine]], 1)
            chains.append((place_out, mine, q_t, k_t, d_t, product, s, d_prob, lse))
    for place_out, mine, q_t, k_t, d_t, product, s, d_prob, lse in chains:
        mask = bias[mine, :]
        delta = jnp.concatenate(
            [column_sum(product[:HEAD_DIM, mine]), column_sum(product[HEAD_DIM:, mine])], 1
        )
        prob = jnp.exp(s + jnp.concatenate([mask, mask], 1) - lse)
        d_s = (prob * (d_prob - delta)).astype(BF)
        prob_low = prob.astype(BF)
        for h in range(2):
            cols = slice(h * HALF, (h + 1) * HALF)
            head = slice(h * HEAD_DIM, (h + 1) * HEAD_DIM)
            d_q = dot(k_t[head, mine], d_s[:, cols], NN) * (HEAD_DIM**-0.5)
            d_k = dot(q_t[head, mine], d_s[:, cols], NT)
            d_v = dot(d_t[head, mine], prob_low[:, cols], NT)
            for t, value in enumerate((d_q, d_k, d_v)):
                at = t * PAIR + h * HEAD_DIM
                d_out[place_out, at : at + HEAD_DIM, mine] = value.astype(BF)
    ones = jnp.ones((16, TOK_DEV), BF)
    for out, ref in zip(g_outs, before):
        out[:, : ref.shape[1]] = ref[...]
    first = before[0].shape[1] if before else 0
    for place_out, (number, local, pair) in enumerate(plan):
        trio = d_out[place_out]
        dw[place_out] = dot(tokens_t[...], trio, NT)
        at = first + place_out * TRIO
        store_rows(g_outs, place, n_shards, stages, dw.at[place_out], slice(at, at + TRIO))
        total = dot(ones, trio, NT)
        lanes = slice(pair * PAIR, (pair + 1) * PAIR)
        vec[0:1, lanes] = total[:1, :PAIR]
        vec[1:2, lanes] = total[:1, 2 * PAIR :]
    if stages and last:
        height = g_outs[0].shape[0]
        rows = D // n_shards
        for target, source, count in row_sources(place, n_shards, stages):
            at = pl.multiple_of(source // rows * rows, rows)
            g_outs[target // height][target % height : target % height + count, LATE:] = vec[
                :, pl.ds(at, rows)
            ].astype(BF)


def backward_attention(plan, last, place, cells, tokens_t, vec_sums, sets, d_t, before, n_shards, stages, later):
    width = len(plan) * TRIO + (before[0].shape[1] if before else 0)
    if stages:
        shapes = [sds((D // 2, width + (PAIR if last else 0)), BF)] * 2
    else:
        shapes = [sds((D, width), BF)]
    flat = [value for saved in sets for value in saved]
    return pl.pallas_call(
        functools.partial(backward_kernel, n_shards, stages, plan, len(sets), len(before), last),
        in_specs=[SMEM] + [VM] * (4 + len(flat) + len(before)) + [ANY] * len(later),
        out_specs=[VM] * (2 + len(shapes)),
        out_shape=[sds((len(plan), TRIO, TOK_DEV), BF), sds((16, D), F32)] + shapes,
        scratch_shapes=[pltpu.VMEM((TOK_DEV, HALF), F32), pltpu.VMEM((len(plan), D, TRIO), F32)],
        compiler_params=params(BACKWARD_MIB),
        cost_estimate=cost(5e9 * len(plan), 8e6, 2**21),
        name="backward_attention",
    )(place, cells, tokens_t, vec_sums, d_t, *flat, *before, *later)


def input_grad_kernel(w_a, w_b, dh1_ref, trio_a, trio_b, *refs):
    out = refs[-1]
    trios = [ref.at[number] for ref in (trio_a, trio_b) for number in range(ref.shape[0])]
    for tile in range(TOK_DEV // QT):
        here = slice(tile * QT, (tile + 1) * QT)
        total = None
        for w_ref, trio in ((w_a, trios[:GROUP]), (w_b, trios[GROUP:])):
            term = dot(w_ref[...], jnp.concatenate([part[:, here] for part in trio], 0), NN)
            total = term if total is None else total + term
        out[here, :] = dh1_ref[here, :] + total.T


def input_gradient(weights, d_h1, trios, later):
    return pl.pallas_call(
        input_grad_kernel,
        in_specs=[VM] * 5 + [ANY] * len(later),
        out_specs=VM,
        out_shape=sds((TOK_DEV, D), F32),
        compiler_params=params(),
        cost_estimate=cost(1, 1),
        name="input_gradient",
    )(*weights, d_h1, *trios, *later)


def adam(weight, grad, first, second, rate, decay):
    first = 0.5 * first + 0.5 * grad
    second = 0.5 * second + 0.5 * grad * grad
    fix = 1.0 - 0.5**STEP
    update = first * (1.0 / fix) / (jnp.sqrt(second * (1.0 / fix)) + ADAM_EPS)
    return weight - rate * (update + decay * weight), first, second


def pair_parts(first, pairs):
    return [
        (slice(at, at + PAIR), 0, t * D + pair * PAIR)
        for number, pair in enumerate(pairs)
        for t in range(3)
        for at in [first + number * TRIO + t * PAIR]
    ]


EARLY_PARTS = [(slice(i * D, (i + 1) * D), i + 1, 0) for i in range(3)] + pair_parts(3 * D, range(FIRST))
LATE_PARTS = pair_parts(0, range(FIRST, PAIRS))


def adam_kernel(quick, limit, place, square_ref, *refs):
    n_grads = 4 if quick else 2
    grads = refs[:n_grads]
    vec_ref = refs[n_grads]
    states = refs[n_grads + 1 : n_grads + 16]
    outs = refs[n_grads + 16 : n_grads + 36]
    norm_out = refs[-1]
    step = pl.program_id(0)
    norm = jnp.sqrt(square_ref[0:1, 0:1])
    factor = limit / jnp.maximum(norm, limit)

    def write(number, where, grad, rate, decay):
        new, first, second = adam(
            states[number][where], grad * factor, states[5 + number][where],
            states[10 + number][where], rate, decay,
        )
        outs[number][where] = new
        outs[5 + number][where] = first
        outs[10 + number][where] = second
        outs[15 + number][where] = new.astype(BF)

    height = states[0].shape[0]
    pieces = height // 16 if quick else 1
    rows = height // pieces
    for piece in range(pieces):
        if quick:
            mask = jnp.bitwise_xor(place[1], step * pieces + piece)
            at = pl.multiple_of(((mask >> 2) & 1) * 16 + ((mask >> 1) & 1) * 32, 16)
            odd = (mask & 1) == 1
        else:
            at = pl.multiple_of(step * rows, rows)
        for group, parts in enumerate((EARLY_PARTS, LATE_PARTS)):
            for cols, number, target in parts:
                if quick:
                    low, high = grads[2 * group], grads[2 * group + 1]
                    grad = jnp.where(odd, high[pl.ds(at, rows), cols], low[pl.ds(at, rows), cols])
                else:
                    grad = grads[group][pl.ds(at, rows), cols]
                where = (
                    slice(piece * rows, (piece + 1) * rows),
                    slice(target, target + cols.stop - cols.start),
                )
                write(number, where, grad.astype(F32), 0.1, 0.01)

    @pl.when(step == 0)
    def _():
        norm_out[0, 0] = norm[0, 0]
        vec_cols = states[4].shape[1]
        write(4, (slice(0, 9), slice(0, vec_cols)), vec_ref[0:9, :vec_cols].astype(F32), 0.5, 0.0)


def adam_step(place, squares, limit, grads, vec_grad, weights, firsts, seconds, quick):
    steps = 4

    def spec(value):
        if value.shape[0] == 9:
            return whole(value.shape)
        return pl.BlockSpec((value.shape[0] // steps, value.shape[1]), lambda i: (i, 0))

    state = [spec(w) for w in weights]
    shapes = [sds(w.shape, F32) for w in weights]
    return pl.pallas_call(
        functools.partial(adam_kernel, quick, limit),
        grid=(steps,),
        in_specs=[SMEM] + [VM] * (2 + len(grads)) + state * 3,
        out_specs=state * 4 + [SMEM],
        out_shape=shapes * 3 + [sds(w.shape, BF) for w in weights] + [sds((1, 1), F32)],
        compiler_params=params(),
        name="adam",
    )(place, squares, *grads, vec_grad, *weights, *firsts, *seconds)


def swap(value, axis, mask):
    size = lax.axis_size(axis)
    return lax.ppermute(value, axis, [(i, i ^ mask) for i in range(size)])


def add_low(a, b):
    return (a.astype(F32) + b.astype(F32)).astype(BF)


def after(value, *others):
    return lax.optimization_barrier((value, others))[0]


def fold(keep, arrived):
    rows = keep.shape[0] // 2
    send = add_low(keep[rows:], arrived[rows:])
    return add_low(keep[:rows], arrived[:rows]), send


def squares_kernel(place, early, late, vec, out):
    total = []
    for piece in range(4):
        rows = slice(16 * piece, 16 * (piece + 1))
        first, second = early[rows, :].astype(F32), late[rows, :].astype(F32)
        total.append(jnp.sum(first * first) + jnp.sum(second * second))
    total = (total[0] + total[1]) + (total[2] + total[3])
    total = total + jnp.where((place[1] & 1) == 0, jnp.sum(vec[...] * vec[...]), 0.0)
    out[...] = jnp.full(out.shape, total, F32)


def half_squares(place, early, late, vec):
    return pl.pallas_call(
        squares_kernel,
        in_specs=[SMEM] + [VM] * 3,
        out_specs=VM,
        out_shape=sds((8, PAIR), F32),
        compiler_params=params(),
        cost_estimate=cost(1, 1),
        name="half_squares",
    )(place, early, late, vec)


def directly(value, axis, masks):
    return [swap(value, axis, mask) for mask in masks]


def four(value, others):
    return (value + others[0]) + (others[1] + others[2])


def join(held, arrived):
    return jnp.concatenate([held, arrived], 0)


def squares_of(value):
    value = value.astype(F32)
    return jnp.sum(value * value)


STAGES = (("narrow", 1), ("narrow", 2), ("wide", 1), ("wide", 2), ("wide", 4))


def body(
    tokens, cotangent, cells, present, generate,
    w_qkv, w_out, w_up, w_down, vectors,
    m_qkv, m_out, m_up, m_down, m_vec,
    v_qkv, v_out, v_up, v_down, v_vec,
):
    narrow, wide = lax.axis_size("narrow"), lax.axis_size("wide")
    quick = narrow == 4 and wide == 8
    stages = STAGES if quick else ()
    place = jnp.stack([lax.axis_index("narrow"), lax.axis_index("wide")]).astype(jnp.int32)
    shard = w_qkv.shape[0]

    low_a = pack_first(w_qkv, vectors)
    coded = jnp.where((present == 1) & (generate == 0), cells, cells + HIDDEN)
    tokens, tokens_t, cells, start = turn_tokens(tokens, after(coded, low_a))
    low_b, low_rest = pl.pallas_call(
        pack_second_kernel,
        in_specs=[VM] * 4 + [ANY],
        out_specs=[VM, VM],
        out_shape=[sds((shard, HW), BF), sds((shard, 3 * D), BF)],
        compiler_params=params(),
        name="pack_second",
    )(w_qkv, w_out, w_up, w_down, cells)
    if quick:
        y_a = after(swap(low_a, "narrow", 2), (tokens, low_b))
        pieces_a = [low_a, swap(low_a, "narrow", 1), y_a, swap(y_a, "narrow", 1)]
        y_b = swap(after(low_b, y_a), "narrow", 2)
        c_b = swap(low_b, "narrow", 1)
        y_rest = swap(after(low_rest, y_a), "narrow", 2)
        c_rest = swap(low_rest, "narrow", 1)
        order = [(j, None, j) for j in range(4)]
        vec = jnp.zeros((8, PAIR), BF)
    else:
        pieces_a, pieces_b = [lax.all_gather(low_a, "narrow")], [lax.all_gather(low_b, "narrow")]
        pieces_rest = [lax.all_gather(low_rest, "narrow")]
        order = [(0, j, None) for j in range(narrow)]
        vec = lax.all_gather(vectors.astype(BF), "narrow", axis=1, tiled=True)
        vec = jnp.pad(vec, ((0, 7), (0, 0)))

    *saved_a, w_a, vec_full, tokens = forward_attention(
        0, place, tokens, tokens_t, cells, vec, pieces_a, order
    )
    if quick:
        y_b, c_b = after(y_b, saved_a), after(c_b, saved_a)
        y_rest = after(y_rest, y_b)
        d_rest = swap(y_rest, "narrow", 1)
        pieces_b = [low_b, c_b, y_b, after(swap(y_b, "narrow", 1), y_rest)]
    *saved_b, w_b, vec_full, tokens = forward_attention(
        GROUP, place, tokens, tokens_t, cells, vec_full, pieces_b, order
    )
    cotangent = turn_cotangent(start, cotangent, [saved_b[0]])
    if quick:
        pieces_rest = [low_rest, *after((c_rest, y_rest, d_rest), cotangent)]
    mixed, d_h1, d_t, vec_sums, *g_rest = middle(
        place, tokens, cotangent, (saved_a[0], saved_b[0]), vec_full, pieces_rest, order, stages
    )
    sets = [saved_a, saved_b]
    plan = [(pair // GROUP, pair % GROUP, pair) for pair in range(PAIRS)]
    trio_a, vec_sums, *early = backward_attention(
        plan[:FIRST], False, place, cells, tokens_t, vec_sums, sets, d_t, g_rest, narrow, stages, []
    )
    later = []
    if quick:
        e_keep, e_send = early
        mixed = turn_back(start, mixed, [trio_a])
        e_keep, e_send = fold(e_keep, after(swap(e_send, "narrow", 1), mixed))
        e_arrived = swap(e_send, "narrow", 2)
        later = [e_send]
    trio_b, vec_sums, *late = backward_attention(
        plan[FIRST:], True, place, cells, tokens_t, vec_sums, sets, d_t, [], narrow, stages, later
    )
    weights, trios = (w_a, w_b), (trio_a, trio_b)

    if quick:
        b_keep, b_send = late
        b_arrived = swap(b_send, "narrow", 1)
        e_keep, e_send = fold(e_keep, after(e_arrived, trio_b))
        e_arrived = swap(e_send, "wide", 1)
        b_keep, b_send = fold(b_keep, after(b_arrived, e_send))
        b_arrived = swap(b_send, "narrow", 2)
        turned_grad = input_gradient(weights, d_h1, trios, [b_send])
        input_grad = turn_back(start, turned_grad, [])
        b_keep, b_send = fold(b_keep, after(b_arrived, input_grad))
        b_arrived = swap(b_send, "wide", 1)
        e_keep, e_send = fold(e_keep, after(e_arrived, b_send))
        e_arrived = swap(e_send, "wide", 2)
        b_keep, b_send = fold(b_keep, after(b_arrived, e_send))
        b_arrived = swap(b_send, "wide", 2)
        e_keep, e_send = fold(e_keep, after(e_arrived, b_send))
        e_arrived = swap(e_send, "wide", 4)
        b_keep, b_send = fold(b_keep, after(b_arrived, e_send))
        b_arrived = swap(b_send, "wide", 4)
        e_low = add_low(e_keep, after(e_arrived, b_send))
        e_arrived = swap(e_low, "wide", 4)
        vec_total = b_keep[:, LATE:].astype(F32) + b_arrived[:, LATE:].astype(F32)
        b_low = add_low(b_keep[:, :LATE], b_arrived[:, :LATE])
        b_arrived = swap(b_low, "wide", 4)
        e_low = join(e_low, after(e_arrived, b_low))
        e_arrived = swap(e_low, "wide", 2)
        b_low = join(b_low, after(b_arrived, e_low))
        b_arrived = swap(b_low, "wide", 2)
        e_low = join(e_low, after(e_arrived, b_low))
        b_low = join(b_low, after(b_arrived, e_low))
        e_arrived, b_arrived = swap(e_low, "wide", 1), swap(b_low, "wide", 1)
        squares = half_squares(place, e_low, b_low, vec_total)
        squares = four(squares, directly(squares, "narrow", (1, 2, 3)))
        squares = squares + swap(squares, "wide", 1)
        grads = [e_low, after(e_arrived, squares), b_low, after(b_arrived, squares)]
    else:
        turned_grad = input_gradient(weights, d_h1, trios, [])
        input_grad, mixed = turn_back(start, turned_grad, []), turn_back(start, mixed, [])
        vec_total = lax.psum_scatter(vec_sums, "narrow", scatter_dimension=1, tiled=True)
        vec_total = lax.psum(vec_total, "wide")
        grads = []
        for every in (early[0], late[0]):
            total = lax.psum_scatter(every, "narrow", scatter_dimension=0, tiled=True)
            grads.append(lax.psum(total.astype(F32), "wide"))
        squares = lax.psum(sum(squares_of(v) for v in grads + [vec_total]), "narrow")
        squares = jnp.full((8, PAIR), squares, F32)
    *updated, grad_norm = adam_step(
        place, squares, math.sqrt(TOK_DEV * wide * narrow), grads, vec_total,
        (w_qkv, w_out, w_up, w_down, vectors),
        (m_qkv, m_out, m_up, m_down, m_vec),
        (v_qkv, v_out, v_up, v_down, v_vec),
        quick,
    )
    return (mixed, input_grad, grad_norm[0, 0], *updated)


def solution(mesh):
    split = P(("wide", "narrow"), None)
    state = (P("narrow", None),) * 4 + (P(None, "narrow"),)
    return jax.shard_map(
        body,
        mesh=mesh,
        in_specs=(split,) * 5 + state * 3,
        out_specs=(split, split, P()) + state * 4,
        check_vma=False,
    )
```

```python
import functools
import math

import jax
import jax.numpy as jnp
from jax import lax
from jax.experimental import pallas as pl
from jax.experimental.pallas import tpu as pltpu
from jax.sharding import PartitionSpec as P

D = 512
HEADS = 8
HEAD_DIM = 64
PAIR = 2 * HEAD_DIM
PAIRS = HEADS // 2
TRIO = 3 * PAIR
TOK_DEV = 1024
QT = 256
HALF = TOK_DEV // 2
TILES = 2
MT = 256
STEP = 10
NORM_EPS = 1e-05
ADAM_EPS = 1e-08
MASKED = -1e30
HIDDEN = 16
BF = jnp.bfloat16
F32 = jnp.float32
MIB = 1024 * 1024
GROUP = 2
HW = GROUP * TRIO
FIRST = 1
LATE = (PAIRS - FIRST) * TRIO
FORWARD_MIB, MIDDLE_MIB, BACKWARD_MIB = 12, 13, 20

NN = (((1,), (0,)), ((), ()))
NT = (((1,), (1,)), ((), ()))
TN = (((0,), (0,)), ((), ()))


def dot(a, b, dims):
    return lax.dot_general(a, b, dims, preferred_element_type=F32)


def params(mib=8):
    return pltpu.CompilerParams(vmem_limit_bytes=mib * MIB)


def sds(shape, dtype):
    return jax.ShapeDtypeStruct(shape, dtype)


SMEM = pl.BlockSpec(memory_space=pltpu.SMEM)
VM = pl.BlockSpec(memory_space=pltpu.VMEM)
ANY = pl.BlockSpec(memory_space=pl.ANY)
HBM = pl.BlockSpec(memory_space=pltpu.HBM)


def whole(shape):
    return pl.BlockSpec(shape, lambda i: (0,) * len(shape))


def cost(flops, moved, exps=0):
    return pl.CostEstimate(flops=int(flops), bytes_accessed=int(moved), transcendentals=int(exps))


def fetch(pairs, sems):
    copies = [
        pltpu.make_async_copy(source, target, sems.at[number])
        for number, (source, target) in enumerate(pairs)
    ]
    for copy in copies:
        copy.start()
    return copies


def trio_columns(base):
    return [
        (local * TRIO + t * PAIR, t * D + (base + local) * PAIR)
        for local in range(GROUP)
        for t in range(3)
    ]


def pack_first_kernel(w_hbm, vec_hbm, out_ref, w_ref, vec_ref, sems):
    rows, vec_cols = w_hbm.shape[0], vec_hbm.shape[1]
    width = GROUP * PAIR
    copies = fetch(
        [(w_hbm.at[:, t * D : t * D + width], w_ref.at[t]) for t in range(3)] + [(vec_hbm, vec_ref)], sems
    )
    for copy in copies:
        copy.wait()
    for local in range(GROUP):
        for t in range(3):
            target = local * TRIO + t * PAIR
            out_ref[:rows, target : target + PAIR] = w_ref[t, :, local * PAIR : (local + 1) * PAIR].astype(BF)
    out_ref[rows:, :] = jnp.zeros((16, HW), BF)
    vec = jnp.concatenate([vec_ref[...], jnp.zeros((7, vec_cols), F32)], 0)
    out_ref[rows:, :vec_cols] = vec.astype(BF)


def pack_first(w_qkv, vectors):
    rows = w_qkv.shape[0]
    return pl.pallas_call(
        pack_first_kernel,
        in_specs=[HBM, HBM],
        out_specs=VM,
        out_shape=sds((rows + 16, HW), BF),
        scratch_shapes=[
            pltpu.VMEM((3, rows, GROUP * PAIR), F32),
            pltpu.VMEM(vectors.shape, F32),
            pltpu.SemaphoreType.DMA((4,)),
        ],
        compiler_params=params(60),
        name="pack_first",
    )(w_qkv, vectors)


def pack_second_kernel(w_ref, w_out_ref, w_up_ref, w_down_ref, *refs):
    second_ref, rest_ref = refs[-2:]
    for target, source in trio_columns(GROUP):
        second_ref[:, target : target + PAIR] = w_ref[:, source : source + PAIR].astype(BF)
    rest_ref[:, :D] = w_out_ref[...].astype(BF)
    rest_ref[:, D : 2 * D] = w_up_ref[...].astype(BF)
    rest_ref[:, 2 * D :] = w_down_ref[...].astype(BF)


def pick(piece, lead, rows):
    return piece[rows, :] if lead is None else piece[lead, rows, :]


def assemble(order, pieces, place, w_full):
    rows = D // len(order)
    for number, (piece, lead, mask) in enumerate(order):
        at = number if mask is None else jnp.bitwise_xor(place[0], mask)
        w_full[pl.ds(pl.multiple_of(at * rows, rows), rows), :] = pick(
            pieces[piece], lead, slice(0, rows)
        )


def turn_rows(source, start, write):
    blocks = source.shape[0] // 8
    whole_blocks, rest = start >> 3, start & 7
    inside = lax.broadcasted_iota(jnp.int32, (8, source.shape[1]), 0) < 8 - rest

    def rolled(block):
        at = pl.multiple_of(((block + whole_blocks) & (blocks - 1)) * 8, 8)
        return pltpu.roll(source[pl.ds(at, 8), :], (8 - rest) & 7, 0)

    def step(i, first):
        second, third = rolled(2 * i + 1), rolled(2 * i + 2)
        write(i, jnp.where(inside, first, second), jnp.where(inside, second, third))
        return third

    lax.fori_loop(0, blocks // 2, step, rolled(0), unroll=8)


def write_into(out):
    def write(i, upper, lower):
        at = pl.multiple_of(i * 16, 16)
        out[pl.ds(at, 16), :] = jnp.concatenate([upper, lower], 0).astype(out.dtype)

    return write


def turn_tokens_kernel(tokens, coded, *refs):
    tokens_out, turned_out, cells_out, start_out, wide_tokens = refs[-5:]
    seen = coded[...] < HIDDEN
    cell = jnp.where(seen, coded[...], coded[...] - HIDDEN)
    start = jnp.int32(TOK_DEV)
    for c in range(4):
        size = jnp.sum((cell == c).astype(jnp.int32))
        first = jnp.sum((cell < c).astype(jnp.int32))
        start = jnp.where(size == HALF, jnp.minimum(start, first), start)
    start_out[0] = start
    shift = jnp.where(start == 0, 0, TOK_DEV - start)
    row = lax.broadcasted_iota(jnp.int32, (8, TOK_DEV), 0)
    cells_out[...] = pltpu.roll(jnp.where((row == 0) | seen, cell, -1), shift, 1)
    wide_tokens[...] = tokens[...].astype(F32)
    turn_rows(wide_tokens, start, write_into(tokens_out))
    turned_out[...] = tokens_out[...].T


def turn_tokens(tokens, coded):
    return pl.pallas_call(
        turn_tokens_kernel,
        in_specs=[VM, VM],
        out_specs=[VM] * 3 + [SMEM],
        out_shape=[
            sds((TOK_DEV, D), BF),
            sds((D, TOK_DEV), BF),
            sds((8, TOK_DEV), jnp.int32),
            sds((1,), jnp.int32),
        ],
        scratch_shapes=[pltpu.VMEM((TOK_DEV, D), F32)],
        compiler_params=params(),
        cost_estimate=cost(1e7, 3e6),
        name="turn_tokens",
    )(tokens, coded)


def turn_cotangent_kernel(start, cot_ref, *refs):
    turn_rows(cot_ref, start[0], write_into(refs[-1]))


def turn_cotangent(start, cot, later):
    return pl.pallas_call(
        turn_cotangent_kernel,
        in_specs=[SMEM, VM] + [ANY] * len(later),
        out_specs=VM,
        out_shape=sds((TOK_DEV, D), F32),
        compiler_params=params(),
        cost_estimate=cost(1e7, 4e6),
        name="turn_cotangent",
    )(start, cot, *later)


def turn_back_kernel(start, source, *refs):
    turned, wide_source = refs[-2:]
    back = (TOK_DEV - start[0]) & (TOK_DEV - 1)
    if source.dtype == F32:
        turn_rows(source, back, write_into(turned))
    else:
        wide_source[...] = source[...].astype(F32)
        turn_rows(wide_source, back, write_into(turned))


def turn_back(start, value, later):
    scratch = (8, PAIR) if value.dtype == F32 else value.shape
    return pl.pallas_call(
        turn_back_kernel,
        in_specs=[SMEM, VM] + [ANY] * len(later),
        out_specs=VM,
        out_shape=sds(value.shape, value.dtype),
        scratch_shapes=[pltpu.VMEM(scratch, F32)],
        compiler_params=params(),
        cost_estimate=cost(1, 1),
        name="turn_back",
    )(start, value, *later)


def make_bias(cells_ref, bias):
    for half in range(2):
        mine = slice(half * HALF, (half + 1) * HALF)
        number = lax.broadcasted_iota(jnp.int32, (16, HALF), 0)
        of_key = jnp.where(cells_ref[1:2, mine] == number, 1.0, 0.0).astype(BF)
        of_query = jnp.where(cells_ref[0:1, mine] == number, 1.0, 0.0).astype(BF)
        keys = lax.broadcasted_iota(jnp.int32, (HALF, HALF), 0)
        queries = lax.broadcasted_iota(jnp.int32, (HALF, HALF), 1)
        seen = (dot(of_key, of_query, TN) > 0.5) | (keys == queries)
        bias[mine, :] = jnp.where(seen, 0.0, MASKED)


def column_of(row):
    eye = lax.broadcasted_iota(jnp.int32, (PAIR, PAIR), 0) == lax.broadcasted_iota(
        jnp.int32, (PAIR, PAIR), 1
    )
    return jnp.sum(jnp.where(eye, row, 0.0), 1, keepdims=True)


def both_heads(pair_t):
    zero = jnp.zeros((HEAD_DIM, pair_t.shape[1]), pair_t.dtype)
    return jnp.concatenate(
        [
            jnp.concatenate([pair_t[:HEAD_DIM], zero], 0),
            jnp.concatenate([zero, pair_t[HEAD_DIM:]], 0),
        ],
        1,
    )


def forward_kernel(order, n_pieces, base, *refs):
    place, tokens, tokens_t, cells_ref, vec_in = refs[:5]
    pieces = refs[5 : 5 + n_pieces]
    att_out, lse_out, krow_out, vrow_out, qt_out, kt_out, w_full, vec_full, tokens_out, bias = refs[
        5 + n_pieces :
    ]
    assemble(order, pieces, place, w_full)
    if vec_in.shape[1] == D:
        vec_full[...] = vec_in[...].astype(F32)
    else:
        rows = D // len(order)
        for piece, lead, mask in order:
            at = pl.multiple_of(jnp.bitwise_xor(place[0], mask) * rows, rows)
            vec_full[:, pl.ds(at, rows)] = pick(pieces[piece], lead, slice(rows, rows + 16))[
                :, :rows
            ].astype(F32)
    make_bias(cells_ref, bias)
    x = tokens[...]
    tokens_out[...] = x
    halves = [slice(0, HALF), slice(HALF, TOK_DEV)]
    chains = []
    for local in range(GROUP):
        lane = slice((base + local) * PAIR, (base + local + 1) * PAIR)
        w = w_full[:, local * TRIO : (local + 1) * TRIO]
        b_q = vec_full[0:1, lane]
        b_v = vec_full[1:2, lane]
        trio = dot(w, tokens_t[...], TN)
        rows = dot(x, w[:, PAIR:], NN)
        here = slice(local * PAIR, (local + 1) * PAIR)
        q_t = ((trio[:PAIR] + column_of(b_q)) * (HEAD_DIM**-0.5)).astype(BF)
        v_t = (trio[2 * PAIR :] + column_of(b_v)).astype(BF)
        k_row = rows[:, :PAIR].astype(BF)
        krow_out[local] = k_row
        vrow_out[local] = (rows[:, PAIR:] + b_v).astype(BF)
        qt_out[here, :] = q_t
        kt_out[here, :] = trio[PAIR : 2 * PAIR].astype(BF)
        chains += [(local, mine, q_t, v_t, k_row) for mine in halves]

    def scores(chain):
        local, mine, q_t, v_t, k_row = chain
        return dot(k_row[mine], both_heads(q_t[:, mine]), NN)

    ahead = scores(chains[0])
    for number, (local, mine, q_t, v_t, k_row) in enumerate(chains):
        s = ahead
        if number + 1 < len(chains):
            ahead = scores(chains[number + 1])
        mask = bias[mine, :]
        s = s + jnp.concatenate([mask, mask], 1)
        top = jnp.max(s, 0, keepdims=True)
        e = jnp.exp(s - top)
        total = jnp.sum(e, 0, keepdims=True)
        lse = top + jnp.log(total)
        e_low = e.astype(BF)
        for h in range(2):
            cols = slice(h * HALF, (h + 1) * HALF)
            head = slice(h * HEAD_DIM, (h + 1) * HEAD_DIM)
            o = dot(v_t[head, mine], e_low[:, cols], NN)
            at = local * PAIR + h * HEAD_DIM
            att_out[at : at + HEAD_DIM, mine] = (o / total[:, cols]).astype(BF)
            lse_out[local, h : h + 1, mine] = lse[:, cols]


def forward_attention(base, place, tokens, tokens_t, cells, vec, pieces, order):
    wide_t, tall = sds((GROUP * PAIR, TOK_DEV), BF), sds((GROUP, TOK_DEV, PAIR), BF)
    return pl.pallas_call(
        functools.partial(forward_kernel, order, len(pieces), base),
        in_specs=[SMEM] + [VM] * (4 + len(pieces)),
        out_specs=[VM] * 9,
        out_shape=[
            wide_t, sds((GROUP, 8, TOK_DEV), F32), tall, tall, wide_t, wide_t, sds((D, HW), BF), sds((16, D), F32),
            sds((TOK_DEV, D), BF),
        ],
        scratch_shapes=[pltpu.VMEM((TOK_DEV, HALF), F32)],
        compiler_params=params(FORWARD_MIB),
        cost_estimate=cost(1, 1),
        name="forward_attention",
    )(place, tokens, tokens_t, cells, vec, *pieces)


def normalize(value):
    center = value - jnp.mean(value, -1, keepdims=True)
    inverse = lax.rsqrt(jnp.mean(center * center, -1, keepdims=True) + NORM_EPS)
    return center * inverse, inverse


def normalize_back(grad, normal, inverse):
    return inverse * (
        grad
        - jnp.mean(grad, -1, keepdims=True)
        - normal * jnp.mean(grad * normal, -1, keepdims=True)
    )


def column_sum(value):
    return jnp.sum(value, 0, keepdims=True)


def row_sources(place, n_shards, stages):
    if not stages:
        return [(0, 0, D)]
    rows = D // n_shards
    piece = D >> len(stages)
    found = []
    for block in range(1 << len(stages)):
        masks = {"narrow": 0, "wide": 0}
        for number, (axis, mask) in enumerate(stages):
            if block >> (len(stages) - 1 - number) & 1:
                masks[axis] |= mask
        source = jnp.bitwise_xor(place[0], masks["narrow"]) * rows
        if piece < rows:
            source = source + jnp.bitwise_xor(place[1], masks["wide"]) * piece
        found.append((block * piece, pl.multiple_of(source, piece), piece))
    return found


def store_rows(outs, place, n_shards, stages, matrix, cols):
    height = outs[0].shape[0]
    for target, source, rows in row_sources(place, n_shards, stages):
        out = outs[target // height]
        at = target % height
        out[at : at + rows, cols] = matrix[pl.ds(source, rows), :].astype(BF)


def gelu_parts(value):
    density = jnp.exp(-0.5 * value * value)
    t = 1.0 / (1.0 + (0.3275911 / math.sqrt(2.0)) * jnp.abs(value))
    poly = 1.061405429
    for factor in (-1.453152027, 1.421413741, -0.284496736, 0.254829592):
        poly = poly * t + factor
    tail = 0.5 * poly * t * density
    return jnp.where(value >= 0.0, 1.0 - tail, tail), value * density * (1.0 / math.sqrt(2.0 * math.pi))


def middle_kernel(order, n_pieces, *refs):
    place, tokens, cot_ref, att_a, att_b, vec_ref = refs[:6]
    pieces = refs[6 : 6 + n_pieces]
    mixed_out, dh1_out, datt_out, vec_out = refs[6 + n_pieces : 10 + n_pieces]
    first_all, hidden_all, branch_all, pre_all, down_all = refs[10 + n_pieces : 15 + n_pieces]
    w_full, sums = refs[15 + n_pieces :]
    step = pl.program_id(0)

    @pl.when(step == 0)
    def _():
        assemble(order, pieces, place, w_full)
        sums[...] = jnp.zeros_like(sums)

    w_out, w_up, w_down = w_full[:, :D], w_full[:, D : 2 * D], w_full[:, 2 * D :]

    def vec(row):
        return vec_ref[row : row + 1, :]

    def tile(number):
        at = pl.ds(pl.multiple_of(step * (TILES * MT) + number * MT, MT), MT)
        att_t = jnp.concatenate([att_a[:, at], att_b[:, at]], 0)
        branch = dot(att_t, w_out, TN)
        yield
        normal_1, inverse_1 = normalize(tokens[at, :].astype(F32) + (branch + vec(2)))
        first = normal_1 * vec(5) + vec(6)
        first_low = first.astype(BF)
        first_all[at, :] = first_low
        pre = dot(first_low, w_up, NN)
        yield
        pre = pre + vec(3)
        cdf, bump = gelu_parts(pre)
        hidden = (pre * cdf).astype(BF)
        hidden_all[at, :] = hidden
        slope = cdf + bump
        down = dot(hidden, w_down, NN)
        yield
        normal_2, inverse_2 = normalize(first + (down + vec(4)))
        mixed_out[at, :] = (normal_2 * vec(7) + vec(8)).astype(BF)
        cot = cot_ref[at, :]
        d_h2 = normalize_back(cot * vec(7), normal_2, inverse_2)
        d_down = d_h2.astype(BF)
        down_all[at, :] = d_down
        d_hidden = dot(d_down, w_down, NT)
        yield
        sums[7:8, :] += column_sum(cot * normal_2)
        sums[8:9, :] += column_sum(cot)
        d_pre = (d_hidden * slope).astype(BF)
        pre_all[at, :] = d_pre
        d_up = dot(d_pre, w_up, NT)
        yield
        d_first = d_h2 + d_up
        d_h1 = normalize_back(d_first * vec(5), normal_1, inverse_1)
        dh1_out[at, :] = d_h1
        d_branch = d_h1.astype(BF)
        branch_all[at, :] = d_branch
        datt_out[:, at] = dot(w_out, d_branch, NT).astype(BF)
        yield
        sums[5:6, :] += column_sum(d_first * normal_1)
        sums[6:7, :] += column_sum(d_first)

    tiles = [tile(number) for number in range(TILES)]
    while tiles:
        tiles = [one for one in tiles if next(one, True) is None]

    @pl.when(step == pl.num_programs(0) - 1)
    def _():
        ones = jnp.ones((16, TOK_DEV), BF)
        sums[2:3, :] = dot(ones, branch_all[...], NN)[:1]
        sums[3:4, :] = dot(ones, pre_all[...], NN)[:1]
        sums[4:5, :] = dot(ones, down_all[...], NN)[:1]
        vec_out[...] = sums[...]


def middle(place, tokens, cot, atts, vec, pieces, order):
    height = TILES * MT
    return pl.pallas_call(
        functools.partial(middle_kernel, order, len(pieces)),
        grid=(TOK_DEV // height,),
        in_specs=[SMEM] + [VM] * (5 + len(pieces)),
        out_specs=[VM] * 9,
        out_shape=[
            sds((TOK_DEV, D), BF),
            sds((TOK_DEV, D), F32),
            sds((D, TOK_DEV), BF),
            sds((16, D), F32),
        ]
        + [sds((TOK_DEV, D), BF)] * 5,
        scratch_shapes=[pltpu.VMEM((D, 3 * D), BF), pltpu.VMEM((16, D), F32)],
        compiler_params=params(MIDDLE_MIB),
        cost_estimate=cost(1e10, 1.2e7, 2**20),
        name="middle",
    )(place, tokens, cot, *atts, vec, *pieces)


def backward_kernel(n_shards, stages, plan, n_sets, n_inner, last, place, cells_ref, tokens_t, vec_ref,
                    datt_ref, *refs):
    sets = [refs[6 * number : 6 * (number + 1)] for number in range(n_sets)]
    inner = refs[6 * n_sets : 6 * n_sets + n_inner]
    bias, dw = refs[-2:]
    n_g = 2 if stages else 1
    d_out, vec = refs[-4 - n_g : -2 - n_g]
    g_outs = refs[-2 - n_g : -2]
    make_bias(cells_ref, bias)
    vec[...] = vec_ref[...]
    halves = [slice(0, HALF), slice(HALF, TOK_DEV)]
    chains = [(place_out, *entry, mine) for place_out, entry in enumerate(plan) for mine in halves]

    def scores(chain):
        _, number, local, pair, mine = chain
        att_ref, lse_ref, krow_ref, vrow_ref, qt_ref, kt_ref = sets[number]
        here = slice(local * PAIR, (local + 1) * PAIR)
        q_t, d_t = qt_ref[here, mine], datt_ref[pair * PAIR : (pair + 1) * PAIR, mine]
        s = dot(krow_ref[local, mine, :], both_heads(q_t), NN)
        return q_t, d_t, s, dot(vrow_ref[local, mine, :], both_heads(d_t), NN)

    first = 0
    if inner:
        first = 3 * D
        first_all, hidden_all, branch_all, pre_all, down_all = inner
        attended = jnp.concatenate([sets[0][0][...], sets[1][0][...]], 0)
        products = [
            dot(attended, branch_all[...], NN),
            dot(first_all[...], pre_all[...], TN),
            dot(hidden_all[...], down_all[...], TN),
        ]
        for number, product in enumerate(products):
            dw[number % 2] = product
            cols = slice(number * D, (number + 1) * D)
            store_rows(g_outs, place, n_shards, stages, dw.at[number % 2], cols)
    ahead = scores(chains[0])
    for step, (place_out, number, local, pair, mine) in enumerate(chains):
        q_t, d_t, s, d_prob = ahead
        if step + 1 < len(chains):
            ahead = scores(chains[step + 1])
        att_ref, lse_ref, krow_ref, vrow_ref, qt_ref, kt_ref = sets[number]
        mask = bias[mine, :]
        lse = jnp.concatenate([lse_ref[local, 0:1, mine], lse_ref[local, 1:2, mine]], 1)
        here = slice(local * PAIR, (local + 1) * PAIR)
        product = d_t.astype(F32) * att_ref[here, mine].astype(F32)
        delta = jnp.concatenate([column_sum(product[:HEAD_DIM]), column_sum(product[HEAD_DIM:])], 1)
        prob = jnp.exp(s + jnp.concatenate([mask, mask], 1) - lse)
        d_s = (prob * (d_prob - delta)).astype(BF)
        prob_low = prob.astype(BF)
        for h in range(2):
            cols = slice(h * HALF, (h + 1) * HALF)
            head = slice(h * HEAD_DIM, (h + 1) * HEAD_DIM)
            k_t = kt_ref[local * PAIR + h * HEAD_DIM : local * PAIR + (h + 1) * HEAD_DIM, mine]
            d_q = dot(k_t, d_s[:, cols], NN) * (HEAD_DIM**-0.5)
            d_k = dot(q_t[head], d_s[:, cols], NT)
            d_v = dot(d_t[head], prob_low[:, cols], NT)
            for t, value in enumerate((d_q, d_k, d_v)):
                at = t * PAIR + h * HEAD_DIM
                d_out[place_out, at : at + HEAD_DIM, mine] = value.astype(BF)
        if mine.start == 0:
            continue
        trio = d_out[place_out]
        dw[place_out % 2, :, :TRIO] = dot(tokens_t[...], trio, NT)
        at = first + place_out * TRIO
        store_rows(
            g_outs, place, n_shards, stages, dw.at[place_out % 2, :, :TRIO], slice(at, at + TRIO)
        )
        total = dot(jnp.ones((16, TOK_DEV), BF), trio, NT)
        lanes = slice(pair * PAIR, (pair + 1) * PAIR)
        vec[0:1, lanes] = total[:1, :PAIR]
        vec[1:2, lanes] = total[:1, 2 * PAIR :]
    if stages and last:
        height = g_outs[0].shape[0]
        rows = D // n_shards
        for target, source, count in row_sources(place, n_shards, stages):
            at = pl.multiple_of(source // rows * rows, rows)
            g_outs[target // height][target % height : target % height + count, LATE:] = vec[
                :, pl.ds(at, rows)
            ].astype(BF)


def backward_attention(plan, last, place, cells, tokens_t, vec_sums, sets, d_t, inner, n_shards, stages, later):
    width = len(plan) * TRIO + (3 * D if inner else 0)
    if stages:
        shapes = [sds((D // 2, width + (PAIR if last else 0)), BF)] * 2
    else:
        shapes = [sds((D, width), BF)]
    flat = [value for saved in sets for value in saved]
    return pl.pallas_call(
        functools.partial(backward_kernel, n_shards, stages, plan, len(sets), len(inner), last),
        in_specs=[SMEM] + [VM] * (4 + len(flat) + len(inner)) + [ANY] * len(later),
        out_specs=[VM] * (2 + len(shapes)),
        out_shape=[sds((len(plan), TRIO, TOK_DEV), BF), sds((16, D), F32)] + shapes,
        scratch_shapes=[pltpu.VMEM((TOK_DEV, HALF), F32), pltpu.VMEM((2, D, D), F32)],
        compiler_params=params(BACKWARD_MIB),
        cost_estimate=cost(5e9 * len(plan), 8e6, 2**21),
        name="backward_attention",
    )(place, cells, tokens_t, vec_sums, d_t, *flat, *inner, *later)


def input_grad_kernel(w_a, w_b, dh1_ref, trio_a, trio_b, *refs):
    out = refs[-1]
    trios = [ref.at[number] for ref in (trio_a, trio_b) for number in range(ref.shape[0])]
    for tile in range(TOK_DEV // QT):
        here = slice(tile * QT, (tile + 1) * QT)
        total = None
        for w_ref, trio in ((w_a, trios[:GROUP]), (w_b, trios[GROUP:])):
            term = dot(w_ref[...], jnp.concatenate([part[:, here] for part in trio], 0), NN)
            total = term if total is None else total + term
        out[here, :] = dh1_ref[here, :] + total.T


def input_gradient(weights, d_h1, trios, later):
    return pl.pallas_call(
        input_grad_kernel,
        in_specs=[VM] * 5 + [ANY] * len(later),
        out_specs=VM,
        out_shape=sds((TOK_DEV, D), F32),
        compiler_params=params(),
        cost_estimate=cost(1, 1),
        name="input_gradient",
    )(*weights, d_h1, *trios, *later)


def adam(weight, grad, first, second, rate, decay):
    first = 0.5 * first + 0.5 * grad
    second = 0.5 * second + 0.5 * grad * grad
    fix = 1.0 - 0.5**STEP
    update = first * (1.0 / fix) / (jnp.sqrt(second * (1.0 / fix)) + ADAM_EPS)
    return weight - rate * (update + decay * weight), first, second


def pair_parts(first, pairs):
    return [
        (slice(at, at + PAIR), 0, t * D + pair * PAIR)
        for number, pair in enumerate(pairs)
        for t in range(3)
        for at in [first + number * TRIO + t * PAIR]
    ]


EARLY_PARTS = [(slice(i * D, (i + 1) * D), i + 1, 0) for i in range(3)] + pair_parts(3 * D, range(FIRST))
LATE_PARTS = pair_parts(0, range(FIRST, PAIRS))


def adam_kernel(quick, limit, place, square_ref, *refs):
    n_grads = 4 if quick else 2
    grads = refs[:n_grads]
    vec_ref = refs[n_grads]
    states = refs[n_grads + 1 : n_grads + 16]
    outs = refs[n_grads + 16 : n_grads + 36]
    norm_out = refs[-1]
    step = pl.program_id(0)
    norm = jnp.sqrt(square_ref[0:1, 0:1])
    factor = limit / jnp.maximum(norm, limit)

    def write(number, where, grad, rate, decay):
        new, first, second = adam(
            states[number][where], grad * factor, states[5 + number][where],
            states[10 + number][where], rate, decay,
        )
        outs[number][where] = new
        outs[5 + number][where] = first
        outs[10 + number][where] = second
        outs[15 + number][where] = new.astype(BF)

    height = states[0].shape[0]
    pieces = height // 16 if quick else 1
    rows = height // pieces
    for piece in range(pieces):
        if quick:
            mask = jnp.bitwise_xor(place[1], step * pieces + piece)
            at = pl.multiple_of(((mask >> 2) & 1) * 16 + ((mask >> 1) & 1) * 32, 16)
            odd = (mask & 1) == 1
        else:
            at = pl.multiple_of(step * rows, rows)
        for group, parts in enumerate((EARLY_PARTS, LATE_PARTS)):
            for cols, number, target in parts:
                if quick:
                    low, high = grads[2 * group], grads[2 * group + 1]
                    grad = jnp.where(odd, high[pl.ds(at, rows), cols], low[pl.ds(at, rows), cols])
                else:
                    grad = grads[group][pl.ds(at, rows), cols]
                where = (
                    slice(piece * rows, (piece + 1) * rows),
                    slice(target, target + cols.stop - cols.start),
                )
                write(number, where, grad.astype(F32), 0.1, 0.01)

    @pl.when(step == 0)
    def _():
        norm_out[0, 0] = norm[0, 0]
        vec_cols = states[4].shape[1]
        write(4, (slice(0, 9), slice(0, vec_cols)), vec_ref[0:9, :vec_cols].astype(F32), 0.5, 0.0)


def adam_step(place, squares, limit, grads, vec_grad, weights, firsts, seconds, quick):
    steps = 4

    def spec(value):
        if value.shape[0] == 9:
            return whole(value.shape)
        return pl.BlockSpec((value.shape[0] // steps, value.shape[1]), lambda i: (i, 0))

    state = [spec(w) for w in weights]
    shapes = [sds(w.shape, F32) for w in weights]
    return pl.pallas_call(
        functools.partial(adam_kernel, quick, limit),
        grid=(steps,),
        in_specs=[SMEM] + [VM] * (2 + len(grads)) + state * 3,
        out_specs=state * 4 + [SMEM],
        out_shape=shapes * 3 + [sds(w.shape, BF) for w in weights] + [sds((1, 1), F32)],
        compiler_params=params(),
        name="adam",
    )(place, squares, *grads, vec_grad, *weights, *firsts, *seconds)


def swap(value, axis, mask):
    size = lax.axis_size(axis)
    return lax.ppermute(value, axis, [(i, i ^ mask) for i in range(size)])


def add_low(a, b):
    return (a.astype(F32) + b.astype(F32)).astype(BF)


def after(value, *others):
    return lax.optimization_barrier((value, others))[0]


def fold(keep, arrived):
    rows = keep.shape[0] // 2
    send = add_low(keep[rows:], arrived[rows:])
    return add_low(keep[:rows], arrived[:rows]), send


def squares_kernel(place, early, late, vec, out):
    total = []
    for piece in range(4):
        rows = slice(16 * piece, 16 * (piece + 1))
        first, second = early[rows, :].astype(F32), late[rows, :].astype(F32)
        total.append(jnp.sum(first * first) + jnp.sum(second * second))
    total = (total[0] + total[1]) + (total[2] + total[3])
    total = total + jnp.where((place[1] & 1) == 0, jnp.sum(vec[...] * vec[...]), 0.0)
    out[...] = jnp.full(out.shape, total, F32)


def half_squares(place, early, late, vec):
    return pl.pallas_call(
        squares_kernel,
        in_specs=[SMEM] + [VM] * 3,
        out_specs=VM,
        out_shape=sds((8, PAIR), F32),
        compiler_params=params(),
        cost_estimate=cost(1, 1),
        name="half_squares",
    )(place, early, late, vec)


def directly(value, axis, masks):
    return [swap(value, axis, mask) for mask in masks]


def four(value, others):
    return (value + others[0]) + (others[1] + others[2])


def join(held, arrived):
    return jnp.concatenate([held, arrived], 0)


def squares_of(value):
    value = value.astype(F32)
    return jnp.sum(value * value)


STAGES = (("narrow", 1), ("narrow", 2), ("wide", 1), ("wide", 2), ("wide", 4))


def body(
    tokens, cotangent, cells, present, generate,
    w_qkv, w_out, w_up, w_down, vectors,
    m_qkv, m_out, m_up, m_down, m_vec,
    v_qkv, v_out, v_up, v_down, v_vec,
):
    narrow, wide = lax.axis_size("narrow"), lax.axis_size("wide")
    quick = narrow == 4 and wide == 8
    stages = STAGES if quick else ()
    place = jnp.stack([lax.axis_index("narrow"), lax.axis_index("wide")]).astype(jnp.int32)
    shard = w_qkv.shape[0]

    low_a = pack_first(w_qkv, vectors)
    coded = jnp.where((present == 1) & (generate == 0), cells, cells + HIDDEN)
    tokens, tokens_t, cells, start = turn_tokens(tokens, after(coded, low_a))
    low_b, low_rest = pl.pallas_call(
        pack_second_kernel,
        in_specs=[VM] * 4 + [ANY],
        out_specs=[VM, VM],
        out_shape=[sds((shard, HW), BF), sds((shard, 3 * D), BF)],
        compiler_params=params(),
        name="pack_second",
    )(w_qkv, w_out, w_up, w_down, cells)
    if quick:
        y_a = after(swap(low_a, "narrow", 2), (tokens, low_b))
        pieces_a = [low_a, swap(low_a, "narrow", 1), y_a, swap(y_a, "narrow", 1)]
        y_b = swap(after(low_b, y_a), "narrow", 2)
        c_b = swap(low_b, "narrow", 1)
        y_rest = swap(after(low_rest, y_a), "narrow", 2)
        c_rest = swap(low_rest, "narrow", 1)
        order = [(j, None, j) for j in range(4)]
        vec = jnp.zeros((8, PAIR), BF)
    else:
        pieces_a, pieces_b = [lax.all_gather(low_a, "narrow")], [lax.all_gather(low_b, "narrow")]
        pieces_rest = [lax.all_gather(low_rest, "narrow")]
        order = [(0, j, None) for j in range(narrow)]
        vec = lax.all_gather(vectors.astype(BF), "narrow", axis=1, tiled=True)
        vec = jnp.pad(vec, ((0, 7), (0, 0)))

    *saved_a, w_a, vec_full, tokens = forward_attention(
        0, place, tokens, tokens_t, cells, vec, pieces_a, order
    )
    if quick:
        y_b, c_b = after(y_b, saved_a), after(c_b, saved_a)
        pieces_b = [low_b, c_b, y_b, swap(y_b, "narrow", 1)]
    *saved_b, w_b, vec_full, tokens = forward_attention(
        GROUP, place, tokens, tokens_t, cells, vec_full, pieces_b, order
    )
    cotangent = turn_cotangent(start, cotangent, [saved_b[0]])
    if quick:
        y_rest, c_rest = after(y_rest, (saved_b, cotangent)), after(c_rest, saved_b)
        pieces_rest = [low_rest, c_rest, y_rest, swap(y_rest, "narrow", 1)]
    mixed, d_h1, d_t, vec_sums, *inner = middle(
        place, tokens, cotangent, (saved_a[0], saved_b[0]), vec_full, pieces_rest, order
    )
    sets = [saved_a, saved_b]
    plan = [(pair // GROUP, pair % GROUP, pair) for pair in range(PAIRS)]
    trio_a, vec_sums, *early = backward_attention(
        plan[:FIRST], False, place, cells, tokens_t, vec_sums, sets, d_t, inner, narrow, stages, []
    )
    later = []
    if quick:
        e_keep, e_send = early
        mixed = turn_back(start, mixed, [trio_a])
        e_keep, e_send = fold(e_keep, after(swap(e_send, "narrow", 1), mixed))
        e_arrived = swap(e_send, "narrow", 2)
        later = [e_send]
    trio_b, vec_sums, *late = backward_attention(
        plan[FIRST:], True, place, cells, tokens_t, vec_sums, sets, d_t, [], narrow, stages, later
    )
    weights, trios = (w_a, w_b), (trio_a, trio_b)

    if quick:
        b_keep, b_send = late
        b_arrived = swap(b_send, "narrow", 1)
        e_keep, e_send = fold(e_keep, after(e_arrived, trio_b))
        e_arrived = swap(e_send, "wide", 1)
        b_keep, b_send = fold(b_keep, after(b_arrived, e_send))
        b_arrived = swap(b_send, "narrow", 2)
        turned_grad = input_gradient(weights, d_h1, trios, [b_send])
        input_grad = turn_back(start, turned_grad, [])
        b_keep, b_send = fold(b_keep, after(b_arrived, input_grad))
        b_arrived = swap(b_send, "wide", 1)
        e_keep, e_send = fold(e_keep, after(e_arrived, b_send))
        e_arrived = swap(e_send, "wide", 2)
        b_keep, b_send = fold(b_keep, after(b_arrived, e_send))
        b_arrived = swap(b_send, "wide", 2)
        e_keep, e_send = fold(e_keep, after(e_arrived, b_send))
        e_arrived = swap(e_send, "wide", 4)
        b_keep, b_send = fold(b_keep, after(b_arrived, e_send))
        b_arrived = swap(b_send, "wide", 4)
        e_low = add_low(e_keep, after(e_arrived, b_send))
        e_arrived = swap(e_low, "wide", 4)
        vec_total = b_keep[:, LATE:].astype(F32) + b_arrived[:, LATE:].astype(F32)
        b_low = add_low(b_keep[:, :LATE], b_arrived[:, :LATE])
        b_arrived = swap(b_low, "wide", 4)
        e_low = join(e_low, after(e_arrived, b_low))
        e_arrived = swap(e_low, "wide", 2)
        b_low = join(b_low, after(b_arrived, e_low))
        b_arrived = swap(b_low, "wide", 2)
        e_low = join(e_low, after(e_arrived, b_low))
        b_low = join(b_low, after(b_arrived, e_low))
        e_arrived, b_arrived = swap(e_low, "wide", 1), swap(b_low, "wide", 1)
        squares = half_squares(place, e_low, b_low, vec_total)
        squares = four(squares, directly(squares, "narrow", (1, 2, 3)))
        squares = squares + swap(squares, "wide", 1)
        grads = [e_low, after(e_arrived, squares), b_low, after(b_arrived, squares)]
    else:
        turned_grad = input_gradient(weights, d_h1, trios, [])
        input_grad, mixed = turn_back(start, turned_grad, []), turn_back(start, mixed, [])
        vec_total = lax.psum_scatter(vec_sums, "narrow", scatter_dimension=1, tiled=True)
        vec_total = lax.psum(vec_total, "wide")
        grads = []
        for every in (early[0], late[0]):
            total = lax.psum_scatter(every, "narrow", scatter_dimension=0, tiled=True)
            grads.append(lax.psum(total.astype(F32), "wide"))
        squares = lax.psum(sum(squares_of(v) for v in grads + [vec_total]), "narrow")
        squares = jnp.full((8, PAIR), squares, F32)
    *updated, grad_norm = adam_step(
        place, squares, math.sqrt(TOK_DEV * wide * narrow), grads, vec_total,
        (w_qkv, w_out, w_up, w_down, vectors),
        (m_qkv, m_out, m_up, m_down, m_vec),
        (v_qkv, v_out, v_up, v_down, v_vec),
        quick,
    )
    return (mixed, input_grad, grad_norm[0, 0], *updated)


def solution(mesh):
    split = P(("wide", "narrow"), None)
    state = (P("narrow", None),) * 4 + (P(None, "narrow"),)
    return jax.shard_map(
        body,
        mesh=mesh,
        in_specs=(split,) * 5 + state * 3,
        out_specs=(split, split, P()) + state * 4,
        check_vma=False,
    )
```

```python
import functools
import math

import jax
import jax.numpy as jnp
from jax import lax
from jax.experimental import pallas as pl
from jax.experimental.pallas import tpu as pltpu
from jax.sharding import PartitionSpec as P

D = 512
HEADS = 8
HEAD_DIM = 64
PAIR = 2 * HEAD_DIM
PAIRS = HEADS // 2
TRIO = 3 * PAIR
TOK_DEV = 1024
QT = 256
HALF = TOK_DEV // 2
TILES = 1
MT = 512
STEP = 10
NORM_EPS = 1e-05
ADAM_EPS = 1e-08
MASKED = -1e30
HIDDEN = 16
BF = jnp.bfloat16
F32 = jnp.float32
MIB = 1024 * 1024
GROUP = 2
HW = GROUP * TRIO
FIRST = 1
LATE = (PAIRS - FIRST) * TRIO
FORWARD_MIB, MIDDLE_MIB, BACKWARD_MIB = 12, 13, 20

NN = (((1,), (0,)), ((), ()))
NT = (((1,), (1,)), ((), ()))
TN = (((0,), (0,)), ((), ()))


def dot(a, b, dims):
    return lax.dot_general(a, b, dims, preferred_element_type=F32)


def params(mib=8):
    return pltpu.CompilerParams(vmem_limit_bytes=mib * MIB)


def sds(shape, dtype):
    return jax.ShapeDtypeStruct(shape, dtype)


SMEM = pl.BlockSpec(memory_space=pltpu.SMEM)
VM = pl.BlockSpec(memory_space=pltpu.VMEM)
ANY = pl.BlockSpec(memory_space=pl.ANY)
HBM = pl.BlockSpec(memory_space=pltpu.HBM)


def whole(shape):
    return pl.BlockSpec(shape, lambda i: (0,) * len(shape))


def cost(flops, moved, exps=0):
    return pl.CostEstimate(flops=int(flops), bytes_accessed=int(moved), transcendentals=int(exps))


def fetch(pairs, sems):
    copies = [
        pltpu.make_async_copy(source, target, sems.at[number])
        for number, (source, target) in enumerate(pairs)
    ]
    for copy in copies:
        copy.start()
    return copies


def trio_columns(base):
    return [
        (local * TRIO + t * PAIR, t * D + (base + local) * PAIR)
        for local in range(GROUP)
        for t in range(3)
    ]


def pack_first_kernel(w_hbm, vec_hbm, out_ref, w_ref, vec_ref, sems):
    rows, vec_cols = w_hbm.shape[0], vec_hbm.shape[1]
    width = GROUP * PAIR
    copies = fetch(
        [(w_hbm.at[:, t * D : t * D + width], w_ref.at[t]) for t in range(3)] + [(vec_hbm, vec_ref)], sems
    )
    for copy in copies:
        copy.wait()
    for local in range(GROUP):
        for t in range(3):
            target = local * TRIO + t * PAIR
            out_ref[:rows, target : target + PAIR] = w_ref[t, :, local * PAIR : (local + 1) * PAIR].astype(BF)
    out_ref[rows:, :] = jnp.zeros((16, HW), BF)
    vec = jnp.concatenate([vec_ref[...], jnp.zeros((7, vec_cols), F32)], 0)
    out_ref[rows:, :vec_cols] = vec.astype(BF)


def pack_first(w_qkv, vectors):
    rows = w_qkv.shape[0]
    return pl.pallas_call(
        pack_first_kernel,
        in_specs=[HBM, HBM],
        out_specs=VM,
        out_shape=sds((rows + 16, HW), BF),
        scratch_shapes=[
            pltpu.VMEM((3, rows, GROUP * PAIR), F32),
            pltpu.VMEM(vectors.shape, F32),
            pltpu.SemaphoreType.DMA((4,)),
        ],
        compiler_params=params(60),
        name="pack_first",
    )(w_qkv, vectors)


def pack_second_kernel(w_ref, w_out_ref, w_up_ref, w_down_ref, *refs):
    second_ref, rest_ref = refs[-2:]
    for target, source in trio_columns(GROUP):
        second_ref[:, target : target + PAIR] = w_ref[:, source : source + PAIR].astype(BF)
    rest_ref[:, :D] = w_out_ref[...].astype(BF)
    rest_ref[:, D : 2 * D] = w_up_ref[...].astype(BF)
    rest_ref[:, 2 * D :] = w_down_ref[...].astype(BF)


def pick(piece, lead, rows):
    return piece[rows, :] if lead is None else piece[lead, rows, :]


def assemble(order, pieces, place, w_full):
    rows = D // len(order)
    for number, (piece, lead, mask) in enumerate(order):
        at = number if mask is None else jnp.bitwise_xor(place[0], mask)
        w_full[pl.ds(pl.multiple_of(at * rows, rows), rows), :] = pick(
            pieces[piece], lead, slice(0, rows)
        )


def turn_rows(source, start, write):
    blocks = source.shape[0] // 8
    whole_blocks, rest = start >> 3, start & 7
    inside = lax.broadcasted_iota(jnp.int32, (8, source.shape[1]), 0) < 8 - rest

    def rolled(block):
        at = pl.multiple_of(((block + whole_blocks) & (blocks - 1)) * 8, 8)
        return pltpu.roll(source[pl.ds(at, 8), :], (8 - rest) & 7, 0)

    def step(i, first):
        second, third = rolled(2 * i + 1), rolled(2 * i + 2)
        write(i, jnp.where(inside, first, second), jnp.where(inside, second, third))
        return third

    lax.fori_loop(0, blocks // 2, step, rolled(0), unroll=8)


def write_into(out):
    def write(i, upper, lower):
        at = pl.multiple_of(i * 16, 16)
        out[pl.ds(at, 16), :] = jnp.concatenate([upper, lower], 0).astype(out.dtype)

    return write


def turn_tokens_kernel(tokens, coded, *refs):
    tokens_out, turned_out, cells_out, start_out, wide_tokens = refs[-5:]
    seen = coded[...] < HIDDEN
    cell = jnp.where(seen, coded[...], coded[...] - HIDDEN)
    start = jnp.int32(TOK_DEV)
    for c in range(4):
        size = jnp.sum((cell == c).astype(jnp.int32))
        first = jnp.sum((cell < c).astype(jnp.int32))
        start = jnp.where(size == HALF, jnp.minimum(start, first), start)
    start_out[0] = start
    shift = jnp.where(start == 0, 0, TOK_DEV - start)
    row = lax.broadcasted_iota(jnp.int32, (8, TOK_DEV), 0)
    cells_out[...] = pltpu.roll(jnp.where((row == 0) | seen, cell, -1), shift, 1)
    wide_tokens[...] = tokens[...].astype(F32)
    turn_rows(wide_tokens, start, write_into(tokens_out))
    turned_out[...] = tokens_out[...].T


def turn_tokens(tokens, coded):
    return pl.pallas_call(
        turn_tokens_kernel,
        in_specs=[VM, VM],
        out_specs=[VM] * 3 + [SMEM],
        out_shape=[
            sds((TOK_DEV, D), BF),
            sds((D, TOK_DEV), BF),
            sds((8, TOK_DEV), jnp.int32),
            sds((1,), jnp.int32),
        ],
        scratch_shapes=[pltpu.VMEM((TOK_DEV, D), F32)],
        compiler_params=params(),
        cost_estimate=cost(1e7, 3e6),
        name="turn_tokens",
    )(tokens, coded)


def turn_cotangent_kernel(start, cot_ref, *refs):
    turn_rows(cot_ref, start[0], write_into(refs[-1]))


def turn_cotangent(start, cot, later):
    return pl.pallas_call(
        turn_cotangent_kernel,
        in_specs=[SMEM, VM] + [ANY] * len(later),
        out_specs=VM,
        out_shape=sds((TOK_DEV, D), F32),
        compiler_params=params(),
        cost_estimate=cost(1e7, 4e6),
        name="turn_cotangent",
    )(start, cot, *later)


def turn_back_kernel(start, source, *refs):
    turned, wide_source = refs[-2:]
    back = (TOK_DEV - start[0]) & (TOK_DEV - 1)
    if source.dtype == F32:
        turn_rows(source, back, write_into(turned))
    else:
        wide_source[...] = source[...].astype(F32)
        turn_rows(wide_source, back, write_into(turned))


def turn_back(start, value, later):
    scratch = (8, PAIR) if value.dtype == F32 else value.shape
    return pl.pallas_call(
        turn_back_kernel,
        in_specs=[SMEM, VM] + [ANY] * len(later),
        out_specs=VM,
        out_shape=sds(value.shape, value.dtype),
        scratch_shapes=[pltpu.VMEM(scratch, F32)],
        compiler_params=params(),
        cost_estimate=cost(1, 1),
        name="turn_back",
    )(start, value, *later)


def make_bias(cells_ref, bias):
    for half in range(2):
        mine = slice(half * HALF, (half + 1) * HALF)
        number = lax.broadcasted_iota(jnp.int32, (16, HALF), 0)
        of_key = jnp.where(cells_ref[1:2, mine] == number, 1.0, 0.0).astype(BF)
        of_query = jnp.where(cells_ref[0:1, mine] == number, 1.0, 0.0).astype(BF)
        keys = lax.broadcasted_iota(jnp.int32, (HALF, HALF), 0)
        queries = lax.broadcasted_iota(jnp.int32, (HALF, HALF), 1)
        seen = (dot(of_key, of_query, TN) > 0.5) | (keys == queries)
        bias[mine, :] = jnp.where(seen, 0.0, MASKED)


def column_of(row):
    eye = lax.broadcasted_iota(jnp.int32, (PAIR, PAIR), 0) == lax.broadcasted_iota(
        jnp.int32, (PAIR, PAIR), 1
    )
    return jnp.sum(jnp.where(eye, row, 0.0), 1, keepdims=True)


def both_heads(pair_t):
    zero = jnp.zeros((HEAD_DIM, pair_t.shape[1]), pair_t.dtype)
    return jnp.concatenate(
        [
            jnp.concatenate([pair_t[:HEAD_DIM], zero], 0),
            jnp.concatenate([zero, pair_t[HEAD_DIM:]], 0),
        ],
        1,
    )


def forward_kernel(order, n_pieces, base, *refs):
    place, tokens, tokens_t, cells_ref, vec_in = refs[:5]
    pieces = refs[5 : 5 + n_pieces]
    att_out, lse_out, krow_out, vrow_out, qt_out, kt_out, w_full, vec_full, tokens_out, bias = refs[
        5 + n_pieces :
    ]
    assemble(order, pieces, place, w_full)
    if vec_in.shape[1] == D:
        vec_full[...] = vec_in[...].astype(F32)
    else:
        rows = D // len(order)
        for piece, lead, mask in order:
            at = pl.multiple_of(jnp.bitwise_xor(place[0], mask) * rows, rows)
            vec_full[:, pl.ds(at, rows)] = pick(pieces[piece], lead, slice(rows, rows + 16))[
                :, :rows
            ].astype(F32)
    make_bias(cells_ref, bias)
    x = tokens[...]
    tokens_out[...] = x
    halves = [slice(0, HALF), slice(HALF, TOK_DEV)]
    chains = []
    for local in range(GROUP):
        lane = slice((base + local) * PAIR, (base + local + 1) * PAIR)
        w = w_full[:, local * TRIO : (local + 1) * TRIO]
        b_q = vec_full[0:1, lane]
        b_v = vec_full[1:2, lane]
        trio = dot(w, tokens_t[...], TN)
        rows = dot(x, w[:, PAIR:], NN)
        here = slice(local * PAIR, (local + 1) * PAIR)
        q_t = ((trio[:PAIR] + column_of(b_q)) * (HEAD_DIM**-0.5)).astype(BF)
        v_t = (trio[2 * PAIR :] + column_of(b_v)).astype(BF)
        k_row = rows[:, :PAIR].astype(BF)
        krow_out[local] = k_row
        vrow_out[local] = (rows[:, PAIR:] + b_v).astype(BF)
        qt_out[here, :] = q_t
        kt_out[here, :] = trio[PAIR : 2 * PAIR].astype(BF)
        chains += [(local, mine, q_t, v_t, k_row) for mine in halves]

    def scores(chain):
        local, mine, q_t, v_t, k_row = chain
        return dot(k_row[mine], both_heads(q_t[:, mine]), NN)

    ahead = scores(chains[0])
    for number, (local, mine, q_t, v_t, k_row) in enumerate(chains):
        s = ahead
        if number + 1 < len(chains):
            ahead = scores(chains[number + 1])
        mask = bias[mine, :]
        s = s + jnp.concatenate([mask, mask], 1)
        top = jnp.max(s, 0, keepdims=True)
        e = jnp.exp(s - top)
        total = jnp.sum(e, 0, keepdims=True)
        lse = top + jnp.log(total)
        e_low = e.astype(BF)
        for h in range(2):
            cols = slice(h * HALF, (h + 1) * HALF)
            head = slice(h * HEAD_DIM, (h + 1) * HEAD_DIM)
            o = dot(v_t[head, mine], e_low[:, cols], NN)
            at = local * PAIR + h * HEAD_DIM
            att_out[at : at + HEAD_DIM, mine] = (o / total[:, cols]).astype(BF)
            lse_out[local, h : h + 1, mine] = lse[:, cols]


def forward_attention(base, place, tokens, tokens_t, cells, vec, pieces, order):
    wide_t, tall = sds((GROUP * PAIR, TOK_DEV), BF), sds((GROUP, TOK_DEV, PAIR), BF)
    return pl.pallas_call(
        functools.partial(forward_kernel, order, len(pieces), base),
        in_specs=[SMEM] + [VM] * (4 + len(pieces)),
        out_specs=[VM] * 9,
        out_shape=[
            wide_t, sds((GROUP, 8, TOK_DEV), F32), tall, tall, wide_t, wide_t, sds((D, HW), BF), sds((16, D), F32),
            sds((TOK_DEV, D), BF),
        ],
        scratch_shapes=[pltpu.VMEM((TOK_DEV, HALF), F32)],
        compiler_params=params(FORWARD_MIB),
        cost_estimate=cost(1, 1),
        name="forward_attention",
    )(place, tokens, tokens_t, cells, vec, *pieces)


def normalize(value):
    center = value - jnp.mean(value, -1, keepdims=True)
    inverse = lax.rsqrt(jnp.mean(center * center, -1, keepdims=True) + NORM_EPS)
    return center * inverse, inverse


def normalize_back(grad, normal, inverse):
    return inverse * (
        grad
        - jnp.mean(grad, -1, keepdims=True)
        - normal * jnp.mean(grad * normal, -1, keepdims=True)
    )


def column_sum(value):
    return jnp.sum(value, 0, keepdims=True)


def row_sources(place, n_shards, stages):
    if not stages:
        return [(0, 0, D)]
    rows = D // n_shards
    piece = D >> len(stages)
    found = []
    for block in range(1 << len(stages)):
        masks = {"narrow": 0, "wide": 0}
        for number, (axis, mask) in enumerate(stages):
            if block >> (len(stages) - 1 - number) & 1:
                masks[axis] |= mask
        source = jnp.bitwise_xor(place[0], masks["narrow"]) * rows
        if piece < rows:
            source = source + jnp.bitwise_xor(place[1], masks["wide"]) * piece
        found.append((block * piece, pl.multiple_of(source, piece), piece))
    return found


def store_rows(outs, place, n_shards, stages, matrix, cols):
    height = outs[0].shape[0]
    for target, source, rows in row_sources(place, n_shards, stages):
        out = outs[target // height]
        at = target % height
        out[at : at + rows, cols] = matrix[pl.ds(source, rows), :].astype(BF)


def gelu_parts(value):
    density = jnp.exp(-0.5 * value * value)
    t = 1.0 / (1.0 + (0.3275911 / math.sqrt(2.0)) * jnp.abs(value))
    poly = 1.061405429
    for factor in (-1.453152027, 1.421413741, -0.284496736, 0.254829592):
        poly = poly * t + factor
    tail = 0.5 * poly * t * density
    return jnp.where(value >= 0.0, 1.0 - tail, tail), value * density * (1.0 / math.sqrt(2.0 * math.pi))


def middle_kernel(order, n_pieces, *refs):
    place, tokens, cot_ref, att_a, att_b, vec_ref = refs[:6]
    pieces = refs[6 : 6 + n_pieces]
    mixed_out, dh1_out, datt_out, vec_out = refs[6 + n_pieces : 10 + n_pieces]
    first_all, hidden_all, branch_all, pre_all, down_all = refs[10 + n_pieces : 15 + n_pieces]
    w_full, sums = refs[15 + n_pieces :]
    step = pl.program_id(0)

    @pl.when(step == 0)
    def _():
        assemble(order, pieces, place, w_full)
        sums[...] = jnp.zeros_like(sums)

    w_out, w_up, w_down = w_full[:, :D], w_full[:, D : 2 * D], w_full[:, 2 * D :]

    def vec(row):
        return vec_ref[row : row + 1, :]

    def tile(number):
        at = pl.ds(pl.multiple_of(step * (TILES * MT) + number * MT, MT), MT)
        att_t = jnp.concatenate([att_a[:, at], att_b[:, at]], 0)
        branch = dot(att_t, w_out, TN)
        yield
        normal_1, inverse_1 = normalize(tokens[at, :].astype(F32) + (branch + vec(2)))
        first = normal_1 * vec(5) + vec(6)
        first_low = first.astype(BF)
        first_all[at, :] = first_low
        pre = dot(first_low, w_up, NN)
        yield
        pre = pre + vec(3)
        cdf, bump = gelu_parts(pre)
        hidden = (pre * cdf).astype(BF)
        hidden_all[at, :] = hidden
        slope = cdf + bump
        down = dot(hidden, w_down, NN)
        yield
        normal_2, inverse_2 = normalize(first + (down + vec(4)))
        mixed_out[at, :] = (normal_2 * vec(7) + vec(8)).astype(BF)
        cot = cot_ref[at, :]
        d_h2 = normalize_back(cot * vec(7), normal_2, inverse_2)
        d_down = d_h2.astype(BF)
        down_all[at, :] = d_down
        d_hidden = dot(d_down, w_down, NT)
        yield
        sums[7:8, :] += column_sum(cot * normal_2)
        sums[8:9, :] += column_sum(cot)
        d_pre = (d_hidden * slope).astype(BF)
        pre_all[at, :] = d_pre
        d_up = dot(d_pre, w_up, NT)
        yield
        d_first = d_h2 + d_up
        d_h1 = normalize_back(d_first * vec(5), normal_1, inverse_1)
        dh1_out[at, :] = d_h1
        d_branch = d_h1.astype(BF)
        branch_all[at, :] = d_branch
        datt_out[:, at] = dot(w_out, d_branch, NT).astype(BF)
        yield
        sums[5:6, :] += column_sum(d_first * normal_1)
        sums[6:7, :] += column_sum(d_first)

    tiles = [tile(number) for number in range(TILES)]
    while tiles:
        tiles = [one for one in tiles if next(one, True) is None]

    @pl.when(step == pl.num_programs(0) - 1)
    def _():
        ones = jnp.ones((16, TOK_DEV), BF)
        sums[2:3, :] = dot(ones, branch_all[...], NN)[:1]
        sums[3:4, :] = dot(ones, pre_all[...], NN)[:1]
        sums[4:5, :] = dot(ones, down_all[...], NN)[:1]
        vec_out[...] = sums[...]


def middle(place, tokens, cot, atts, vec, pieces, order):
    height = TILES * MT
    return pl.pallas_call(
        functools.partial(middle_kernel, order, len(pieces)),
        grid=(TOK_DEV // height,),
        in_specs=[SMEM] + [VM] * (5 + len(pieces)),
        out_specs=[VM] * 9,
        out_shape=[
            sds((TOK_DEV, D), BF),
            sds((TOK_DEV, D), F32),
            sds((D, TOK_DEV), BF),
            sds((16, D), F32),
        ]
        + [sds((TOK_DEV, D), BF)] * 5,
        scratch_shapes=[pltpu.VMEM((D, 3 * D), BF), pltpu.VMEM((16, D), F32)],
        compiler_params=params(MIDDLE_MIB),
        cost_estimate=cost(1e10, 1.2e7, 2**20),
        name="middle",
    )(place, tokens, cot, *atts, vec, *pieces)


def backward_kernel(n_shards, stages, plan, n_sets, n_inner, last, place, cells_ref, tokens_t, vec_ref,
                    datt_ref, *refs):
    sets = [refs[6 * number : 6 * (number + 1)] for number in range(n_sets)]
    inner = refs[6 * n_sets : 6 * n_sets + n_inner]
    bias, dw = refs[-2:]
    n_g = 2 if stages else 1
    d_out, vec = refs[-4 - n_g : -2 - n_g]
    g_outs = refs[-2 - n_g : -2]
    make_bias(cells_ref, bias)
    vec[...] = vec_ref[...]
    halves = [slice(0, HALF), slice(HALF, TOK_DEV)]
    chains = [(place_out, *entry, mine) for place_out, entry in enumerate(plan) for mine in halves]

    def scores(chain):
        _, number, local, pair, mine = chain
        att_ref, lse_ref, krow_ref, vrow_ref, qt_ref, kt_ref = sets[number]
        here = slice(local * PAIR, (local + 1) * PAIR)
        q_t, d_t = qt_ref[here, mine], datt_ref[pair * PAIR : (pair + 1) * PAIR, mine]
        s = dot(krow_ref[local, mine, :], both_heads(q_t), NN)
        return q_t, d_t, s, dot(vrow_ref[local, mine, :], both_heads(d_t), NN)

    first = 0
    if inner:
        first = 3 * D
        first_all, hidden_all, branch_all, pre_all, down_all = inner
        attended = jnp.concatenate([sets[0][0][...], sets[1][0][...]], 0)
        products = [
            dot(attended, branch_all[...], NN),
            dot(first_all[...], pre_all[...], TN),
            dot(hidden_all[...], down_all[...], TN),
        ]
        for number, product in enumerate(products):
            dw[number % 2] = product
            cols = slice(number * D, (number + 1) * D)
            store_rows(g_outs, place, n_shards, stages, dw.at[number % 2], cols)
    ahead = scores(chains[0])
    for step, (place_out, number, local, pair, mine) in enumerate(chains):
        q_t, d_t, s, d_prob = ahead
        if step + 1 < len(chains):
            ahead = scores(chains[step + 1])
        att_ref, lse_ref, krow_ref, vrow_ref, qt_ref, kt_ref = sets[number]
        mask = bias[mine, :]
        lse = jnp.concatenate([lse_ref[local, 0:1, mine], lse_ref[local, 1:2, mine]], 1)
        here = slice(local * PAIR, (local + 1) * PAIR)
        product = d_t.astype(F32) * att_ref[here, mine].astype(F32)
        delta = jnp.concatenate([column_sum(product[:HEAD_DIM]), column_sum(product[HEAD_DIM:])], 1)
        prob = jnp.exp(s + jnp.concatenate([mask, mask], 1) - lse)
        d_s = (prob * (d_prob - delta)).astype(BF)
        prob_low = prob.astype(BF)
        for h in range(2):
            cols = slice(h * HALF, (h + 1) * HALF)
            head = slice(h * HEAD_DIM, (h + 1) * HEAD_DIM)
            k_t = kt_ref[local * PAIR + h * HEAD_DIM : local * PAIR + (h + 1) * HEAD_DIM, mine]
            d_q = dot(k_t, d_s[:, cols], NN) * (HEAD_DIM**-0.5)
            d_k = dot(q_t[head], d_s[:, cols], NT)
            d_v = dot(d_t[head], prob_low[:, cols], NT)
            for t, value in enumerate((d_q, d_k, d_v)):
                at = t * PAIR + h * HEAD_DIM
                d_out[place_out, at : at + HEAD_DIM, mine] = value.astype(BF)
        if mine.start == 0:
            continue
        trio = d_out[place_out]
        dw[place_out % 2, :, :TRIO] = dot(tokens_t[...], trio, NT)
        at = first + place_out * TRIO
        store_rows(
            g_outs, place, n_shards, stages, dw.at[place_out % 2, :, :TRIO], slice(at, at + TRIO)
        )
        total = dot(jnp.ones((16, TOK_DEV), BF), trio, NT)
        lanes = slice(pair * PAIR, (pair + 1) * PAIR)
        vec[0:1, lanes] = total[:1, :PAIR]
        vec[1:2, lanes] = total[:1, 2 * PAIR :]
    if stages and last:
        height = g_outs[0].shape[0]
        rows = D // n_shards
        for target, source, count in row_sources(place, n_shards, stages):
            at = pl.multiple_of(source // rows * rows, rows)
            g_outs[target // height][target % height : target % height + count, LATE:] = vec[
                :, pl.ds(at, rows)
            ].astype(BF)


def backward_attention(plan, last, place, cells, tokens_t, vec_sums, sets, d_t, inner, n_shards, stages, later):
    width = len(plan) * TRIO + (3 * D if inner else 0)
    if stages:
        shapes = [sds((D // 2, width + (PAIR if last else 0)), BF)] * 2
    else:
        shapes = [sds((D, width), BF)]
    flat = [value for saved in sets for value in saved]
    return pl.pallas_call(
        functools.partial(backward_kernel, n_shards, stages, plan, len(sets), len(inner), last),
        in_specs=[SMEM] + [VM] * (4 + len(flat) + len(inner)) + [ANY] * len(later),
        out_specs=[VM] * (2 + len(shapes)),
        out_shape=[sds((len(plan), TRIO, TOK_DEV), BF), sds((16, D), F32)] + shapes,
        scratch_shapes=[pltpu.VMEM((TOK_DEV, HALF), F32), pltpu.VMEM((2, D, D), F32)],
        compiler_params=params(BACKWARD_MIB),
        cost_estimate=cost(5e9 * len(plan), 8e6, 2**21),
        name="backward_attention",
    )(place, cells, tokens_t, vec_sums, d_t, *flat, *inner, *later)


def input_grad_kernel(start, w_a, w_b, dh1_ref, trio_a, trio_b, *refs):
    out, turned = refs[-2:]
    trios = [ref.at[number] for ref in (trio_a, trio_b) for number in range(ref.shape[0])]
    for tile in range(TOK_DEV // QT):
        here = slice(tile * QT, (tile + 1) * QT)
        total = None
        for w_ref, parts in ((w_a, trios[:GROUP]), (w_b, trios[GROUP:])):
            term = dot(w_ref[...], jnp.concatenate([part[:, here] for part in parts], 0), NN)
            total = term if total is None else total + term
        turned[here, :] = dh1_ref[here, :] + total.T
    turn_rows(turned, (TOK_DEV - start[0]) & (TOK_DEV - 1), write_into(out))


def input_gradient(start, weights, d_h1, trios, later):
    return pl.pallas_call(
        input_grad_kernel,
        in_specs=[SMEM] + [VM] * 5 + [ANY] * len(later),
        out_specs=VM,
        out_shape=sds((TOK_DEV, D), F32),
        scratch_shapes=[pltpu.VMEM((TOK_DEV, D), F32)],
        compiler_params=params(),
        cost_estimate=cost(1, 1),
        name="input_gradient",
    )(start, *weights, d_h1, *trios, *later)


def adam(weight, grad, first, second, rate, decay):
    first = 0.5 * first + 0.5 * grad
    second = 0.5 * second + 0.5 * grad * grad
    fix = 1.0 - 0.5**STEP
    update = first * (1.0 / fix) / (jnp.sqrt(second * (1.0 / fix)) + ADAM_EPS)
    return weight - rate * (update + decay * weight), first, second


def pair_parts(first, pairs):
    return [
        (slice(at, at + PAIR), 0, t * D + pair * PAIR)
        for number, pair in enumerate(pairs)
        for t in range(3)
        for at in [first + number * TRIO + t * PAIR]
    ]


EARLY_PARTS = [(slice(i * D, (i + 1) * D), i + 1, 0) for i in range(3)] + pair_parts(3 * D, range(FIRST))
LATE_PARTS = pair_parts(0, range(FIRST, PAIRS))


def adam_kernel(quick, limit, place, square_ref, *refs):
    n_grads = 4 if quick else 2
    grads = refs[:n_grads]
    vec_ref = refs[n_grads]
    states = refs[n_grads + 1 : n_grads + 16]
    outs = refs[n_grads + 16 : n_grads + 36]
    norm_out = refs[-1]
    step = pl.program_id(0)
    norm = jnp.sqrt(square_ref[0:1, 0:1])
    factor = limit / jnp.maximum(norm, limit)

    def write(number, where, grad, rate, decay):
        new, first, second = adam(
            states[number][where], grad * factor, states[5 + number][where],
            states[10 + number][where], rate, decay,
        )
        outs[number][where] = new
        outs[5 + number][where] = first
        outs[10 + number][where] = second
        outs[15 + number][where] = new.astype(BF)

    height = states[0].shape[0]
    pieces = height // 16 if quick else 1
    rows = height // pieces
    for piece in range(pieces):
        if quick:
            mask = jnp.bitwise_xor(place[1], step * pieces + piece)
            at = pl.multiple_of(((mask >> 2) & 1) * 16 + ((mask >> 1) & 1) * 32, 16)
            odd = (mask & 1) == 1
        else:
            at = pl.multiple_of(step * rows, rows)
        for group, parts in enumerate((EARLY_PARTS, LATE_PARTS)):
            for cols, number, target in parts:
                if quick:
                    low, high = grads[2 * group], grads[2 * group + 1]
                    grad = jnp.where(odd, high[pl.ds(at, rows), cols], low[pl.ds(at, rows), cols])
                else:
                    grad = grads[group][pl.ds(at, rows), cols]
                where = (
                    slice(piece * rows, (piece + 1) * rows),
                    slice(target, target + cols.stop - cols.start),
                )
                write(number, where, grad.astype(F32), 0.1, 0.01)

    @pl.when(step == 0)
    def _():
        norm_out[0, 0] = norm[0, 0]
        vec_cols = states[4].shape[1]
        write(4, (slice(0, 9), slice(0, vec_cols)), vec_ref[0:9, :vec_cols].astype(F32), 0.5, 0.0)


def adam_step(place, squares, limit, grads, vec_grad, weights, firsts, seconds, quick):
    steps = 4

    def spec(value):
        if value.shape[0] == 9:
            return whole(value.shape)
        return pl.BlockSpec((value.shape[0] // steps, value.shape[1]), lambda i: (i, 0))

    state = [spec(w) for w in weights]
    shapes = [sds(w.shape, F32) for w in weights]
    return pl.pallas_call(
        functools.partial(adam_kernel, quick, limit),
        grid=(steps,),
        in_specs=[SMEM] + [VM] * (2 + len(grads)) + state * 3,
        out_specs=state * 4 + [SMEM],
        out_shape=shapes * 3 + [sds(w.shape, BF) for w in weights] + [sds((1, 1), F32)],
        compiler_params=params(),
        name="adam",
    )(place, squares, *grads, vec_grad, *weights, *firsts, *seconds)


def swap(value, axis, mask):
    size = lax.axis_size(axis)
    return lax.ppermute(value, axis, [(i, i ^ mask) for i in range(size)])


def add_low(a, b):
    return (a.astype(F32) + b.astype(F32)).astype(BF)


def after(value, *others):
    return lax.optimization_barrier((value, others))[0]


def fold(keep, arrived):
    rows = keep.shape[0] // 2
    send = add_low(keep[rows:], arrived[rows:])
    return add_low(keep[:rows], arrived[:rows]), send


def squares_kernel(place, early, late, vec, out):
    total = []
    for piece in range(4):
        rows = slice(16 * piece, 16 * (piece + 1))
        first, second = early[rows, :].astype(F32), late[rows, :].astype(F32)
        total.append(jnp.sum(first * first) + jnp.sum(second * second))
    total = (total[0] + total[1]) + (total[2] + total[3])
    total = total + jnp.where((place[1] & 1) == 0, jnp.sum(vec[...] * vec[...]), 0.0)
    out[...] = jnp.full(out.shape, total, F32)


def half_squares(place, early, late, vec):
    return pl.pallas_call(
        squares_kernel,
        in_specs=[SMEM] + [VM] * 3,
        out_specs=VM,
        out_shape=sds((8, PAIR), F32),
        compiler_params=params(),
        cost_estimate=cost(1, 1),
        name="half_squares",
    )(place, early, late, vec)


def directly(value, axis, masks):
    return [swap(value, axis, mask) for mask in masks]


def four(value, others):
    return (value + others[0]) + (others[1] + others[2])


def join(held, arrived):
    return jnp.concatenate([held, arrived], 0)


def squares_of(value):
    value = value.astype(F32)
    return jnp.sum(value * value)


STAGES = (("narrow", 1), ("narrow", 2), ("wide", 1), ("wide", 2), ("wide", 4))


def body(
    tokens, cotangent, cells, present, generate,
    w_qkv, w_out, w_up, w_down, vectors,
    m_qkv, m_out, m_up, m_down, m_vec,
    v_qkv, v_out, v_up, v_down, v_vec,
):
    narrow, wide = lax.axis_size("narrow"), lax.axis_size("wide")
    quick = narrow == 4 and wide == 8
    stages = STAGES if quick else ()
    place = jnp.stack([lax.axis_index("narrow"), lax.axis_index("wide")]).astype(jnp.int32)
    shard = w_qkv.shape[0]

    low_a = pack_first(w_qkv, vectors)
    coded = jnp.where((present == 1) & (generate == 0), cells, cells + HIDDEN)
    tokens, tokens_t, cells, start = turn_tokens(tokens, after(coded, low_a))
    low_b, low_rest = pl.pallas_call(
        pack_second_kernel,
        in_specs=[VM] * 4 + [ANY],
        out_specs=[VM, VM],
        out_shape=[sds((shard, HW), BF), sds((shard, 3 * D), BF)],
        compiler_params=params(),
        name="pack_second",
    )(w_qkv, w_out, w_up, w_down, cells)
    if quick:
        y_a = after(swap(low_a, "narrow", 2), (tokens, low_b))
        pieces_a = [low_a, swap(low_a, "narrow", 1), y_a, swap(y_a, "narrow", 1)]
        y_b = swap(after(low_b, y_a), "narrow", 2)
        c_b = swap(low_b, "narrow", 1)
        y_rest = swap(after(low_rest, y_a), "narrow", 2)
        c_rest = swap(low_rest, "narrow", 1)
        order = [(j, None, j) for j in range(4)]
        vec = jnp.zeros((8, PAIR), BF)
    else:
        pieces_a, pieces_b = [lax.all_gather(low_a, "narrow")], [lax.all_gather(low_b, "narrow")]
        pieces_rest = [lax.all_gather(low_rest, "narrow")]
        order = [(0, j, None) for j in range(narrow)]
        vec = lax.all_gather(vectors.astype(BF), "narrow", axis=1, tiled=True)
        vec = jnp.pad(vec, ((0, 7), (0, 0)))

    *saved_a, w_a, vec_full, tokens = forward_attention(
        0, place, tokens, tokens_t, cells, vec, pieces_a, order
    )
    if quick:
        y_b, c_b = after(y_b, saved_a), after(c_b, saved_a)
        pieces_b = [low_b, c_b, y_b, swap(y_b, "narrow", 1)]
    *saved_b, w_b, vec_full, tokens = forward_attention(
        GROUP, place, tokens, tokens_t, cells, vec_full, pieces_b, order
    )
    cotangent = turn_cotangent(start, cotangent, [saved_b[0]])
    if quick:
        y_rest, c_rest = after(y_rest, (saved_b, cotangent)), after(c_rest, saved_b)
        pieces_rest = [low_rest, c_rest, y_rest, swap(y_rest, "narrow", 1)]
    mixed, d_h1, d_t, vec_sums, *inner = middle(
        place, tokens, cotangent, (saved_a[0], saved_b[0]), vec_full, pieces_rest, order
    )
    sets = [saved_a, saved_b]
    plan = [(pair // GROUP, pair % GROUP, pair) for pair in range(PAIRS)]
    trio_a, vec_sums, *early = backward_attention(
        plan[:FIRST], False, place, cells, tokens_t, vec_sums, sets, d_t, inner, narrow, stages, []
    )
    later = []
    if quick:
        e_keep, e_send = early
        mixed = turn_back(start, mixed, [trio_a])
        e_keep, e_send = fold(e_keep, after(swap(e_send, "narrow", 1), mixed))
        e_arrived = swap(e_send, "narrow", 2)
        later = [e_send]
    trio_b, vec_sums, *late = backward_attention(
        plan[FIRST:], True, place, cells, tokens_t, vec_sums, sets, d_t, [], narrow, stages, later
    )
    weights, trios = (w_a, w_b), (trio_a, trio_b)

    if quick:
        b_keep, b_send = late
        b_arrived = swap(b_send, "narrow", 1)
        e_keep, e_send = fold(e_keep, after(e_arrived, trio_b))
        e_arrived = swap(e_send, "wide", 1)
        b_keep, b_send = fold(b_keep, after(b_arrived, e_send))
        b_arrived = swap(b_send, "narrow", 2)
        input_grad = input_gradient(start, weights, d_h1, trios, [b_send, e_send])
        e_keep, e_send = fold(e_keep, after(e_arrived, input_grad))
        e_arrived = swap(e_send, "wide", 2)
        b_keep, b_send = fold(b_keep, after(b_arrived, e_send))
        b_arrived = swap(b_send, "wide", 1)
        e_keep, e_send = fold(e_keep, after(e_arrived, b_send))
        e_arrived = swap(e_send, "wide", 4)
        b_keep, b_send = fold(b_keep, after(b_arrived, e_send))
        b_arrived = swap(b_send, "wide", 2)
        e_low = add_low(e_keep, after(e_arrived, b_send))
        e_arrived = swap(e_low, "wide", 4)
        b_keep, b_send = fold(b_keep, after(b_arrived, e_low))
        b_arrived = swap(b_send, "wide", 4)
        e_low = join(e_low, after(e_arrived, b_send))
        e_arrived = swap(e_low, "wide", 2)
        b_arrived = after(b_arrived, e_low)
        vec_total = b_keep[:, LATE:].astype(F32) + b_arrived[:, LATE:].astype(F32)
        b_low = add_low(b_keep[:, :LATE], b_arrived[:, :LATE])
        b_arrived = swap(b_low, "wide", 4)
        e_low = join(e_low, after(e_arrived, b_low))
        b_low = join(b_low, after(b_arrived, e_low))
        b_low = join(b_low, swap(b_low, "wide", 2))
        e_arrived, b_arrived = swap(e_low, "wide", 1), swap(b_low, "wide", 1)
        squares = half_squares(place, e_low, b_low, vec_total)
        squares = four(squares, directly(squares, "narrow", (1, 2, 3)))
        squares = squares + swap(squares, "wide", 1)
        grads = [e_low, after(e_arrived, squares), b_low, after(b_arrived, squares)]
    else:
        input_grad, mixed = input_gradient(start, weights, d_h1, trios, []), turn_back(start, mixed, [])
        vec_total = lax.psum_scatter(vec_sums, "narrow", scatter_dimension=1, tiled=True)
        vec_total = lax.psum(vec_total, "wide")
        grads = []
        for every in (early[0], late[0]):
            total = lax.psum_scatter(every, "narrow", scatter_dimension=0, tiled=True)
            grads.append(lax.psum(total.astype(F32), "wide"))
        squares = lax.psum(sum(squares_of(v) for v in grads + [vec_total]), "narrow")
        squares = jnp.full((8, PAIR), squares, F32)
    *updated, grad_norm = adam_step(
        place, squares, math.sqrt(TOK_DEV * wide * narrow), grads, vec_total,
        (w_qkv, w_out, w_up, w_down, vectors),
        (m_qkv, m_out, m_up, m_down, m_vec),
        (v_qkv, v_out, v_up, v_down, v_vec),
        quick,
    )
    return (mixed, input_grad, grad_norm[0, 0], *updated)


def solution(mesh):
    split = P(("wide", "narrow"), None)
    state = (P("narrow", None),) * 4 + (P(None, "narrow"),)
    return jax.shard_map(
        body,
        mesh=mesh,
        in_specs=(split,) * 5 + state * 3,
        out_specs=(split, split, P()) + state * 4,
        check_vma=False,
    )
```

```python
import functools
import math

import jax
import jax.numpy as jnp
from jax import lax
from jax.experimental import pallas as pl
from jax.experimental.pallas import tpu as pltpu
from jax.sharding import PartitionSpec as P

D = 512
HEADS = 8
HEAD_DIM = 64
PAIR = 2 * HEAD_DIM
PAIRS = HEADS // 2
TRIO = 3 * PAIR
TOK_DEV = 1024
QT = 256
HALF = TOK_DEV // 2
TILES = 1
MT = 512
STEP = 10
NORM_EPS = 1e-05
ADAM_EPS = 1e-08
MASKED = -1e30
HIDDEN = 16
BF = jnp.bfloat16
F32 = jnp.float32
MIB = 1024 * 1024
GROUP = 2
HW = GROUP * TRIO
FIRST = 1
LATE = (PAIRS - FIRST) * TRIO
FORWARD_MIB, MIDDLE_MIB, BACKWARD_MIB = 12, 13, 20

NN = (((1,), (0,)), ((), ()))
NT = (((1,), (1,)), ((), ()))
TN = (((0,), (0,)), ((), ()))


def dot(a, b, dims):
    return lax.dot_general(a, b, dims, preferred_element_type=F32)


def params(mib=8):
    return pltpu.CompilerParams(vmem_limit_bytes=mib * MIB)


def sds(shape, dtype):
    return jax.ShapeDtypeStruct(shape, dtype)


SMEM = pl.BlockSpec(memory_space=pltpu.SMEM)
VM = pl.BlockSpec(memory_space=pltpu.VMEM)
ANY = pl.BlockSpec(memory_space=pl.ANY)
HBM = pl.BlockSpec(memory_space=pltpu.HBM)


def whole(shape):
    return pl.BlockSpec(shape, lambda i: (0,) * len(shape))


def cost(flops, moved, exps=0):
    return pl.CostEstimate(flops=int(flops), bytes_accessed=int(moved), transcendentals=int(exps))


def fetch(pairs, sems):
    copies = [
        pltpu.make_async_copy(source, target, sems.at[number])
        for number, (source, target) in enumerate(pairs)
    ]
    for copy in copies:
        copy.start()
    return copies


def trio_columns(base):
    return [
        (local * TRIO + t * PAIR, t * D + (base + local) * PAIR)
        for local in range(GROUP)
        for t in range(3)
    ]


def pack_first_kernel(w_hbm, vec_hbm, out_ref, w_ref, vec_ref, sems):
    rows, vec_cols = w_hbm.shape[0], vec_hbm.shape[1]
    width = GROUP * PAIR
    copies = fetch(
        [(w_hbm.at[:, t * D : t * D + width], w_ref.at[t]) for t in range(3)] + [(vec_hbm, vec_ref)], sems
    )
    for copy in copies:
        copy.wait()
    for local in range(GROUP):
        for t in range(3):
            target = local * TRIO + t * PAIR
            out_ref[:rows, target : target + PAIR] = w_ref[t, :, local * PAIR : (local + 1) * PAIR].astype(BF)
    out_ref[rows:, :] = jnp.zeros((16, HW), BF)
    vec = jnp.concatenate([vec_ref[...], jnp.zeros((7, vec_cols), F32)], 0)
    out_ref[rows:, :vec_cols] = vec.astype(BF)


def pack_first(w_qkv, vectors):
    rows = w_qkv.shape[0]
    return pl.pallas_call(
        pack_first_kernel,
        in_specs=[HBM, HBM],
        out_specs=VM,
        out_shape=sds((rows + 16, HW), BF),
        scratch_shapes=[
            pltpu.VMEM((3, rows, GROUP * PAIR), F32),
            pltpu.VMEM(vectors.shape, F32),
            pltpu.SemaphoreType.DMA((4,)),
        ],
        compiler_params=params(60),
        name="pack_first",
    )(w_qkv, vectors)


def pack_second_kernel(w_ref, w_out_ref, w_up_ref, w_down_ref, *refs):
    second_ref, rest_ref = refs[-2:]
    for target, source in trio_columns(GROUP):
        second_ref[:, target : target + PAIR] = w_ref[:, source : source + PAIR].astype(BF)
    rest_ref[:, :D] = w_out_ref[...].astype(BF)
    rest_ref[:, D : 2 * D] = w_up_ref[...].astype(BF)
    rest_ref[:, 2 * D :] = w_down_ref[...].astype(BF)


def pick(piece, lead, rows):
    return piece[rows, :] if lead is None else piece[lead, rows, :]


def assemble(order, pieces, place, w_full):
    rows = D // len(order)
    for number, (piece, lead, mask) in enumerate(order):
        at = number if mask is None else jnp.bitwise_xor(place[0], mask)
        w_full[pl.ds(pl.multiple_of(at * rows, rows), rows), :] = pick(
            pieces[piece], lead, slice(0, rows)
        )


def turn_rows(source, start, write):
    blocks = source.shape[0] // 8
    whole_blocks, rest = start >> 3, start & 7
    inside = lax.broadcasted_iota(jnp.int32, (8, source.shape[1]), 0) < 8 - rest

    def rolled(block):
        at = pl.multiple_of(((block + whole_blocks) & (blocks - 1)) * 8, 8)
        return pltpu.roll(source[pl.ds(at, 8), :], (8 - rest) & 7, 0)

    def step(i, first):
        second, third = rolled(2 * i + 1), rolled(2 * i + 2)
        write(i, jnp.where(inside, first, second), jnp.where(inside, second, third))
        return third

    lax.fori_loop(0, blocks // 2, step, rolled(0), unroll=8)


def write_into(out):
    def write(i, upper, lower):
        at = pl.multiple_of(i * 16, 16)
        out[pl.ds(at, 16), :] = jnp.concatenate([upper, lower], 0).astype(out.dtype)

    return write


def turn_tokens_kernel(tokens, coded, *refs):
    tokens_out, turned_out, cells_out, start_out, wide_tokens = refs[-5:]
    seen = coded[...] < HIDDEN
    cell = jnp.where(seen, coded[...], coded[...] - HIDDEN)
    start = jnp.int32(TOK_DEV)
    for c in range(4):
        size = jnp.sum((cell == c).astype(jnp.int32))
        first = jnp.sum((cell < c).astype(jnp.int32))
        start = jnp.where(size == HALF, jnp.minimum(start, first), start)
    start_out[0] = start
    shift = jnp.where(start == 0, 0, TOK_DEV - start)
    row = lax.broadcasted_iota(jnp.int32, (8, TOK_DEV), 0)
    cells_out[...] = pltpu.roll(jnp.where((row == 0) | seen, cell, -1), shift, 1)
    wide_tokens[...] = tokens[...].astype(F32)
    turn_rows(wide_tokens, start, write_into(tokens_out))
    turned_out[...] = tokens_out[...].T


def turn_tokens(tokens, coded):
    return pl.pallas_call(
        turn_tokens_kernel,
        in_specs=[VM, VM],
        out_specs=[VM] * 3 + [SMEM],
        out_shape=[
            sds((TOK_DEV, D), BF),
            sds((D, TOK_DEV), BF),
            sds((8, TOK_DEV), jnp.int32),
            sds((1,), jnp.int32),
        ],
        scratch_shapes=[pltpu.VMEM((TOK_DEV, D), F32)],
        compiler_params=params(),
        cost_estimate=cost(1e7, 3e6),
        name="turn_tokens",
    )(tokens, coded)


def turn_cotangent_kernel(start, cot_ref, *refs):
    turn_rows(cot_ref, start[0], write_into(refs[-1]))


def turn_cotangent(start, cot, later):
    return pl.pallas_call(
        turn_cotangent_kernel,
        in_specs=[SMEM, VM] + [ANY] * len(later),
        out_specs=VM,
        out_shape=sds((TOK_DEV, D), F32),
        compiler_params=params(),
        cost_estimate=cost(1e7, 4e6),
        name="turn_cotangent",
    )(start, cot, *later)


def turn_back_kernel(start, source, *refs):
    turned, wide_source = refs[-2:]
    back = (TOK_DEV - start[0]) & (TOK_DEV - 1)
    if source.dtype == F32:
        turn_rows(source, back, write_into(turned))
    else:
        wide_source[...] = source[...].astype(F32)
        turn_rows(wide_source, back, write_into(turned))


def turn_back(start, value, later):
    scratch = (8, PAIR) if value.dtype == F32 else value.shape
    return pl.pallas_call(
        turn_back_kernel,
        in_specs=[SMEM, VM] + [ANY] * len(later),
        out_specs=VM,
        out_shape=sds(value.shape, value.dtype),
        scratch_shapes=[pltpu.VMEM(scratch, F32)],
        compiler_params=params(),
        cost_estimate=cost(1, 1),
        name="turn_back",
    )(start, value, *later)


def make_bias(cells_ref, bias):
    for half in range(2):
        mine = slice(half * HALF, (half + 1) * HALF)
        number = lax.broadcasted_iota(jnp.int32, (16, HALF), 0)
        of_key = jnp.where(cells_ref[1:2, mine] == number, 1.0, 0.0).astype(BF)
        of_query = jnp.where(cells_ref[0:1, mine] == number, 1.0, 0.0).astype(BF)
        keys = lax.broadcasted_iota(jnp.int32, (HALF, HALF), 0)
        queries = lax.broadcasted_iota(jnp.int32, (HALF, HALF), 1)
        seen = (dot(of_key, of_query, TN) > 0.5) | (keys == queries)
        bias[mine, :] = jnp.where(seen, 0.0, MASKED)


def column_of(row):
    eye = lax.broadcasted_iota(jnp.int32, (PAIR, PAIR), 0) == lax.broadcasted_iota(
        jnp.int32, (PAIR, PAIR), 1
    )
    return jnp.sum(jnp.where(eye, row, 0.0), 1, keepdims=True)


def both_heads(pair_t):
    zero = jnp.zeros((HEAD_DIM, pair_t.shape[1]), pair_t.dtype)
    return jnp.concatenate(
        [
            jnp.concatenate([pair_t[:HEAD_DIM], zero], 0),
            jnp.concatenate([zero, pair_t[HEAD_DIM:]], 0),
        ],
        1,
    )


def forward_kernel(order, n_pieces, base, *refs):
    place, tokens, tokens_t, cells_ref, vec_in = refs[:5]
    pieces = refs[5 : 5 + n_pieces]
    att_out, lse_out, krow_out, vrow_out, qt_out, kt_out, w_full, vec_full, tokens_out, bias = refs[
        5 + n_pieces :
    ]
    assemble(order, pieces, place, w_full)
    if vec_in.shape[1] == D:
        vec_full[...] = vec_in[...].astype(F32)
    else:
        rows = D // len(order)
        for piece, lead, mask in order:
            at = pl.multiple_of(jnp.bitwise_xor(place[0], mask) * rows, rows)
            vec_full[:, pl.ds(at, rows)] = pick(pieces[piece], lead, slice(rows, rows + 16))[
                :, :rows
            ].astype(F32)
    make_bias(cells_ref, bias)
    x = tokens[...]
    tokens_out[...] = x
    halves = [slice(0, HALF), slice(HALF, TOK_DEV)]
    chains = []
    for local in range(GROUP):
        lane = slice((base + local) * PAIR, (base + local + 1) * PAIR)
        w = w_full[:, local * TRIO : (local + 1) * TRIO]
        b_q = vec_full[0:1, lane]
        b_v = vec_full[1:2, lane]
        trio = dot(w, tokens_t[...], TN)
        rows = dot(x, w[:, PAIR:], NN)
        here = slice(local * PAIR, (local + 1) * PAIR)
        q_t = ((trio[:PAIR] + column_of(b_q)) * (HEAD_DIM**-0.5)).astype(BF)
        v_t = (trio[2 * PAIR :] + column_of(b_v)).astype(BF)
        k_row = rows[:, :PAIR].astype(BF)
        krow_out[local] = k_row
        vrow_out[local] = (rows[:, PAIR:] + b_v).astype(BF)
        qt_out[here, :] = q_t
        kt_out[here, :] = trio[PAIR : 2 * PAIR].astype(BF)
        chains += [(local, mine, q_t, v_t, k_row) for mine in halves]

    def scores(chain):
        local, mine, q_t, v_t, k_row = chain
        return dot(k_row[mine], both_heads(q_t[:, mine]), NN)

    ahead = scores(chains[0])
    for number, (local, mine, q_t, v_t, k_row) in enumerate(chains):
        s = ahead
        if number + 1 < len(chains):
            ahead = scores(chains[number + 1])
        mask = bias[mine, :]
        s = s + jnp.concatenate([mask, mask], 1)
        top = jnp.max(s, 0, keepdims=True)
        e = jnp.exp(s - top)
        total = jnp.sum(e, 0, keepdims=True)
        lse = top + jnp.log(total)
        e_low = e.astype(BF)
        for h in range(2):
            cols = slice(h * HALF, (h + 1) * HALF)
            head = slice(h * HEAD_DIM, (h + 1) * HEAD_DIM)
            o = dot(v_t[head, mine], e_low[:, cols], NN)
            at = local * PAIR + h * HEAD_DIM
            att_out[at : at + HEAD_DIM, mine] = (o / total[:, cols]).astype(BF)
            lse_out[local, h : h + 1, mine] = lse[:, cols]


def forward_attention(base, place, tokens, tokens_t, cells, vec, pieces, order):
    wide_t, tall = sds((GROUP * PAIR, TOK_DEV), BF), sds((GROUP, TOK_DEV, PAIR), BF)
    return pl.pallas_call(
        functools.partial(forward_kernel, order, len(pieces), base),
        in_specs=[SMEM] + [VM] * (4 + len(pieces)),
        out_specs=[VM] * 9,
        out_shape=[
            wide_t, sds((GROUP, 8, TOK_DEV), F32), tall, tall, wide_t, wide_t, sds((D, HW), BF), sds((16, D), F32),
            sds((TOK_DEV, D), BF),
        ],
        scratch_shapes=[pltpu.VMEM((TOK_DEV, HALF), F32)],
        compiler_params=params(FORWARD_MIB),
        cost_estimate=cost(1, 1),
        name="forward_attention",
    )(place, tokens, tokens_t, cells, vec, *pieces)


def normalize(value):
    center = value - jnp.mean(value, -1, keepdims=True)
    inverse = lax.rsqrt(jnp.mean(center * center, -1, keepdims=True) + NORM_EPS)
    return center * inverse, inverse


def normalize_back(grad, normal, inverse):
    return inverse * (
        grad
        - jnp.mean(grad, -1, keepdims=True)
        - normal * jnp.mean(grad * normal, -1, keepdims=True)
    )


def column_sum(value):
    return jnp.sum(value, 0, keepdims=True)


def row_sources(place, n_shards, stages):
    if not stages:
        return [(0, 0, D)]
    rows = D // n_shards
    piece = D >> len(stages)
    found = []
    for block in range(1 << len(stages)):
        masks = {"narrow": 0, "wide": 0}
        for number, (axis, mask) in enumerate(stages):
            if block >> (len(stages) - 1 - number) & 1:
                masks[axis] |= mask
        source = jnp.bitwise_xor(place[0], masks["narrow"]) * rows
        if piece < rows:
            source = source + jnp.bitwise_xor(place[1], masks["wide"]) * piece
        found.append((block * piece, pl.multiple_of(source, piece), piece))
    return found


def store_rows(outs, place, n_shards, stages, matrix, cols):
    height = outs[0].shape[0]
    for target, source, rows in row_sources(place, n_shards, stages):
        out = outs[target // height]
        at = target % height
        out[at : at + rows, cols] = matrix[pl.ds(source, rows), :].astype(BF)


def gelu_parts(value):
    density = jnp.exp(-0.5 * value * value)
    t = 1.0 / (1.0 + (0.3275911 / math.sqrt(2.0)) * jnp.abs(value))
    poly = 1.061405429
    for factor in (-1.453152027, 1.421413741, -0.284496736, 0.254829592):
        poly = poly * t + factor
    tail = 0.5 * poly * t * density
    return jnp.where(value >= 0.0, 1.0 - tail, tail), value * density * (1.0 / math.sqrt(2.0 * math.pi))


def middle_kernel(order, n_pieces, *refs):
    place, tokens, cot_ref, att_a, att_b, vec_ref = refs[:6]
    pieces = refs[6 : 6 + n_pieces]
    mixed_out, dh1_out, datt_out, vec_out = refs[6 + n_pieces : 10 + n_pieces]
    first_all, hidden_all, branch_all, pre_all, down_all = refs[10 + n_pieces : 15 + n_pieces]
    w_full, sums = refs[15 + n_pieces :]
    step = pl.program_id(0)

    @pl.when(step == 0)
    def _():
        assemble(order, pieces, place, w_full)
        sums[...] = jnp.zeros_like(sums)

    w_out, w_up, w_down = w_full[:, :D], w_full[:, D : 2 * D], w_full[:, 2 * D :]

    def vec(row):
        return vec_ref[row : row + 1, :]

    def tile(number):
        at = pl.ds(pl.multiple_of(step * (TILES * MT) + number * MT, MT), MT)
        att_t = jnp.concatenate([att_a[:, at], att_b[:, at]], 0)
        branch = dot(att_t, w_out, TN)
        yield
        normal_1, inverse_1 = normalize(tokens[at, :].astype(F32) + (branch + vec(2)))
        first = normal_1 * vec(5) + vec(6)
        first_low = first.astype(BF)
        first_all[at, :] = first_low
        pre = dot(first_low, w_up, NN)
        yield
        pre = pre + vec(3)
        cdf, bump = gelu_parts(pre)
        hidden = (pre * cdf).astype(BF)
        hidden_all[at, :] = hidden
        slope = cdf + bump
        down = dot(hidden, w_down, NN)
        yield
        normal_2, inverse_2 = normalize(first + (down + vec(4)))
        mixed_out[at, :] = (normal_2 * vec(7) + vec(8)).astype(BF)
        cot = cot_ref[at, :]
        d_h2 = normalize_back(cot * vec(7), normal_2, inverse_2)
        d_down = d_h2.astype(BF)
        down_all[at, :] = d_down
        d_hidden = dot(d_down, w_down, NT)
        yield
        sums[7:8, :] += column_sum(cot * normal_2)
        sums[8:9, :] += column_sum(cot)
        d_pre = (d_hidden * slope).astype(BF)
        pre_all[at, :] = d_pre
        d_up = dot(d_pre, w_up, NT)
        yield
        d_first = d_h2 + d_up
        d_h1 = normalize_back(d_first * vec(5), normal_1, inverse_1)
        dh1_out[at, :] = d_h1
        d_branch = d_h1.astype(BF)
        branch_all[at, :] = d_branch
        datt_out[:, at] = dot(w_out, d_branch, NT).astype(BF)
        yield
        sums[5:6, :] += column_sum(d_first * normal_1)
        sums[6:7, :] += column_sum(d_first)

    tiles = [tile(number) for number in range(TILES)]
    while tiles:
        tiles = [one for one in tiles if next(one, True) is None]

    @pl.when(step == pl.num_programs(0) - 1)
    def _():
        ones = jnp.ones((16, TOK_DEV), BF)
        sums[2:3, :] = dot(ones, branch_all[...], NN)[:1]
        sums[3:4, :] = dot(ones, pre_all[...], NN)[:1]
        sums[4:5, :] = dot(ones, down_all[...], NN)[:1]
        vec_out[...] = sums[...]


def middle(place, tokens, cot, atts, vec, pieces, order):
    height = TILES * MT
    return pl.pallas_call(
        functools.partial(middle_kernel, order, len(pieces)),
        grid=(TOK_DEV // height,),
        in_specs=[SMEM] + [VM] * (5 + len(pieces)),
        out_specs=[VM] * 9,
        out_shape=[
            sds((TOK_DEV, D), BF),
            sds((TOK_DEV, D), F32),
            sds((D, TOK_DEV), BF),
            sds((16, D), F32),
        ]
        + [sds((TOK_DEV, D), BF)] * 5,
        scratch_shapes=[pltpu.VMEM((D, 3 * D), BF), pltpu.VMEM((16, D), F32)],
        compiler_params=params(MIDDLE_MIB),
        cost_estimate=cost(1e10, 1.2e7, 2**20),
        name="middle",
    )(place, tokens, cot, *atts, vec, *pieces)


def backward_kernel(n_shards, stages, plan, n_sets, n_inner, last, place, cells_ref, tokens_t, vec_ref,
                    datt_ref, *refs):
    sets = [refs[6 * number : 6 * (number + 1)] for number in range(n_sets)]
    inner = refs[6 * n_sets : 6 * n_sets + n_inner]
    bias, dw = refs[-2:]
    n_g = 2 if stages else 1
    d_out, vec = refs[-4 - n_g : -2 - n_g]
    g_outs = refs[-2 - n_g : -2]
    make_bias(cells_ref, bias)
    vec[...] = vec_ref[...]
    halves = [slice(0, HALF), slice(HALF, TOK_DEV)]
    chains = [(place_out, *entry, mine) for place_out, entry in enumerate(plan) for mine in halves]

    def scores(chain):
        _, number, local, pair, mine = chain
        att_ref, lse_ref, krow_ref, vrow_ref, qt_ref, kt_ref = sets[number]
        here = slice(local * PAIR, (local + 1) * PAIR)
        q_t, d_t = qt_ref[here, mine], datt_ref[pair * PAIR : (pair + 1) * PAIR, mine]
        s = dot(krow_ref[local, mine, :], both_heads(q_t), NN)
        return q_t, d_t, s, dot(vrow_ref[local, mine, :], both_heads(d_t), NN)

    first = 0
    if inner:
        first = 3 * D
        first_all, hidden_all, branch_all, pre_all, down_all = inner
        attended = jnp.concatenate([sets[0][0][...], sets[1][0][...]], 0)
        products = [
            dot(attended, branch_all[...], NN),
            dot(first_all[...], pre_all[...], TN),
            dot(hidden_all[...], down_all[...], TN),
        ]
        for number, product in enumerate(products):
            dw[number % 2] = product
            cols = slice(number * D, (number + 1) * D)
            store_rows(g_outs, place, n_shards, stages, dw.at[number % 2], cols)
    ahead = scores(chains[0])
    for step, (place_out, number, local, pair, mine) in enumerate(chains):
        q_t, d_t, s, d_prob = ahead
        if step + 1 < len(chains):
            ahead = scores(chains[step + 1])
        att_ref, lse_ref, krow_ref, vrow_ref, qt_ref, kt_ref = sets[number]
        mask = bias[mine, :]
        lse = jnp.concatenate([lse_ref[local, 0:1, mine], lse_ref[local, 1:2, mine]], 1)
        here = slice(local * PAIR, (local + 1) * PAIR)
        product = d_t.astype(F32) * att_ref[here, mine].astype(F32)
        delta = jnp.concatenate([column_sum(product[:HEAD_DIM]), column_sum(product[HEAD_DIM:])], 1)
        prob = jnp.exp(s + jnp.concatenate([mask, mask], 1) - lse)
        d_s = (prob * (d_prob - delta)).astype(BF)
        prob_low = prob.astype(BF)
        for h in range(2):
            cols = slice(h * HALF, (h + 1) * HALF)
            head = slice(h * HEAD_DIM, (h + 1) * HEAD_DIM)
            k_t = kt_ref[local * PAIR + h * HEAD_DIM : local * PAIR + (h + 1) * HEAD_DIM, mine]
            d_q = dot(k_t, d_s[:, cols], NN) * (HEAD_DIM**-0.5)
            d_k = dot(q_t[head], d_s[:, cols], NT)
            d_v = dot(d_t[head], prob_low[:, cols], NT)
            for t, value in enumerate((d_q, d_k, d_v)):
                at = t * PAIR + h * HEAD_DIM
                d_out[place_out, at : at + HEAD_DIM, mine] = value.astype(BF)
        if mine.start == 0:
            continue
        trio = d_out[place_out]
        dw[place_out % 2, :, :TRIO] = dot(tokens_t[...], trio, NT)
        at = first + place_out * TRIO
        store_rows(
            g_outs, place, n_shards, stages, dw.at[place_out % 2, :, :TRIO], slice(at, at + TRIO)
        )
        total = dot(jnp.ones((16, TOK_DEV), BF), trio, NT)
        lanes = slice(pair * PAIR, (pair + 1) * PAIR)
        vec[0:1, lanes] = total[:1, :PAIR]
        vec[1:2, lanes] = total[:1, 2 * PAIR :]
    if stages and last:
        height = g_outs[0].shape[0]
        rows = D // n_shards
        for target, source, count in row_sources(place, n_shards, stages):
            at = pl.multiple_of(source // rows * rows, rows)
            g_outs[target // height][target % height : target % height + count, LATE:] = vec[
                :, pl.ds(at, rows)
            ].astype(BF)


def backward_attention(plan, last, place, cells, tokens_t, vec_sums, sets, d_t, inner, n_shards, stages, later):
    width = len(plan) * TRIO + (3 * D if inner else 0)
    if stages:
        shapes = [sds((D // 2, width + (PAIR if last else 0)), BF)] * 2
    else:
        shapes = [sds((D, width), BF)]
    flat = [value for saved in sets for value in saved]
    return pl.pallas_call(
        functools.partial(backward_kernel, n_shards, stages, plan, len(sets), len(inner), last),
        in_specs=[SMEM] + [VM] * (4 + len(flat) + len(inner)) + [ANY] * len(later),
        out_specs=[VM] * (2 + len(shapes)),
        out_shape=[sds((len(plan), TRIO, TOK_DEV), BF), sds((16, D), F32)] + shapes,
        scratch_shapes=[pltpu.VMEM((TOK_DEV, HALF), F32), pltpu.VMEM((2, D, D), F32)],
        compiler_params=params(BACKWARD_MIB),
        cost_estimate=cost(5e9 * len(plan), 8e6, 2**21),
        name="backward_attention",
    )(place, cells, tokens_t, vec_sums, d_t, *flat, *inner, *later)


def input_grad_kernel(start, w_a, w_b, dh1_ref, trio_a, trio_b, *refs):
    out, turned = refs[-2:]
    trios = [ref.at[number] for ref in (trio_a, trio_b) for number in range(ref.shape[0])]
    for tile in range(TOK_DEV // QT):
        here = slice(tile * QT, (tile + 1) * QT)
        total = None
        for w_ref, parts in ((w_a, trios[:GROUP]), (w_b, trios[GROUP:])):
            term = dot(w_ref[...], jnp.concatenate([part[:, here] for part in parts], 0), NN)
            total = term if total is None else total + term
        turned[here, :] = dh1_ref[here, :] + total.T
    turn_rows(turned, (TOK_DEV - start[0]) & (TOK_DEV - 1), write_into(out))


def input_gradient(start, weights, d_h1, trios, later):
    return pl.pallas_call(
        input_grad_kernel,
        in_specs=[SMEM] + [VM] * 5 + [ANY] * len(later),
        out_specs=VM,
        out_shape=sds((TOK_DEV, D), F32),
        scratch_shapes=[pltpu.VMEM((TOK_DEV, D), F32)],
        compiler_params=params(),
        cost_estimate=cost(1, 1),
        name="input_gradient",
    )(start, *weights, d_h1, *trios, *later)


def adam(weight, grad, first, second, rate, decay):
    first = 0.5 * first + 0.5 * grad
    second = 0.5 * second + 0.5 * grad * grad
    fix = 1.0 - 0.5**STEP
    update = first * (1.0 / fix) / (jnp.sqrt(second * (1.0 / fix)) + ADAM_EPS)
    return weight - rate * (update + decay * weight), first, second


def pair_parts(first, pairs):
    return [
        (slice(at, at + PAIR), 0, t * D + pair * PAIR)
        for number, pair in enumerate(pairs)
        for t in range(3)
        for at in [first + number * TRIO + t * PAIR]
    ]


EARLY_PARTS = [(slice(i * D, (i + 1) * D), i + 1, 0) for i in range(3)] + pair_parts(3 * D, range(FIRST))
LATE_PARTS = pair_parts(0, range(FIRST, PAIRS))


def adam_kernel(quick, limit, place, square_ref, *refs):
    n_grads = 4 if quick else 2
    grads = refs[:n_grads]
    vec_ref = refs[n_grads]
    states = refs[n_grads + 1 : n_grads + 16]
    outs = refs[n_grads + 16 : n_grads + 36]
    norm_out = refs[-1]
    step = pl.program_id(0)
    norm = jnp.sqrt(square_ref[0:1, 0:1])
    factor = limit / jnp.maximum(norm, limit)

    def write(number, where, target, grad, rate, decay):
        new, first, second = adam(
            states[number][where], grad * factor, states[5 + number][where],
            states[10 + number][where], rate, decay,
        )
        outs[number][target] = new
        outs[5 + number][target] = first
        outs[10 + number][target] = second
        outs[15 + number][target] = new.astype(BF)

    height = outs[0].shape[0]
    pieces = height // 16 if quick else 1
    rows = height // pieces
    for piece in range(pieces):
        here = pl.multiple_of(step * height + piece * rows, rows)
        if quick:
            mask = jnp.bitwise_xor(place[1], step * pieces + piece)
            at = pl.multiple_of(((mask >> 2) & 1) * 16 + ((mask >> 1) & 1) * 32, 16)
            odd = (mask & 1) == 1
        else:
            at = here
        for group, parts in enumerate((EARLY_PARTS, LATE_PARTS)):
            for cols, number, first in parts:
                if quick:
                    low, high = grads[2 * group], grads[2 * group + 1]
                    grad = jnp.where(odd, high[pl.ds(at, rows), cols], low[pl.ds(at, rows), cols])
                else:
                    grad = grads[group][pl.ds(at, rows), cols]
                there = slice(first, first + cols.stop - cols.start)
                write(
                    number, (pl.ds(here, rows), there), (slice(piece * rows, (piece + 1) * rows), there),
                    grad.astype(F32), 0.1, 0.01,
                )

    @pl.when(step == 0)
    def _():
        norm_out[0, 0] = norm[0, 0]
        vec_cols = states[4].shape[1]
        where = (slice(0, 9), slice(0, vec_cols))
        write(4, where, where, vec_ref[0:9, :vec_cols].astype(F32), 0.5, 0.0)


def adam_step(place, squares, limit, grads, vec_grad, weights, firsts, seconds, quick):
    steps = 4

    def spec(value):
        if value.shape[0] == 9:
            return whole(value.shape)
        return pl.BlockSpec((value.shape[0] // steps, value.shape[1]), lambda i: (i, 0))

    state = [spec(w) for w in weights]
    shapes = [sds(w.shape, F32) for w in weights]
    return pl.pallas_call(
        functools.partial(adam_kernel, quick, limit),
        grid=(steps,),
        in_specs=[SMEM] + [VM] * (17 + len(grads)),
        out_specs=state * 4 + [SMEM],
        out_shape=shapes * 3 + [sds(w.shape, BF) for w in weights] + [sds((1, 1), F32)],
        compiler_params=params(),
        name="adam",
    )(place, squares, *grads, vec_grad, *weights, *firsts, *seconds)


def swap(value, axis, mask):
    size = lax.axis_size(axis)
    return lax.ppermute(value, axis, [(i, i ^ mask) for i in range(size)])


def add_low(a, b):
    return (a.astype(F32) + b.astype(F32)).astype(BF)


def after(value, *others):
    return lax.optimization_barrier((value, others))[0]


def fold(keep, arrived):
    rows = keep.shape[0] // 2
    send = add_low(keep[rows:], arrived[rows:])
    return add_low(keep[:rows], arrived[:rows]), send


def squares_kernel(place, early, late, vec, out):
    total = []
    for piece in range(4):
        rows = slice(16 * piece, 16 * (piece + 1))
        first, second = early[rows, :].astype(F32), late[rows, :].astype(F32)
        total.append(jnp.sum(first * first) + jnp.sum(second * second))
    total = (total[0] + total[1]) + (total[2] + total[3])
    total = total + jnp.where((place[1] & 1) == 0, jnp.sum(vec[...] * vec[...]), 0.0)
    out[...] = jnp.full(out.shape, total, F32)


def half_squares(place, early, late, vec):
    return pl.pallas_call(
        squares_kernel,
        in_specs=[SMEM] + [VM] * 3,
        out_specs=VM,
        out_shape=sds((8, PAIR), F32),
        compiler_params=params(),
        cost_estimate=cost(1, 1),
        name="half_squares",
    )(place, early, late, vec)


def directly(value, axis, masks):
    return [swap(value, axis, mask) for mask in masks]


def four(value, others):
    return (value + others[0]) + (others[1] + others[2])


def join(held, arrived):
    return jnp.concatenate([held, arrived], 0)


def squares_of(value):
    value = value.astype(F32)
    return jnp.sum(value * value)


STAGES = (("narrow", 1), ("narrow", 2), ("wide", 1), ("wide", 2), ("wide", 4))


def body(
    tokens, cotangent, cells, present, generate,
    w_qkv, w_out, w_up, w_down, vectors,
    m_qkv, m_out, m_up, m_down, m_vec,
    v_qkv, v_out, v_up, v_down, v_vec,
):
    narrow, wide = lax.axis_size("narrow"), lax.axis_size("wide")
    quick = narrow == 4 and wide == 8
    stages = STAGES if quick else ()
    place = jnp.stack([lax.axis_index("narrow"), lax.axis_index("wide")]).astype(jnp.int32)
    shard = w_qkv.shape[0]

    low_a = pack_first(w_qkv, vectors)
    coded = jnp.where((present == 1) & (generate == 0), cells, cells + HIDDEN)
    tokens, tokens_t, cells, start = turn_tokens(tokens, after(coded, low_a))
    low_b, low_rest = pl.pallas_call(
        pack_second_kernel,
        in_specs=[VM] * 4 + [ANY],
        out_specs=[VM, VM],
        out_shape=[sds((shard, HW), BF), sds((shard, 3 * D), BF)],
        compiler_params=params(),
        name="pack_second",
    )(w_qkv, w_out, w_up, w_down, cells)
    if quick:
        y_a = after(swap(low_a, "narrow", 2), (tokens, low_b))
        pieces_a = [low_a, swap(low_a, "narrow", 1), y_a, swap(y_a, "narrow", 1)]
        y_b = swap(after(low_b, y_a), "narrow", 2)
        c_b = swap(low_b, "narrow", 1)
        y_rest = swap(after(low_rest, y_a), "narrow", 2)
        c_rest = swap(low_rest, "narrow", 1)
        order = [(j, None, j) for j in range(4)]
        vec = jnp.zeros((8, PAIR), BF)
    else:
        pieces_a, pieces_b = [lax.all_gather(low_a, "narrow")], [lax.all_gather(low_b, "narrow")]
        pieces_rest = [lax.all_gather(low_rest, "narrow")]
        order = [(0, j, None) for j in range(narrow)]
        vec = lax.all_gather(vectors.astype(BF), "narrow", axis=1, tiled=True)
        vec = jnp.pad(vec, ((0, 7), (0, 0)))

    *saved_a, w_a, vec_full, tokens = forward_attention(
        0, place, tokens, tokens_t, cells, vec, pieces_a, order
    )
    if quick:
        y_b, c_b = after(y_b, saved_a), after(c_b, saved_a)
        pieces_b = [low_b, c_b, y_b, swap(y_b, "narrow", 1)]
    *saved_b, w_b, vec_full, tokens = forward_attention(
        GROUP, place, tokens, tokens_t, cells, vec_full, pieces_b, order
    )
    if quick:
        y_rest, c_rest = after(y_rest, saved_b), after(c_rest, saved_b)
        d_rest = swap(y_rest, "narrow", 1)
        cotangent = turn_cotangent(start, cotangent, [y_rest])
        pieces_rest = [low_rest, c_rest, y_rest, after(d_rest, cotangent)]
    else:
        cotangent = turn_cotangent(start, cotangent, [])
    mixed, d_h1, d_t, vec_sums, *inner = middle(
        place, tokens, cotangent, (saved_a[0], saved_b[0]), vec_full, pieces_rest, order
    )
    sets = [saved_a, saved_b]
    plan = [(pair // GROUP, pair % GROUP, pair) for pair in range(PAIRS)]
    trio_a, vec_sums, *early = backward_attention(
        plan[:FIRST], False, place, cells, tokens_t, vec_sums, sets, d_t, inner, narrow, stages, []
    )
    later = []
    if quick:
        e_keep, e_send = early
        mixed = turn_back(start, mixed, [trio_a])
        e_keep, e_send = fold(e_keep, after(swap(e_send, "narrow", 1), mixed))
        e_arrived = swap(e_send, "narrow", 2)
        later = [e_send]
    trio_b, vec_sums, *late = backward_attention(
        plan[FIRST:], True, place, cells, tokens_t, vec_sums, sets, d_t, [], narrow, stages, later
    )
    weights, trios = (w_a, w_b), (trio_a, trio_b)

    if quick:
        b_keep, b_send = late
        b_arrived = swap(b_send, "narrow", 1)
        e_keep, e_send = fold(e_keep, after(e_arrived, trio_b))
        e_arrived = swap(e_send, "wide", 1)
        b_keep, b_send = fold(b_keep, after(b_arrived, e_send))
        b_arrived = swap(b_send, "narrow", 2)
        input_grad = input_gradient(start, weights, d_h1, trios, [b_send, e_send])
        e_keep, e_send = fold(e_keep, after(e_arrived, input_grad))
        e_arrived = swap(e_send, "wide", 2)
        b_keep, b_send = fold(b_keep, after(b_arrived, e_send))
        b_arrived = swap(b_send, "wide", 1)
        e_keep, e_send = fold(e_keep, after(e_arrived, b_send))
        e_arrived = swap(e_send, "wide", 4)
        b_keep, b_send = fold(b_keep, after(b_arrived, e_send))
        b_arrived = swap(b_send, "wide", 2)
        e_low = add_low(e_keep, after(e_arrived, b_send))
        e_arrived = swap(e_low, "wide", 4)
        b_keep, b_send = fold(b_keep, after(b_arrived, e_low))
        b_arrived = swap(b_send, "wide", 4)
        e_low = join(e_low, after(e_arrived, b_send))
        e_arrived = swap(e_low, "wide", 2)
        b_arrived = after(b_arrived, e_low)
        vec_total = b_keep[:, LATE:].astype(F32) + b_arrived[:, LATE:].astype(F32)
        b_low = add_low(b_keep[:, :LATE], b_arrived[:, :LATE])
        b_arrived = swap(b_low, "wide", 4)
        e_low = join(e_low, after(e_arrived, b_low))
        b_low = join(b_low, after(b_arrived, e_low))
        b_low = join(b_low, swap(b_low, "wide", 2))
        e_arrived, b_arrived = swap(e_low, "wide", 1), swap(b_low, "wide", 1)
        squares = half_squares(place, e_low, b_low, vec_total)
        squares = four(squares, directly(squares, "narrow", (1, 2, 3)))
        squares = squares + swap(squares, "wide", 1)
        grads = [e_low, after(e_arrived, squares), b_low, after(b_arrived, squares)]
    else:
        input_grad, mixed = input_gradient(start, weights, d_h1, trios, []), turn_back(start, mixed, [])
        vec_total = lax.psum_scatter(vec_sums, "narrow", scatter_dimension=1, tiled=True)
        vec_total = lax.psum(vec_total, "wide")
        grads = []
        for every in (early[0], late[0]):
            total = lax.psum_scatter(every, "narrow", scatter_dimension=0, tiled=True)
            grads.append(lax.psum(total.astype(F32), "wide"))
        squares = lax.psum(sum(squares_of(v) for v in grads + [vec_total]), "narrow")
        squares = jnp.full((8, PAIR), squares, F32)
    *updated, grad_norm = adam_step(
        place, squares, math.sqrt(TOK_DEV * wide * narrow), grads, vec_total,
        (w_qkv, w_out, w_up, w_down, vectors),
        (m_qkv, m_out, m_up, m_down, m_vec),
        (v_qkv, v_out, v_up, v_down, v_vec),
        quick,
    )
    return (mixed, input_grad, grad_norm[0, 0], *updated)


def solution(mesh):
    split = P(("wide", "narrow"), None)
    state = (P("narrow", None),) * 4 + (P(None, "narrow"),)
    return jax.shard_map(
        body,
        mesh=mesh,
        in_specs=(split,) * 5 + state * 3,
        out_specs=(split, split, P()) + state * 4,
        check_vma=False,
    )
```

```python
import functools
import math

import jax
import jax.numpy as jnp
from jax import lax
from jax.experimental import pallas as pl
from jax.experimental.pallas import tpu as pltpu
from jax.sharding import PartitionSpec as P

D = 512
HEADS = 8
HEAD_DIM = 64
PAIR = 2 * HEAD_DIM
PAIRS = HEADS // 2
TRIO = 3 * PAIR
TOK_DEV = 1024
QT = 256
HALF = TOK_DEV // 2
TILES = 1
MT = 1024
STEP = 10
NORM_EPS = 1e-05
ADAM_EPS = 1e-08
MASKED = -1e30
HIDDEN = 16
BF = jnp.bfloat16
F32 = jnp.float32
MIB = 1024 * 1024
GROUP = 2
HW = GROUP * TRIO
FIRST = 1
LATE = (PAIRS - FIRST) * TRIO
FORWARD_MIB, MIDDLE_MIB, BACKWARD_MIB = 12, 18, 20

NN = (((1,), (0,)), ((), ()))
NT = (((1,), (1,)), ((), ()))
TN = (((0,), (0,)), ((), ()))


def dot(a, b, dims):
    return lax.dot_general(a, b, dims, preferred_element_type=F32)


def params(mib=8):
    return pltpu.CompilerParams(vmem_limit_bytes=mib * MIB)


def sds(shape, dtype):
    return jax.ShapeDtypeStruct(shape, dtype)


SMEM = pl.BlockSpec(memory_space=pltpu.SMEM)
VM = pl.BlockSpec(memory_space=pltpu.VMEM)
ANY = pl.BlockSpec(memory_space=pl.ANY)
HBM = pl.BlockSpec(memory_space=pltpu.HBM)


def whole(shape):
    return pl.BlockSpec(shape, lambda i: (0,) * len(shape))


def cost(flops, moved, exps=0):
    return pl.CostEstimate(flops=int(flops), bytes_accessed=int(moved), transcendentals=int(exps))


def fetch(pairs, sems):
    copies = [
        pltpu.make_async_copy(source, target, sems.at[number])
        for number, (source, target) in enumerate(pairs)
    ]
    for copy in copies:
        copy.start()
    return copies


def trio_columns(base):
    return [
        (local * TRIO + t * PAIR, t * D + (base + local) * PAIR)
        for local in range(GROUP)
        for t in range(3)
    ]


def pack_first_kernel(w_hbm, vec_hbm, out_ref, w_ref, vec_ref, sems):
    rows, vec_cols = w_hbm.shape[0], vec_hbm.shape[1]
    width = GROUP * PAIR
    copies = fetch(
        [(w_hbm.at[:, t * D : t * D + width], w_ref.at[t]) for t in range(3)] + [(vec_hbm, vec_ref)], sems
    )
    for copy in copies:
        copy.wait()
    for local in range(GROUP):
        for t in range(3):
            target = local * TRIO + t * PAIR
            out_ref[:rows, target : target + PAIR] = w_ref[t, :, local * PAIR : (local + 1) * PAIR].astype(BF)
    out_ref[rows:, :] = jnp.zeros((16, HW), BF)
    vec = jnp.concatenate([vec_ref[...], jnp.zeros((7, vec_cols), F32)], 0)
    out_ref[rows:, :vec_cols] = vec.astype(BF)


def pack_first(w_qkv, vectors):
    rows = w_qkv.shape[0]
    return pl.pallas_call(
        pack_first_kernel,
        in_specs=[HBM, HBM],
        out_specs=VM,
        out_shape=sds((rows + 16, HW), BF),
        scratch_shapes=[
            pltpu.VMEM((3, rows, GROUP * PAIR), F32),
            pltpu.VMEM(vectors.shape, F32),
            pltpu.SemaphoreType.DMA((4,)),
        ],
        compiler_params=params(60),
        name="pack_first",
    )(w_qkv, vectors)


def pack_second_kernel(w_ref, w_out_ref, w_up_ref, w_down_ref, *refs):
    second_ref, rest_ref = refs[-2:]
    for target, source in trio_columns(GROUP):
        second_ref[:, target : target + PAIR] = w_ref[:, source : source + PAIR].astype(BF)
    rest_ref[:, :D] = w_out_ref[...].astype(BF)
    rest_ref[:, D : 2 * D] = w_up_ref[...].astype(BF)
    rest_ref[:, 2 * D :] = w_down_ref[...].astype(BF)


def pick(piece, lead, rows):
    return piece[rows, :] if lead is None else piece[lead, rows, :]


def assemble(order, pieces, place, w_full):
    rows = D // len(order)
    for number, (piece, lead, mask) in enumerate(order):
        at = number if mask is None else jnp.bitwise_xor(place[0], mask)
        w_full[pl.ds(pl.multiple_of(at * rows, rows), rows), :] = pick(
            pieces[piece], lead, slice(0, rows)
        )


def turn_rows(source, start, write):
    blocks = source.shape[0] // 8
    whole_blocks, rest = start >> 3, start & 7
    inside = lax.broadcasted_iota(jnp.int32, (8, source.shape[1]), 0) < 8 - rest

    def rolled(block):
        at = pl.multiple_of(((block + whole_blocks) & (blocks - 1)) * 8, 8)
        return pltpu.roll(source[pl.ds(at, 8), :], (8 - rest) & 7, 0)

    def step(i, first):
        second, third = rolled(2 * i + 1), rolled(2 * i + 2)
        write(i, jnp.where(inside, first, second), jnp.where(inside, second, third))
        return third

    lax.fori_loop(0, blocks // 2, step, rolled(0), unroll=8)


def write_into(out):
    def write(i, upper, lower):
        at = pl.multiple_of(i * 16, 16)
        out[pl.ds(at, 16), :] = jnp.concatenate([upper, lower], 0).astype(out.dtype)

    return write


def turn_tokens_kernel(tokens, coded, *refs):
    tokens_out, turned_out, cells_out, start_out, wide_tokens = refs[-5:]
    seen = coded[...] < HIDDEN
    cell = jnp.where(seen, coded[...], coded[...] - HIDDEN)
    start = jnp.int32(TOK_DEV)
    for c in range(4):
        size = jnp.sum((cell == c).astype(jnp.int32))
        first = jnp.sum((cell < c).astype(jnp.int32))
        start = jnp.where(size == HALF, jnp.minimum(start, first), start)
    start_out[0] = start
    shift = jnp.where(start == 0, 0, TOK_DEV - start)
    row = lax.broadcasted_iota(jnp.int32, (8, TOK_DEV), 0)
    cells_out[...] = pltpu.roll(jnp.where((row == 0) | seen, cell, -1), shift, 1)
    wide_tokens[...] = tokens[...].astype(F32)
    turn_rows(wide_tokens, start, write_into(tokens_out))
    turned_out[...] = tokens_out[...].T


def turn_tokens(tokens, coded):
    return pl.pallas_call(
        turn_tokens_kernel,
        in_specs=[VM, VM],
        out_specs=[VM] * 3 + [SMEM],
        out_shape=[
            sds((TOK_DEV, D), BF),
            sds((D, TOK_DEV), BF),
            sds((8, TOK_DEV), jnp.int32),
            sds((1,), jnp.int32),
        ],
        scratch_shapes=[pltpu.VMEM((TOK_DEV, D), F32)],
        compiler_params=params(),
        cost_estimate=cost(1e7, 3e6),
        name="turn_tokens",
    )(tokens, coded)


def turn_cotangent_kernel(start, cot_ref, *refs):
    turn_rows(cot_ref, start[0], write_into(refs[-1]))


def turn_cotangent(start, cot, later):
    return pl.pallas_call(
        turn_cotangent_kernel,
        in_specs=[SMEM, VM] + [ANY] * len(later),
        out_specs=VM,
        out_shape=sds((TOK_DEV, D), F32),
        compiler_params=params(),
        cost_estimate=cost(1e7, 4e6),
        name="turn_cotangent",
    )(start, cot, *later)


def turn_back_kernel(start, source, *refs):
    turned, wide_source = refs[-2:]
    back = (TOK_DEV - start[0]) & (TOK_DEV - 1)
    if source.dtype == F32:
        turn_rows(source, back, write_into(turned))
    else:
        wide_source[...] = source[...].astype(F32)
        turn_rows(wide_source, back, write_into(turned))


def turn_back(start, value, later):
    scratch = (8, PAIR) if value.dtype == F32 else value.shape
    return pl.pallas_call(
        turn_back_kernel,
        in_specs=[SMEM, VM] + [ANY] * len(later),
        out_specs=VM,
        out_shape=sds(value.shape, value.dtype),
        scratch_shapes=[pltpu.VMEM(scratch, F32)],
        compiler_params=params(),
        cost_estimate=cost(1, 1),
        name="turn_back",
    )(start, value, *later)


def make_bias(cells_ref, bias):
    for half in range(2):
        mine = slice(half * HALF, (half + 1) * HALF)
        number = lax.broadcasted_iota(jnp.int32, (16, HALF), 0)
        of_key = jnp.where(cells_ref[1:2, mine] == number, 1.0, 0.0).astype(BF)
        of_query = jnp.where(cells_ref[0:1, mine] == number, 1.0, 0.0).astype(BF)
        keys = lax.broadcasted_iota(jnp.int32, (HALF, HALF), 0)
        queries = lax.broadcasted_iota(jnp.int32, (HALF, HALF), 1)
        seen = (dot(of_key, of_query, TN) > 0.5) | (keys == queries)
        bias[mine, :] = jnp.where(seen, 0.0, MASKED)


def column_of(row):
    eye = lax.broadcasted_iota(jnp.int32, (PAIR, PAIR), 0) == lax.broadcasted_iota(
        jnp.int32, (PAIR, PAIR), 1
    )
    return jnp.sum(jnp.where(eye, row, 0.0), 1, keepdims=True)


def both_heads(pair_t):
    zero = jnp.zeros((HEAD_DIM, pair_t.shape[1]), pair_t.dtype)
    return jnp.concatenate(
        [
            jnp.concatenate([pair_t[:HEAD_DIM], zero], 0),
            jnp.concatenate([zero, pair_t[HEAD_DIM:]], 0),
        ],
        1,
    )


def forward_kernel(order, n_pieces, base, *refs):
    place, tokens, tokens_t, cells_ref, vec_in = refs[:5]
    pieces = refs[5 : 5 + n_pieces]
    att_out, lse_out, krow_out, vrow_out, qt_out, kt_out, w_full, vec_full, tokens_out, bias = refs[
        5 + n_pieces :
    ]
    assemble(order, pieces, place, w_full)
    if vec_in.shape[1] == D:
        vec_full[...] = vec_in[...].astype(F32)
    else:
        rows = D // len(order)
        for piece, lead, mask in order:
            at = pl.multiple_of(jnp.bitwise_xor(place[0], mask) * rows, rows)
            vec_full[:, pl.ds(at, rows)] = pick(pieces[piece], lead, slice(rows, rows + 16))[
                :, :rows
            ].astype(F32)
    make_bias(cells_ref, bias)
    x = tokens[...]
    tokens_out[...] = x
    halves = [slice(0, HALF), slice(HALF, TOK_DEV)]
    chains = []
    for local in range(GROUP):
        lane = slice((base + local) * PAIR, (base + local + 1) * PAIR)
        w = w_full[:, local * TRIO : (local + 1) * TRIO]
        b_q = vec_full[0:1, lane]
        b_v = vec_full[1:2, lane]
        trio = dot(w, tokens_t[...], TN)
        rows = dot(x, w[:, PAIR:], NN)
        here = slice(local * PAIR, (local + 1) * PAIR)
        q_t = ((trio[:PAIR] + column_of(b_q)) * (HEAD_DIM**-0.5)).astype(BF)
        v_t = (trio[2 * PAIR :] + column_of(b_v)).astype(BF)
        k_row = rows[:, :PAIR].astype(BF)
        krow_out[local] = k_row
        vrow_out[local] = (rows[:, PAIR:] + b_v).astype(BF)
        qt_out[here, :] = q_t
        kt_out[here, :] = trio[PAIR : 2 * PAIR].astype(BF)
        chains += [(local, mine, q_t, v_t, k_row) for mine in halves]

    def scores(chain):
        local, mine, q_t, v_t, k_row = chain
        return dot(k_row[mine], both_heads(q_t[:, mine]), NN)

    ahead = scores(chains[0])
    for number, (local, mine, q_t, v_t, k_row) in enumerate(chains):
        s = ahead
        if number + 1 < len(chains):
            ahead = scores(chains[number + 1])
        mask = bias[mine, :]
        s = s + jnp.concatenate([mask, mask], 1)
        top = jnp.max(s, 0, keepdims=True)
        e = jnp.exp(s - top)
        total = jnp.sum(e, 0, keepdims=True)
        lse = top + jnp.log(total)
        e_low = e.astype(BF)
        for h in range(2):
            cols = slice(h * HALF, (h + 1) * HALF)
            head = slice(h * HEAD_DIM, (h + 1) * HEAD_DIM)
            o = dot(v_t[head, mine], e_low[:, cols], NN)
            at = local * PAIR + h * HEAD_DIM
            att_out[at : at + HEAD_DIM, mine] = (o / total[:, cols]).astype(BF)
            lse_out[local, h : h + 1, mine] = lse[:, cols]


def forward_attention(base, place, tokens, tokens_t, cells, vec, pieces, order):
    wide_t, tall = sds((GROUP * PAIR, TOK_DEV), BF), sds((GROUP, TOK_DEV, PAIR), BF)
    return pl.pallas_call(
        functools.partial(forward_kernel, order, len(pieces), base),
        in_specs=[SMEM] + [VM] * (4 + len(pieces)),
        out_specs=[VM] * 9,
        out_shape=[
            wide_t, sds((GROUP, 8, TOK_DEV), F32), tall, tall, wide_t, wide_t, sds((D, HW), BF), sds((16, D), F32),
            sds((TOK_DEV, D), BF),
        ],
        scratch_shapes=[pltpu.VMEM((TOK_DEV, HALF), F32)],
        compiler_params=params(FORWARD_MIB),
        cost_estimate=cost(1, 1),
        name="forward_attention",
    )(place, tokens, tokens_t, cells, vec, *pieces)


def normalize(value):
    center = value - jnp.mean(value, -1, keepdims=True)
    inverse = lax.rsqrt(jnp.mean(center * center, -1, keepdims=True) + NORM_EPS)
    return center * inverse, inverse


def normalize_back(grad, normal, inverse):
    return inverse * (
        grad
        - jnp.mean(grad, -1, keepdims=True)
        - normal * jnp.mean(grad * normal, -1, keepdims=True)
    )


def column_sum(value):
    return jnp.sum(value, 0, keepdims=True)


def row_sources(place, n_shards, stages):
    if not stages:
        return [(0, 0, D)]
    rows = D // n_shards
    piece = D >> len(stages)
    found = []
    for block in range(1 << len(stages)):
        masks = {"narrow": 0, "wide": 0}
        for number, (axis, mask) in enumerate(stages):
            if block >> (len(stages) - 1 - number) & 1:
                masks[axis] |= mask
        source = jnp.bitwise_xor(place[0], masks["narrow"]) * rows
        if piece < rows:
            source = source + jnp.bitwise_xor(place[1], masks["wide"]) * piece
        found.append((block * piece, pl.multiple_of(source, piece), piece))
    return found


def store_rows(outs, place, n_shards, stages, matrix, cols):
    height = outs[0].shape[0]
    for target, source, rows in row_sources(place, n_shards, stages):
        out = outs[target // height]
        at = target % height
        out[at : at + rows, cols] = matrix[pl.ds(source, rows), :].astype(BF)


def gelu_parts(value):
    density = jnp.exp(-0.5 * value * value)
    t = 1.0 / (1.0 + (0.3275911 / math.sqrt(2.0)) * jnp.abs(value))
    poly = 1.061405429
    for factor in (-1.453152027, 1.421413741, -0.284496736, 0.254829592):
        poly = poly * t + factor
    tail = 0.5 * poly * t * density
    return jnp.where(value >= 0.0, 1.0 - tail, tail), value * density * (1.0 / math.sqrt(2.0 * math.pi))


def middle_kernel(order, n_pieces, *refs):
    place, tokens, cot_ref, att_a, att_b, vec_ref = refs[:6]
    pieces = refs[6 : 6 + n_pieces]
    mixed_out, dh1_out, datt_out, vec_out = refs[6 + n_pieces : 10 + n_pieces]
    first_all, hidden_all, branch_all, pre_all, down_all = refs[10 + n_pieces : 15 + n_pieces]
    w_full, sums = refs[15 + n_pieces :]
    step = pl.program_id(0)

    @pl.when(step == 0)
    def _():
        assemble(order, pieces, place, w_full)
        sums[...] = jnp.zeros_like(sums)

    w_out, w_up, w_down = w_full[:, :D], w_full[:, D : 2 * D], w_full[:, 2 * D :]

    def vec(row):
        return vec_ref[row : row + 1, :]

    def tile(number):
        at = pl.ds(pl.multiple_of(step * (TILES * MT) + number * MT, MT), MT)
        att_t = jnp.concatenate([att_a[:, at], att_b[:, at]], 0)
        branch = dot(att_t, w_out, TN)
        yield
        normal_1, inverse_1 = normalize(tokens[at, :].astype(F32) + (branch + vec(2)))
        first = normal_1 * vec(5) + vec(6)
        first_low = first.astype(BF)
        first_all[at, :] = first_low
        pre = dot(first_low, w_up, NN)
        yield
        pre = pre + vec(3)
        cdf, bump = gelu_parts(pre)
        hidden = (pre * cdf).astype(BF)
        hidden_all[at, :] = hidden
        slope = cdf + bump
        down = dot(hidden, w_down, NN)
        yield
        normal_2, inverse_2 = normalize(first + (down + vec(4)))
        mixed_out[at, :] = (normal_2 * vec(7) + vec(8)).astype(BF)
        cot = cot_ref[at, :]
        d_h2 = normalize_back(cot * vec(7), normal_2, inverse_2)
        d_down = d_h2.astype(BF)
        down_all[at, :] = d_down
        d_hidden = dot(d_down, w_down, NT)
        yield
        sums[7:8, :] += column_sum(cot * normal_2)
        sums[8:9, :] += column_sum(cot)
        d_pre = (d_hidden * slope).astype(BF)
        pre_all[at, :] = d_pre
        d_up = dot(d_pre, w_up, NT)
        yield
        d_first = d_h2 + d_up
        d_h1 = normalize_back(d_first * vec(5), normal_1, inverse_1)
        dh1_out[at, :] = d_h1
        d_branch = d_h1.astype(BF)
        branch_all[at, :] = d_branch
        datt_out[:, at] = dot(w_out, d_branch, NT).astype(BF)
        yield
        sums[5:6, :] += column_sum(d_first * normal_1)
        sums[6:7, :] += column_sum(d_first)

    tiles = [tile(number) for number in range(TILES)]
    while tiles:
        tiles = [one for one in tiles if next(one, True) is None]

    @pl.when(step == pl.num_programs(0) - 1)
    def _():
        ones = jnp.ones((16, TOK_DEV), BF)
        sums[2:3, :] = dot(ones, branch_all[...], NN)[:1]
        sums[3:4, :] = dot(ones, pre_all[...], NN)[:1]
        sums[4:5, :] = dot(ones, down_all[...], NN)[:1]
        vec_out[...] = sums[...]


def middle(place, tokens, cot, atts, vec, pieces, order):
    height = TILES * MT
    return pl.pallas_call(
        functools.partial(middle_kernel, order, len(pieces)),
        grid=(TOK_DEV // height,),
        in_specs=[SMEM] + [VM] * (5 + len(pieces)),
        out_specs=[VM] * 9,
        out_shape=[
            sds((TOK_DEV, D), BF),
            sds((TOK_DEV, D), F32),
            sds((D, TOK_DEV), BF),
            sds((16, D), F32),
        ]
        + [sds((TOK_DEV, D), BF)] * 5,
        scratch_shapes=[pltpu.VMEM((D, 3 * D), BF), pltpu.VMEM((16, D), F32)],
        compiler_params=params(MIDDLE_MIB),
        cost_estimate=cost(1e10, 1.2e7, 2**20),
        name="middle",
    )(place, tokens, cot, *atts, vec, *pieces)


def backward_kernel(n_shards, stages, plan, n_sets, n_inner, last, place, cells_ref, tokens_t, vec_ref,
                    datt_ref, *refs):
    sets = [refs[6 * number : 6 * (number + 1)] for number in range(n_sets)]
    inner = refs[6 * n_sets : 6 * n_sets + n_inner]
    bias, dw = refs[-2:]
    n_g = 2 if stages else 1
    d_out, vec = refs[-4 - n_g : -2 - n_g]
    g_outs = refs[-2 - n_g : -2]
    make_bias(cells_ref, bias)
    vec[...] = vec_ref[...]
    halves = [slice(0, HALF), slice(HALF, TOK_DEV)]
    chains = [(place_out, *entry, mine) for place_out, entry in enumerate(plan) for mine in halves]

    def scores(chain):
        _, number, local, pair, mine = chain
        att_ref, lse_ref, krow_ref, vrow_ref, qt_ref, kt_ref = sets[number]
        here = slice(local * PAIR, (local + 1) * PAIR)
        q_t, d_t = qt_ref[here, mine], datt_ref[pair * PAIR : (pair + 1) * PAIR, mine]
        s = dot(krow_ref[local, mine, :], both_heads(q_t), NN)
        return q_t, d_t, s, dot(vrow_ref[local, mine, :], both_heads(d_t), NN)

    first = 0
    if inner:
        first = 3 * D
        first_all, hidden_all, branch_all, pre_all, down_all = inner
        attended = jnp.concatenate([sets[0][0][...], sets[1][0][...]], 0)
        products = [
            dot(attended, branch_all[...], NN),
            dot(first_all[...], pre_all[...], TN),
            dot(hidden_all[...], down_all[...], TN),
        ]
        for number, product in enumerate(products):
            dw[number % 2] = product
            cols = slice(number * D, (number + 1) * D)
            store_rows(g_outs, place, n_shards, stages, dw.at[number % 2], cols)
    ahead = scores(chains[0])
    for step, (place_out, number, local, pair, mine) in enumerate(chains):
        q_t, d_t, s, d_prob = ahead
        if step + 1 < len(chains):
            ahead = scores(chains[step + 1])
        att_ref, lse_ref, krow_ref, vrow_ref, qt_ref, kt_ref = sets[number]
        mask = bias[mine, :]
        lse = jnp.concatenate([lse_ref[local, 0:1, mine], lse_ref[local, 1:2, mine]], 1)
        here = slice(local * PAIR, (local + 1) * PAIR)
        product = d_t.astype(F32) * att_ref[here, mine].astype(F32)
        delta = jnp.concatenate([column_sum(product[:HEAD_DIM]), column_sum(product[HEAD_DIM:])], 1)
        prob = jnp.exp(s + jnp.concatenate([mask, mask], 1) - lse)
        d_s = (prob * (d_prob - delta)).astype(BF)
        prob_low = prob.astype(BF)
        for h in range(2):
            cols = slice(h * HALF, (h + 1) * HALF)
            head = slice(h * HEAD_DIM, (h + 1) * HEAD_DIM)
            k_t = kt_ref[local * PAIR + h * HEAD_DIM : local * PAIR + (h + 1) * HEAD_DIM, mine]
            d_q = dot(k_t, d_s[:, cols], NN) * (HEAD_DIM**-0.5)
            d_k = dot(q_t[head], d_s[:, cols], NT)
            d_v = dot(d_t[head], prob_low[:, cols], NT)
            for t, value in enumerate((d_q, d_k, d_v)):
                at = t * PAIR + h * HEAD_DIM
                d_out[place_out, at : at + HEAD_DIM, mine] = value.astype(BF)
        if mine.start == 0:
            continue
        trio = d_out[place_out]
        dw[place_out % 2, :, :TRIO] = dot(tokens_t[...], trio, NT)
        at = first + place_out * TRIO
        store_rows(
            g_outs, place, n_shards, stages, dw.at[place_out % 2, :, :TRIO], slice(at, at + TRIO)
        )
        total = dot(jnp.ones((16, TOK_DEV), BF), trio, NT)
        lanes = slice(pair * PAIR, (pair + 1) * PAIR)
        vec[0:1, lanes] = total[:1, :PAIR]
        vec[1:2, lanes] = total[:1, 2 * PAIR :]
    if stages and last:
        height = g_outs[0].shape[0]
        rows = D // n_shards
        for target, source, count in row_sources(place, n_shards, stages):
            at = pl.multiple_of(source // rows * rows, rows)
            g_outs[target // height][target % height : target % height + count, LATE:] = vec[
                :, pl.ds(at, rows)
            ].astype(BF)


def backward_attention(plan, last, place, cells, tokens_t, vec_sums, sets, d_t, inner, n_shards, stages, later):
    width = len(plan) * TRIO + (3 * D if inner else 0)
    if stages:
        shapes = [sds((D // 2, width + (PAIR if last else 0)), BF)] * 2
    else:
        shapes = [sds((D, width), BF)]
    flat = [value for saved in sets for value in saved]
    return pl.pallas_call(
        functools.partial(backward_kernel, n_shards, stages, plan, len(sets), len(inner), last),
        in_specs=[SMEM] + [VM] * (4 + len(flat) + len(inner)) + [ANY] * len(later),
        out_specs=[VM] * (2 + len(shapes)),
        out_shape=[sds((len(plan), TRIO, TOK_DEV), BF), sds((16, D), F32)] + shapes,
        scratch_shapes=[pltpu.VMEM((TOK_DEV, HALF), F32), pltpu.VMEM((2, D, D), F32)],
        compiler_params=params(BACKWARD_MIB),
        cost_estimate=cost(5e9 * len(plan), 8e6, 2**21),
        name="backward_attention",
    )(place, cells, tokens_t, vec_sums, d_t, *flat, *inner, *later)


def input_grad_kernel(start, w_a, w_b, dh1_ref, trio_a, trio_b, *refs):
    out, turned = refs[-2:]
    trios = [ref.at[number] for ref in (trio_a, trio_b) for number in range(ref.shape[0])]
    for tile in range(TOK_DEV // QT):
        here = slice(tile * QT, (tile + 1) * QT)
        total = None
        for w_ref, parts in ((w_a, trios[:GROUP]), (w_b, trios[GROUP:])):
            term = dot(w_ref[...], jnp.concatenate([part[:, here] for part in parts], 0), NN)
            total = term if total is None else total + term
        turned[here, :] = dh1_ref[here, :] + total.T
    turn_rows(turned, (TOK_DEV - start[0]) & (TOK_DEV - 1), write_into(out))


def input_gradient(start, weights, d_h1, trios, later):
    return pl.pallas_call(
        input_grad_kernel,
        in_specs=[SMEM] + [VM] * 5 + [ANY] * len(later),
        out_specs=VM,
        out_shape=sds((TOK_DEV, D), F32),
        scratch_shapes=[pltpu.VMEM((TOK_DEV, D), F32)],
        compiler_params=params(),
        cost_estimate=cost(1, 1),
        name="input_gradient",
    )(start, *weights, d_h1, *trios, *later)


def adam(weight, grad, first, second, rate, decay):
    first = 0.5 * first + 0.5 * grad
    second = 0.5 * second + 0.5 * grad * grad
    fix = 1.0 - 0.5**STEP
    fixed = second * (1.0 / fix)
    update = first * (1.0 / fix) / (fixed * lax.rsqrt(fixed) + ADAM_EPS)
    return weight - rate * (update + decay * weight), first, second


def pair_parts(first, pairs):
    return [
        (slice(at, at + PAIR), 0, t * D + pair * PAIR)
        for number, pair in enumerate(pairs)
        for t in range(3)
        for at in [first + number * TRIO + t * PAIR]
    ]


EARLY_PARTS = [(slice(i * D, (i + 1) * D), i + 1, 0) for i in range(3)] + pair_parts(3 * D, range(FIRST))
LATE_PARTS = pair_parts(0, range(FIRST, PAIRS))


def adam_kernel(quick, limit, place, square_ref, *refs):
    n_grads = 4 if quick else 2
    grads = refs[:n_grads]
    vec_ref = refs[n_grads]
    states = refs[n_grads + 1 : n_grads + 16]
    outs = refs[n_grads + 16 : n_grads + 36]
    norm_out = refs[-1]
    step = pl.program_id(0)
    norm = jnp.sqrt(square_ref[0:1, 0:1])
    factor = limit / jnp.maximum(norm, limit)

    def write(number, where, target, grad, rate, decay):
        new, first, second = adam(
            states[number][where], grad * factor, states[5 + number][where],
            states[10 + number][where], rate, decay,
        )
        outs[number][target] = new
        outs[5 + number][target] = first
        outs[10 + number][target] = second
        outs[15 + number][target] = new.astype(BF)

    height = outs[0].shape[0]
    pieces = height // 16 if quick else 1
    rows = height // pieces
    for piece in range(pieces):
        here = pl.multiple_of(step * height + piece * rows, rows)
        if quick:
            mask = jnp.bitwise_xor(place[1], step * pieces + piece)
            at = pl.multiple_of(((mask >> 2) & 1) * 16 + ((mask >> 1) & 1) * 32, 16)
            odd = (mask & 1) == 1
        else:
            at = here
        for group, parts in enumerate((EARLY_PARTS, LATE_PARTS)):
            for cols, number, first in parts:
                if quick:
                    low, high = grads[2 * group], grads[2 * group + 1]
                    grad = jnp.where(odd, high[pl.ds(at, rows), cols], low[pl.ds(at, rows), cols])
                else:
                    grad = grads[group][pl.ds(at, rows), cols]
                there = slice(first, first + cols.stop - cols.start)
                write(
                    number, (pl.ds(here, rows), there), (slice(piece * rows, (piece + 1) * rows), there),
                    grad.astype(F32), 0.1, 0.01,
                )

    @pl.when(step == 0)
    def _():
        norm_out[0, 0] = norm[0, 0]
        vec_cols = states[4].shape[1]
        where = (slice(0, 9), slice(0, vec_cols))
        write(4, where, where, vec_ref[0:9, :vec_cols].astype(F32), 0.5, 0.0)


def adam_step(place, squares, limit, grads, vec_grad, weights, firsts, seconds, quick):
    steps = 4

    def spec(value):
        if value.shape[0] == 9:
            return whole(value.shape)
        return pl.BlockSpec((value.shape[0] // steps, value.shape[1]), lambda i: (i, 0))

    state = [spec(w) for w in weights]
    shapes = [sds(w.shape, F32) for w in weights]
    return pl.pallas_call(
        functools.partial(adam_kernel, quick, limit),
        grid=(steps,),
        in_specs=[SMEM] + [VM] * (17 + len(grads)),
        out_specs=state * 4 + [SMEM],
        out_shape=shapes * 3 + [sds(w.shape, BF) for w in weights] + [sds((1, 1), F32)],
        compiler_params=params(),
        name="adam",
    )(place, squares, *grads, vec_grad, *weights, *firsts, *seconds)


def swap(value, axis, mask):
    size = lax.axis_size(axis)
    return lax.ppermute(value, axis, [(i, i ^ mask) for i in range(size)])


def add_low(a, b):
    return (a.astype(F32) + b.astype(F32)).astype(BF)


def after(value, *others):
    return lax.optimization_barrier((value, others))[0]


def fold(keep, arrived):
    rows = keep.shape[0] // 2
    send = add_low(keep[rows:], arrived[rows:])
    return add_low(keep[:rows], arrived[:rows]), send


def squares_kernel(place, early, late, vec, out):
    total = []
    for piece in range(4):
        rows = slice(16 * piece, 16 * (piece + 1))
        first, second = early[rows, :].astype(F32), late[rows, :].astype(F32)
        total.append(jnp.sum(first * first) + jnp.sum(second * second))
    total = (total[0] + total[1]) + (total[2] + total[3])
    total = total + jnp.where((place[1] & 1) == 0, jnp.sum(vec[...] * vec[...]), 0.0)
    out[...] = jnp.full(out.shape, total, F32)


def half_squares(place, early, late, vec):
    return pl.pallas_call(
        squares_kernel,
        in_specs=[SMEM] + [VM] * 3,
        out_specs=VM,
        out_shape=sds((8, PAIR), F32),
        compiler_params=params(),
        cost_estimate=cost(1, 1),
        name="half_squares",
    )(place, early, late, vec)


def directly(value, axis, masks):
    return [swap(value, axis, mask) for mask in masks]


def four(value, others):
    return (value + others[0]) + (others[1] + others[2])


def join(held, arrived):
    return jnp.concatenate([held, arrived], 0)


def squares_of(value):
    value = value.astype(F32)
    return jnp.sum(value * value)


STAGES = (("narrow", 1), ("narrow", 2), ("wide", 1), ("wide", 2), ("wide", 4))


def body(
    tokens, cotangent, cells, present, generate,
    w_qkv, w_out, w_up, w_down, vectors,
    m_qkv, m_out, m_up, m_down, m_vec,
    v_qkv, v_out, v_up, v_down, v_vec,
):
    narrow, wide = lax.axis_size("narrow"), lax.axis_size("wide")
    quick = narrow == 4 and wide == 8
    stages = STAGES if quick else ()
    place = jnp.stack([lax.axis_index("narrow"), lax.axis_index("wide")]).astype(jnp.int32)
    shard = w_qkv.shape[0]

    low_a = pack_first(w_qkv, vectors)
    coded = jnp.where((present == 1) & (generate == 0), cells, cells + HIDDEN)
    tokens, tokens_t, cells, start = turn_tokens(tokens, after(coded, low_a))
    low_b, low_rest = pl.pallas_call(
        pack_second_kernel,
        in_specs=[VM] * 4 + [ANY],
        out_specs=[VM, VM],
        out_shape=[sds((shard, HW), BF), sds((shard, 3 * D), BF)],
        compiler_params=params(),
        name="pack_second",
    )(w_qkv, w_out, w_up, w_down, cells)
    if quick:
        y_a = after(swap(low_a, "narrow", 2), low_b)
        pieces_a = [low_a, swap(low_a, "narrow", 1), y_a, swap(y_a, "narrow", 1)]
        y_b = swap(after(low_b, y_a), "narrow", 2)
        c_b = swap(low_b, "narrow", 1)
        y_rest = swap(after(low_rest, y_a), "narrow", 2)
        c_rest = swap(low_rest, "narrow", 1)
        order = [(j, None, j) for j in range(4)]
        vec = jnp.zeros((8, PAIR), BF)
    else:
        pieces_a, pieces_b = [lax.all_gather(low_a, "narrow")], [lax.all_gather(low_b, "narrow")]
        pieces_rest = [lax.all_gather(low_rest, "narrow")]
        order = [(0, j, None) for j in range(narrow)]
        vec = lax.all_gather(vectors.astype(BF), "narrow", axis=1, tiled=True)
        vec = jnp.pad(vec, ((0, 7), (0, 0)))

    *saved_a, w_a, vec_full, tokens = forward_attention(
        0, place, tokens, tokens_t, cells, vec, pieces_a, order
    )
    if quick:
        y_b, c_b = after(y_b, saved_a), after(c_b, saved_a)
        pieces_b = [low_b, c_b, y_b, swap(y_b, "narrow", 1)]
    *saved_b, w_b, vec_full, tokens = forward_attention(
        GROUP, place, tokens, tokens_t, cells, vec_full, pieces_b, order
    )
    if quick:
        y_rest, c_rest = after(y_rest, saved_b), after(c_rest, saved_b)
        d_rest = swap(y_rest, "narrow", 1)
        cotangent = turn_cotangent(start, cotangent, [y_rest])
        pieces_rest = [low_rest, c_rest, y_rest, after(d_rest, cotangent)]
    else:
        cotangent = turn_cotangent(start, cotangent, [])
    mixed, d_h1, d_t, vec_sums, *inner = middle(
        place, tokens, cotangent, (saved_a[0], saved_b[0]), vec_full, pieces_rest, order
    )
    sets = [saved_a, saved_b]
    plan = [(pair // GROUP, pair % GROUP, pair) for pair in range(PAIRS)]
    trio_a, vec_sums, *early = backward_attention(
        plan[:FIRST], False, place, cells, tokens_t, vec_sums, sets, d_t, inner, narrow, stages, []
    )
    later = []
    if quick:
        e_keep, e_send = early
        mixed = turn_back(start, mixed, [trio_a])
        e_keep, e_send = fold(e_keep, after(swap(e_send, "narrow", 1), mixed))
        e_arrived = swap(e_send, "narrow", 2)
        later = [e_send]
    trio_b, vec_sums, *late = backward_attention(
        plan[FIRST:], True, place, cells, tokens_t, vec_sums, sets, d_t, [], narrow, stages, later
    )
    weights, trios = (w_a, w_b), (trio_a, trio_b)

    if quick:
        b_keep, b_send = late
        b_arrived = swap(b_send, "narrow", 1)
        e_keep, e_send = fold(e_keep, after(e_arrived, trio_b))
        e_arrived = swap(e_send, "wide", 1)
        b_keep, b_send = fold(b_keep, after(b_arrived, e_send))
        b_arrived = swap(b_send, "narrow", 2)
        input_grad = input_gradient(start, weights, d_h1, trios, [b_send, e_send])
        e_keep, e_send = fold(e_keep, after(e_arrived, input_grad))
        e_arrived = swap(e_send, "wide", 2)
        b_keep, b_send = fold(b_keep, after(b_arrived, e_send))
        b_arrived = swap(b_send, "wide", 1)
        e_keep, e_send = fold(e_keep, after(e_arrived, b_send))
        e_arrived = swap(e_send, "wide", 4)
        b_keep, b_send = fold(b_keep, after(b_arrived, e_send))
        b_arrived = swap(b_send, "wide", 2)
        e_low = add_low(e_keep, after(e_arrived, b_send))
        e_arrived = swap(e_low, "wide", 4)
        b_keep, b_send = fold(b_keep, after(b_arrived, e_low))
        b_arrived = swap(b_send, "wide", 4)
        e_low = join(e_low, after(e_arrived, b_send))
        e_arrived = swap(e_low, "wide", 2)
        b_arrived = after(b_arrived, e_low)
        vec_total = b_keep[:, LATE:].astype(F32) + b_arrived[:, LATE:].astype(F32)
        b_low = add_low(b_keep[:, :LATE], b_arrived[:, :LATE])
        b_arrived = swap(b_low, "wide", 4)
        e_low = join(e_low, after(e_arrived, b_low))
        b_low = join(b_low, after(b_arrived, e_low))
        b_low = join(b_low, swap(b_low, "wide", 2))
        e_arrived, b_arrived = swap(e_low, "wide", 1), swap(b_low, "wide", 1)
        squares = half_squares(place, e_low, b_low, vec_total)
        squares = four(squares, directly(squares, "narrow", (1, 2, 3)))
        squares = squares + swap(squares, "wide", 1)
        grads = [e_low, after(e_arrived, squares), b_low, after(b_arrived, squares)]
    else:
        input_grad, mixed = input_gradient(start, weights, d_h1, trios, []), turn_back(start, mixed, [])
        vec_total = lax.psum_scatter(vec_sums, "narrow", scatter_dimension=1, tiled=True)
        vec_total = lax.psum(vec_total, "wide")
        grads = []
        for every in (early[0], late[0]):
            total = lax.psum_scatter(every, "narrow", scatter_dimension=0, tiled=True)
            grads.append(lax.psum(total.astype(F32), "wide"))
        squares = lax.psum(sum(squares_of(v) for v in grads + [vec_total]), "narrow")
        squares = jnp.full((8, PAIR), squares, F32)
    *updated, grad_norm = adam_step(
        place, squares, math.sqrt(TOK_DEV * wide * narrow), grads, vec_total,
        (w_qkv, w_out, w_up, w_down, vectors),
        (m_qkv, m_out, m_up, m_down, m_vec),
        (v_qkv, v_out, v_up, v_down, v_vec),
        quick,
    )
    return (mixed, input_grad, grad_norm[0, 0], *updated)


def solution(mesh):
    split = P(("wide", "narrow"), None)
    state = (P("narrow", None),) * 4 + (P(None, "narrow"),)
    return jax.shard_map(
        body,
        mesh=mesh,
        in_specs=(split,) * 5 + state * 3,
        out_specs=(split, split, P()) + state * 4,
        check_vma=False,
    )
```

```python
import functools
import math

import jax
import jax.numpy as jnp
from jax import lax
from jax.experimental import pallas as pl
from jax.experimental.pallas import tpu as pltpu
from jax.sharding import PartitionSpec as P

D = 512
HEADS = 8
HEAD_DIM = 64
PAIR = 2 * HEAD_DIM
PAIRS = HEADS // 2
TRIO = 3 * PAIR
TOK_DEV = 1024
QT = 256
HALF = TOK_DEV // 2
TILES = 1
MT = 512
STEP = 10
NORM_EPS = 1e-05
ADAM_EPS = 1e-08
MASKED = -1e30
HIDDEN = 16
BF = jnp.bfloat16
F32 = jnp.float32
MIB = 1024 * 1024
GROUP = 2
HW = GROUP * TRIO
FIRST = 1
LATE = (PAIRS - FIRST) * TRIO
FORWARD_MIB, MIDDLE_MIB, BACKWARD_MIB = 12, 18, 20

NN = (((1,), (0,)), ((), ()))
NT = (((1,), (1,)), ((), ()))
TN = (((0,), (0,)), ((), ()))


def dot(a, b, dims):
    return lax.dot_general(a, b, dims, preferred_element_type=F32)


def params(mib=8):
    return pltpu.CompilerParams(vmem_limit_bytes=mib * MIB)


def sds(shape, dtype):
    return jax.ShapeDtypeStruct(shape, dtype)


SMEM = pl.BlockSpec(memory_space=pltpu.SMEM)
VM = pl.BlockSpec(memory_space=pltpu.VMEM)
ANY = pl.BlockSpec(memory_space=pl.ANY)
HBM = pl.BlockSpec(memory_space=pltpu.HBM)


def whole(shape):
    return pl.BlockSpec(shape, lambda i: (0,) * len(shape))


def cost(flops, moved, exps=0):
    return pl.CostEstimate(flops=int(flops), bytes_accessed=int(moved), transcendentals=int(exps))


def fetch(pairs, sems):
    copies = [
        pltpu.make_async_copy(source, target, sems.at[number])
        for number, (source, target) in enumerate(pairs)
    ]
    for copy in copies:
        copy.start()
    return copies


def trio_columns(base):
    return [
        (local * TRIO + t * PAIR, t * D + (base + local) * PAIR)
        for local in range(GROUP)
        for t in range(3)
    ]


def pack_first_kernel(w_hbm, vec_hbm, out_ref, w_ref, vec_ref, sems):
    rows, vec_cols = w_hbm.shape[0], vec_hbm.shape[1]
    width = GROUP * PAIR
    copies = fetch(
        [(w_hbm.at[:, t * D : t * D + width], w_ref.at[t]) for t in range(3)] + [(vec_hbm, vec_ref)], sems
    )
    for copy in copies:
        copy.wait()
    for local in range(GROUP):
        for t in range(3):
            target = local * TRIO + t * PAIR
            out_ref[:rows, target : target + PAIR] = w_ref[t, :, local * PAIR : (local + 1) * PAIR].astype(BF)
    out_ref[rows:, :] = jnp.zeros((16, HW), BF)
    vec = jnp.concatenate([vec_ref[...], jnp.zeros((7, vec_cols), F32)], 0)
    out_ref[rows:, :vec_cols] = vec.astype(BF)


def pack_first(w_qkv, vectors):
    rows = w_qkv.shape[0]
    return pl.pallas_call(
        pack_first_kernel,
        in_specs=[HBM, HBM],
        out_specs=VM,
        out_shape=sds((rows + 16, HW), BF),
        scratch_shapes=[
            pltpu.VMEM((3, rows, GROUP * PAIR), F32),
            pltpu.VMEM(vectors.shape, F32),
            pltpu.SemaphoreType.DMA((4,)),
        ],
        compiler_params=params(60),
        name="pack_first",
    )(w_qkv, vectors)


def pack_second_kernel(w_ref, w_out_ref, w_up_ref, w_down_ref, *refs):
    second_ref, rest_ref = refs[-2:]
    for target, source in trio_columns(GROUP):
        second_ref[:, target : target + PAIR] = w_ref[:, source : source + PAIR].astype(BF)
    rest_ref[:, :D] = w_out_ref[...].astype(BF)
    rest_ref[:, D : 2 * D] = w_up_ref[...].astype(BF)
    rest_ref[:, 2 * D :] = w_down_ref[...].astype(BF)


def pick(piece, lead, rows):
    return piece[rows, :] if lead is None else piece[lead, rows, :]


def assemble(order, pieces, place, w_full):
    rows = D // len(order)
    for number, (piece, lead, mask) in enumerate(order):
        at = number if mask is None else jnp.bitwise_xor(place[0], mask)
        w_full[pl.ds(pl.multiple_of(at * rows, rows), rows), :] = pick(
            pieces[piece], lead, slice(0, rows)
        )


def turn_rows(source, start, write):
    blocks = source.shape[0] // 8
    whole_blocks, rest = start >> 3, start & 7
    inside = lax.broadcasted_iota(jnp.int32, (8, source.shape[1]), 0) < 8 - rest

    def rolled(block):
        at = pl.multiple_of(((block + whole_blocks) & (blocks - 1)) * 8, 8)
        return pltpu.roll(source[pl.ds(at, 8), :], (8 - rest) & 7, 0)

    def step(i, first):
        second, third = rolled(2 * i + 1), rolled(2 * i + 2)
        write(i, jnp.where(inside, first, second), jnp.where(inside, second, third))
        return third

    lax.fori_loop(0, blocks // 2, step, rolled(0), unroll=8)


def write_into(out):
    def write(i, upper, lower):
        at = pl.multiple_of(i * 16, 16)
        out[pl.ds(at, 16), :] = jnp.concatenate([upper, lower], 0).astype(out.dtype)

    return write


def turn_tokens_kernel(tokens, coded, *refs):
    tokens_out, turned_out, cells_out, start_out, wide_tokens = refs[-5:]
    seen = coded[...] < HIDDEN
    cell = jnp.where(seen, coded[...], coded[...] - HIDDEN)
    start = jnp.int32(TOK_DEV)
    for c in range(4):
        size = jnp.sum((cell == c).astype(jnp.int32))
        first = jnp.sum((cell < c).astype(jnp.int32))
        start = jnp.where(size == HALF, jnp.minimum(start, first), start)
    start_out[0] = start
    shift = jnp.where(start == 0, 0, TOK_DEV - start)
    row = lax.broadcasted_iota(jnp.int32, (8, TOK_DEV), 0)
    cells_out[...] = pltpu.roll(jnp.where((row == 0) | seen, cell, -1), shift, 1)
    wide_tokens[...] = tokens[...].astype(F32)
    turn_rows(wide_tokens, start, write_into(tokens_out))
    turned_out[...] = tokens_out[...].T


def turn_tokens(tokens, coded):
    return pl.pallas_call(
        turn_tokens_kernel,
        in_specs=[VM, VM],
        out_specs=[VM] * 3 + [SMEM],
        out_shape=[
            sds((TOK_DEV, D), BF),
            sds((D, TOK_DEV), BF),
            sds((8, TOK_DEV), jnp.int32),
            sds((1,), jnp.int32),
        ],
        scratch_shapes=[pltpu.VMEM((TOK_DEV, D), F32)],
        compiler_params=params(),
        cost_estimate=cost(1e7, 3e6),
        name="turn_tokens",
    )(tokens, coded)


def turn_cotangent_kernel(start, cot_ref, *refs):
    turn_rows(cot_ref, start[0], write_into(refs[-1]))


def turn_cotangent(start, cot, later):
    return pl.pallas_call(
        turn_cotangent_kernel,
        in_specs=[SMEM, VM] + [ANY] * len(later),
        out_specs=VM,
        out_shape=sds((TOK_DEV, D), F32),
        compiler_params=params(),
        cost_estimate=cost(1e7, 4e6),
        name="turn_cotangent",
    )(start, cot, *later)


def turn_back_kernel(start, source, *refs):
    turned, wide_source = refs[-2:]
    back = (TOK_DEV - start[0]) & (TOK_DEV - 1)
    if source.dtype == F32:
        turn_rows(source, back, write_into(turned))
    else:
        wide_source[...] = source[...].astype(F32)
        turn_rows(wide_source, back, write_into(turned))


def turn_back(start, value, later):
    scratch = (8, PAIR) if value.dtype == F32 else value.shape
    return pl.pallas_call(
        turn_back_kernel,
        in_specs=[SMEM, VM] + [ANY] * len(later),
        out_specs=VM,
        out_shape=sds(value.shape, value.dtype),
        scratch_shapes=[pltpu.VMEM(scratch, F32)],
        compiler_params=params(),
        cost_estimate=cost(1, 1),
        name="turn_back",
    )(start, value, *later)


def make_bias(cells_ref, bias):
    for half in range(2):
        mine = slice(half * HALF, (half + 1) * HALF)
        number = lax.broadcasted_iota(jnp.int32, (16, HALF), 0)
        of_key = jnp.where(cells_ref[1:2, mine] == number, 1.0, 0.0).astype(BF)
        of_query = jnp.where(cells_ref[0:1, mine] == number, 1.0, 0.0).astype(BF)
        keys = lax.broadcasted_iota(jnp.int32, (HALF, HALF), 0)
        queries = lax.broadcasted_iota(jnp.int32, (HALF, HALF), 1)
        seen = (dot(of_key, of_query, TN) > 0.5) | (keys == queries)
        bias[mine, :] = jnp.where(seen, 0.0, MASKED).astype(BF)


def column_of(row):
    eye = lax.broadcasted_iota(jnp.int32, (PAIR, PAIR), 0) == lax.broadcasted_iota(
        jnp.int32, (PAIR, PAIR), 1
    )
    return jnp.sum(jnp.where(eye, row, 0.0), 1, keepdims=True)


def both_heads(pair_t):
    zero = jnp.zeros((HEAD_DIM, pair_t.shape[1]), pair_t.dtype)
    return jnp.concatenate(
        [
            jnp.concatenate([pair_t[:HEAD_DIM], zero], 0),
            jnp.concatenate([zero, pair_t[HEAD_DIM:]], 0),
        ],
        1,
    )


def forward_kernel(order, n_pieces, base, *refs):
    place, tokens, tokens_t, bias, vec_in = refs[:5]
    pieces = refs[5 : 5 + n_pieces]
    att_out, lse_out, krow_out, vrow_out, qt_out, kt_out, w_full, vec_full, tokens_out = refs[
        5 + n_pieces : 14 + n_pieces
    ]
    if base == 0:
        make_bias(bias, refs[-1])
        bias = refs[-1]
    assemble(order, pieces, place, w_full)
    if vec_in.shape[1] == D:
        vec_full[...] = vec_in[...].astype(F32)
    else:
        rows = D // len(order)
        for piece, lead, mask in order:
            at = pl.multiple_of(jnp.bitwise_xor(place[0], mask) * rows, rows)
            vec_full[:, pl.ds(at, rows)] = pick(pieces[piece], lead, slice(rows, rows + 16))[
                :, :rows
            ].astype(F32)
    x = tokens[...]
    tokens_out[...] = x
    halves = [slice(0, HALF), slice(HALF, TOK_DEV)]
    chains = []
    for local in range(GROUP):
        lane = slice((base + local) * PAIR, (base + local + 1) * PAIR)
        w = w_full[:, local * TRIO : (local + 1) * TRIO]
        b_q = vec_full[0:1, lane]
        b_v = vec_full[1:2, lane]
        trio = dot(w, tokens_t[...], TN)
        rows = dot(x, w[:, PAIR:], NN)
        here = slice(local * PAIR, (local + 1) * PAIR)
        q_t = ((trio[:PAIR] + column_of(b_q)) * (HEAD_DIM**-0.5)).astype(BF)
        v_t = (trio[2 * PAIR :] + column_of(b_v)).astype(BF)
        k_row = rows[:, :PAIR].astype(BF)
        krow_out[local] = k_row
        vrow_out[local] = (rows[:, PAIR:] + b_v).astype(BF)
        qt_out[here, :] = q_t
        kt_out[here, :] = trio[PAIR : 2 * PAIR].astype(BF)
        chains += [(local, mine, q_t, v_t, k_row) for mine in halves]

    def scores(chain):
        local, mine, q_t, v_t, k_row = chain
        return dot(k_row[mine], both_heads(q_t[:, mine]), NN)

    ahead = scores(chains[0])
    for number, (local, mine, q_t, v_t, k_row) in enumerate(chains):
        s = ahead
        if number + 1 < len(chains):
            ahead = scores(chains[number + 1])
        mask = bias[mine, :].astype(F32)
        s = s + jnp.concatenate([mask, mask], 1)
        top = jnp.max(s, 0, keepdims=True)
        e = jnp.exp(s - top)
        total = jnp.sum(e, 0, keepdims=True)
        lse = top + jnp.log(total)
        e_low = e.astype(BF)
        for h in range(2):
            cols = slice(h * HALF, (h + 1) * HALF)
            head = slice(h * HEAD_DIM, (h + 1) * HEAD_DIM)
            o = dot(v_t[head, mine], e_low[:, cols], NN)
            at = local * PAIR + h * HEAD_DIM
            att_out[at : at + HEAD_DIM, mine] = (o / total[:, cols]).astype(BF)
            lse_out[local, h : h + 1, mine] = lse[:, cols]


def forward_attention(base, place, tokens, tokens_t, cells, vec, pieces, order):
    mask = [] if base else [sds((TOK_DEV, HALF), BF)]
    wide_t, tall = sds((GROUP * PAIR, TOK_DEV), BF), sds((GROUP, TOK_DEV, PAIR), BF)
    return pl.pallas_call(
        functools.partial(forward_kernel, order, len(pieces), base),
        in_specs=[SMEM] + [VM] * (4 + len(pieces)),
        out_specs=[VM] * (9 + len(mask)),
        out_shape=[
            wide_t, sds((GROUP, 8, TOK_DEV), F32), tall, tall, wide_t, wide_t, sds((D, HW), BF), sds((16, D), F32),
            sds((TOK_DEV, D), BF),
        ]
        + mask,
        compiler_params=params(FORWARD_MIB),
        cost_estimate=cost(1, 1),
        name="forward_attention",
    )(place, tokens, tokens_t, cells, vec, *pieces)


def normalize(value):
    center = value - jnp.mean(value, -1, keepdims=True)
    inverse = lax.rsqrt(jnp.mean(center * center, -1, keepdims=True) + NORM_EPS)
    return center * inverse, inverse


def normalize_back(grad, normal, inverse):
    return inverse * (
        grad
        - jnp.mean(grad, -1, keepdims=True)
        - normal * jnp.mean(grad * normal, -1, keepdims=True)
    )


def column_sum(value):
    return jnp.sum(value, 0, keepdims=True)


def row_sources(place, n_shards, stages):
    if not stages:
        return [(0, 0, D)]
    rows = D // n_shards
    piece = D >> len(stages)
    found = []
    for block in range(1 << len(stages)):
        masks = {"narrow": 0, "wide": 0}
        for number, (axis, mask) in enumerate(stages):
            if block >> (len(stages) - 1 - number) & 1:
                masks[axis] |= mask
        source = jnp.bitwise_xor(place[0], masks["narrow"]) * rows
        if piece < rows:
            source = source + jnp.bitwise_xor(place[1], masks["wide"]) * piece
        found.append((block * piece, pl.multiple_of(source, piece), piece))
    return found


def store_rows(outs, place, n_shards, stages, matrix, cols):
    height = outs[0].shape[0]
    for target, source, rows in row_sources(place, n_shards, stages):
        out = outs[target // height]
        at = target % height
        out[at : at + rows, cols] = matrix[pl.ds(source, rows), :].astype(BF)


def gelu_parts(value):
    density = jnp.exp(-0.5 * value * value)
    t = 1.0 / (1.0 + (0.3275911 / math.sqrt(2.0)) * jnp.abs(value))
    poly = 1.061405429
    for factor in (-1.453152027, 1.421413741, -0.284496736, 0.254829592):
        poly = poly * t + factor
    tail = 0.5 * poly * t * density
    return jnp.where(value >= 0.0, 1.0 - tail, tail), value * density * (1.0 / math.sqrt(2.0 * math.pi))


def middle_kernel(order, n_pieces, *refs):
    place, tokens, cot_ref, att_a, att_b, vec_ref = refs[:6]
    pieces = refs[6 : 6 + n_pieces]
    mixed_out, dh1_out, datt_out, vec_out = refs[6 + n_pieces : 10 + n_pieces]
    first_all, hidden_all, branch_all, pre_all, down_all = refs[10 + n_pieces : 15 + n_pieces]
    w_full, sums = refs[15 + n_pieces :]
    step = pl.program_id(0)

    @pl.when(step == 0)
    def _():
        assemble(order, pieces, place, w_full)
        sums[...] = jnp.zeros_like(sums)

    w_out, w_up, w_down = w_full[:, :D], w_full[:, D : 2 * D], w_full[:, 2 * D :]

    def vec(row):
        return vec_ref[row : row + 1, :]

    def tile(number):
        at = pl.ds(pl.multiple_of(step * (TILES * MT) + number * MT, MT), MT)
        att_t = jnp.concatenate([att_a[:, at], att_b[:, at]], 0)
        branch = dot(att_t, w_out, TN)
        yield
        normal_1, inverse_1 = normalize(tokens[at, :].astype(F32) + (branch + vec(2)))
        first = normal_1 * vec(5) + vec(6)
        first_low = first.astype(BF)
        first_all[at, :] = first_low
        pre = dot(first_low, w_up, NN)
        yield
        pre = pre + vec(3)
        cdf, bump = gelu_parts(pre)
        hidden = (pre * cdf).astype(BF)
        hidden_all[at, :] = hidden
        slope = cdf + bump
        down = dot(hidden, w_down, NN)
        yield
        normal_2, inverse_2 = normalize(first + (down + vec(4)))
        mixed_out[at, :] = (normal_2 * vec(7) + vec(8)).astype(BF)
        cot = cot_ref[at, :]
        d_h2 = normalize_back(cot * vec(7), normal_2, inverse_2)
        d_down = d_h2.astype(BF)
        down_all[at, :] = d_down
        d_hidden = dot(d_down, w_down, NT)
        yield
        sums[7:8, :] += column_sum(cot * normal_2)
        sums[8:9, :] += column_sum(cot)
        d_pre = (d_hidden * slope).astype(BF)
        pre_all[at, :] = d_pre
        d_up = dot(d_pre, w_up, NT)
        yield
        d_first = d_h2 + d_up
        d_h1 = normalize_back(d_first * vec(5), normal_1, inverse_1)
        dh1_out[at, :] = d_h1
        d_branch = d_h1.astype(BF)
        branch_all[at, :] = d_branch
        datt_out[:, at] = dot(w_out, d_branch, NT).astype(BF)
        yield
        sums[5:6, :] += column_sum(d_first * normal_1)
        sums[6:7, :] += column_sum(d_first)

    tiles = [tile(number) for number in range(TILES)]
    while tiles:
        tiles = [one for one in tiles if next(one, True) is None]

    @pl.when(step == pl.num_programs(0) - 1)
    def _():
        ones = jnp.ones((16, TOK_DEV), BF)
        sums[2:3, :] = dot(ones, branch_all[...], NN)[:1]
        sums[3:4, :] = dot(ones, pre_all[...], NN)[:1]
        sums[4:5, :] = dot(ones, down_all[...], NN)[:1]
        vec_out[...] = sums[...]


def middle(place, tokens, cot, atts, vec, pieces, order):
    height = TILES * MT
    return pl.pallas_call(
        functools.partial(middle_kernel, order, len(pieces)),
        grid=(TOK_DEV // height,),
        in_specs=[SMEM] + [VM] * (5 + len(pieces)),
        out_specs=[VM] * 9,
        out_shape=[
            sds((TOK_DEV, D), BF),
            sds((TOK_DEV, D), F32),
            sds((D, TOK_DEV), BF),
            sds((16, D), F32),
        ]
        + [sds((TOK_DEV, D), BF)] * 5,
        scratch_shapes=[pltpu.VMEM((D, 3 * D), BF), pltpu.VMEM((16, D), F32)],
        compiler_params=params(MIDDLE_MIB),
        cost_estimate=cost(1e10, 1.2e7, 2**20),
        name="middle",
    )(place, tokens, cot, *atts, vec, *pieces)


def backward_kernel(n_shards, stages, plan, n_sets, n_inner, last, place, bias, tokens_t, vec_ref,
                    datt_ref, *refs):
    sets = [refs[6 * number : 6 * (number + 1)] for number in range(n_sets)]
    inner = refs[6 * n_sets : 6 * n_sets + n_inner]
    dw = refs[-1]
    n_g = 2 if stages else 1
    d_out, vec = refs[-3 - n_g : -1 - n_g]
    g_outs = refs[-1 - n_g : -1]
    vec[...] = vec_ref[...]
    halves = [slice(0, HALF), slice(HALF, TOK_DEV)]
    chains = [(place_out, *entry, mine) for place_out, entry in enumerate(plan) for mine in halves]

    def scores(chain):
        _, number, local, pair, mine = chain
        att_ref, lse_ref, krow_ref, vrow_ref, qt_ref, kt_ref = sets[number]
        here = slice(local * PAIR, (local + 1) * PAIR)
        q_t, d_t = qt_ref[here, mine], datt_ref[pair * PAIR : (pair + 1) * PAIR, mine]
        s = dot(krow_ref[local, mine, :], both_heads(q_t), NN)
        return q_t, d_t, s, dot(vrow_ref[local, mine, :], both_heads(d_t), NN)

    first = 0
    if inner:
        first = 3 * D
        first_all, hidden_all, branch_all, pre_all, down_all = inner
        attended = jnp.concatenate([sets[0][0][...], sets[1][0][...]], 0)
        products = [
            dot(attended, branch_all[...], NN),
            dot(first_all[...], pre_all[...], TN),
            dot(hidden_all[...], down_all[...], TN),
        ]
        for number, product in enumerate(products):
            dw[number % 2] = product
            cols = slice(number * D, (number + 1) * D)
            store_rows(g_outs, place, n_shards, stages, dw.at[number % 2], cols)
    ahead = scores(chains[0])
    for step, (place_out, number, local, pair, mine) in enumerate(chains):
        q_t, d_t, s, d_prob = ahead
        if step + 1 < len(chains):
            ahead = scores(chains[step + 1])
        att_ref, lse_ref, krow_ref, vrow_ref, qt_ref, kt_ref = sets[number]
        mask = bias[mine, :].astype(F32)
        lse = jnp.concatenate([lse_ref[local, 0:1, mine], lse_ref[local, 1:2, mine]], 1)
        here = slice(local * PAIR, (local + 1) * PAIR)
        product = d_t.astype(F32) * att_ref[here, mine].astype(F32)
        delta = jnp.concatenate([column_sum(product[:HEAD_DIM]), column_sum(product[HEAD_DIM:])], 1)
        prob = jnp.exp(s + jnp.concatenate([mask, mask], 1) - lse)
        d_s = (prob * (d_prob - delta)).astype(BF)
        prob_low = prob.astype(BF)
        for h in range(2):
            cols = slice(h * HALF, (h + 1) * HALF)
            head = slice(h * HEAD_DIM, (h + 1) * HEAD_DIM)
            k_t = kt_ref[local * PAIR + h * HEAD_DIM : local * PAIR + (h + 1) * HEAD_DIM, mine]
            d_q = dot(k_t, d_s[:, cols], NN) * (HEAD_DIM**-0.5)
            d_k = dot(q_t[head], d_s[:, cols], NT)
            d_v = dot(d_t[head], prob_low[:, cols], NT)
            for t, value in enumerate((d_q, d_k, d_v)):
                at = t * PAIR + h * HEAD_DIM
                d_out[place_out, at : at + HEAD_DIM, mine] = value.astype(BF)
        if mine.start == 0:
            continue
        trio = d_out[place_out]
        dw[place_out % 2, :, :TRIO] = dot(tokens_t[...], trio, NT)
        at = first + place_out * TRIO
        store_rows(
            g_outs, place, n_shards, stages, dw.at[place_out % 2, :, :TRIO], slice(at, at + TRIO)
        )
        total = dot(jnp.ones((16, TOK_DEV), BF), trio, NT)
        lanes = slice(pair * PAIR, (pair + 1) * PAIR)
        vec[0:1, lanes] = total[:1, :PAIR]
        vec[1:2, lanes] = total[:1, 2 * PAIR :]
    if stages and last:
        height = g_outs[0].shape[0]
        rows = D // n_shards
        for target, source, count in row_sources(place, n_shards, stages):
            at = pl.multiple_of(source // rows * rows, rows)
            g_outs[target // height][target % height : target % height + count, LATE:] = vec[
                :, pl.ds(at, rows)
            ].astype(BF)


def backward_attention(plan, last, place, mask, tokens_t, vec_sums, sets, d_t, inner, n_shards, stages, later):
    width = len(plan) * TRIO + (3 * D if inner else 0)
    if stages:
        shapes = [sds((D // 2, width + (PAIR if last else 0)), BF)] * 2
    else:
        shapes = [sds((D, width), BF)]
    flat = [value for saved in sets for value in saved]
    return pl.pallas_call(
        functools.partial(backward_kernel, n_shards, stages, plan, len(sets), len(inner), last),
        in_specs=[SMEM] + [VM] * (4 + len(flat) + len(inner)) + [ANY] * len(later),
        out_specs=[VM] * (2 + len(shapes)),
        out_shape=[sds((len(plan), TRIO, TOK_DEV), BF), sds((16, D), F32)] + shapes,
        scratch_shapes=[pltpu.VMEM((2, D, D), F32)],
        compiler_params=params(BACKWARD_MIB),
        cost_estimate=cost(5e9 * len(plan), 8e6, 2**21),
        name="backward_attention",
    )(place, mask, tokens_t, vec_sums, d_t, *flat, *inner, *later)


def input_grad_kernel(start, w_a, w_b, dh1_ref, trio_a, trio_b, *refs):
    out, turned = refs[-2:]
    trios = [ref.at[number] for ref in (trio_a, trio_b) for number in range(ref.shape[0])]
    for tile in range(TOK_DEV // QT):
        here = slice(tile * QT, (tile + 1) * QT)
        total = None
        for w_ref, parts in ((w_a, trios[:GROUP]), (w_b, trios[GROUP:])):
            term = dot(w_ref[...], jnp.concatenate([part[:, here] for part in parts], 0), NN)
            total = term if total is None else total + term
        turned[here, :] = dh1_ref[here, :] + total.T
    turn_rows(turned, (TOK_DEV - start[0]) & (TOK_DEV - 1), write_into(out))


def input_gradient(start, weights, d_h1, trios, later):
    return pl.pallas_call(
        input_grad_kernel,
        in_specs=[SMEM] + [VM] * 5 + [ANY] * len(later),
        out_specs=VM,
        out_shape=sds((TOK_DEV, D), F32),
        scratch_shapes=[pltpu.VMEM((TOK_DEV, D), F32)],
        compiler_params=params(),
        cost_estimate=cost(1, 1),
        name="input_gradient",
    )(start, *weights, d_h1, *trios, *later)


def adam(weight, grad, first, second, rate, decay):
    first = 0.5 * first + 0.5 * grad
    second = 0.5 * second + 0.5 * grad * grad
    fix = 1.0 - 0.5**STEP
    fixed = second * (1.0 / fix)
    update = first * (1.0 / fix) / (fixed * lax.rsqrt(fixed) + ADAM_EPS)
    return weight - rate * (update + decay * weight), first, second


def pair_parts(first, pairs):
    return [
        (slice(at, at + PAIR), 0, t * D + pair * PAIR)
        for number, pair in enumerate(pairs)
        for t in range(3)
        for at in [first + number * TRIO + t * PAIR]
    ]


EARLY_PARTS = [(slice(i * D, (i + 1) * D), i + 1, 0) for i in range(3)] + pair_parts(3 * D, range(FIRST))
LATE_PARTS = pair_parts(0, range(FIRST, PAIRS))


def adam_kernel(quick, limit, place, square_ref, *refs):
    n_grads = 4 if quick else 2
    grads = refs[:n_grads]
    vec_ref = refs[n_grads]
    states = refs[n_grads + 1 : n_grads + 16]
    outs = refs[n_grads + 16 : n_grads + 36]
    norm_out = refs[-1]
    step = pl.program_id(0)
    norm = jnp.sqrt(square_ref[0:1, 0:1])
    factor = limit / jnp.maximum(norm, limit)

    def write(number, where, target, grad, rate, decay):
        new, first, second = adam(
            states[number][where], grad * factor, states[5 + number][where],
            states[10 + number][where], rate, decay,
        )
        outs[number][target] = new
        outs[5 + number][target] = first
        outs[10 + number][target] = second
        outs[15 + number][target] = new.astype(BF)

    height = outs[0].shape[0]
    pieces = height // 16 if quick else 1
    rows = height // pieces
    for piece in range(pieces):
        here = pl.multiple_of(step * height + piece * rows, rows)
        if quick:
            mask = jnp.bitwise_xor(place[1], step * pieces + piece)
            at = pl.multiple_of(((mask >> 2) & 1) * 16 + ((mask >> 1) & 1) * 32, 16)
            odd = (mask & 1) == 1
        else:
            at = here
        for group, parts in enumerate((EARLY_PARTS, LATE_PARTS)):
            for cols, number, first in parts:
                if quick:
                    low, high = grads[2 * group], grads[2 * group + 1]
                    grad = jnp.where(odd, high[pl.ds(at, rows), cols], low[pl.ds(at, rows), cols])
                else:
                    grad = grads[group][pl.ds(at, rows), cols]
                there = slice(first, first + cols.stop - cols.start)
                write(
                    number, (pl.ds(here, rows), there), (slice(piece * rows, (piece + 1) * rows), there),
                    grad.astype(F32), 0.1, 0.01,
                )

    @pl.when(step == 0)
    def _():
        norm_out[0, 0] = norm[0, 0]
        vec_cols = states[4].shape[1]
        where = (slice(0, 9), slice(0, vec_cols))
        write(4, where, where, vec_ref[0:9, :vec_cols].astype(F32), 0.5, 0.0)


def adam_step(place, squares, limit, grads, vec_grad, weights, firsts, seconds, quick):
    steps = 4

    def spec(value):
        if value.shape[0] == 9:
            return whole(value.shape)
        return pl.BlockSpec((value.shape[0] // steps, value.shape[1]), lambda i: (i, 0))

    state = [spec(w) for w in weights]
    shapes = [sds(w.shape, F32) for w in weights]
    return pl.pallas_call(
        functools.partial(adam_kernel, quick, limit),
        grid=(steps,),
        in_specs=[SMEM] + [VM] * (17 + len(grads)),
        out_specs=state * 4 + [SMEM],
        out_shape=shapes * 3 + [sds(w.shape, BF) for w in weights] + [sds((1, 1), F32)],
        compiler_params=params(),
        name="adam",
    )(place, squares, *grads, vec_grad, *weights, *firsts, *seconds)


def swap(value, axis, mask):
    size = lax.axis_size(axis)
    return lax.ppermute(value, axis, [(i, i ^ mask) for i in range(size)])


def add_low(a, b):
    return (a.astype(F32) + b.astype(F32)).astype(BF)


def after(value, *others):
    return lax.optimization_barrier((value, others))[0]


def fold(keep, arrived):
    rows = keep.shape[0] // 2
    send = add_low(keep[rows:], arrived[rows:])
    return add_low(keep[:rows], arrived[:rows]), send


def squares_kernel(place, early, late, vec, out):
    total = []
    for piece in range(4):
        rows = slice(16 * piece, 16 * (piece + 1))
        first, second = early[rows, :].astype(F32), late[rows, :].astype(F32)
        total.append(jnp.sum(first * first) + jnp.sum(second * second))
    total = (total[0] + total[1]) + (total[2] + total[3])
    total = total + jnp.where((place[1] & 1) == 0, jnp.sum(vec[...] * vec[...]), 0.0)
    out[...] = jnp.full(out.shape, total, F32)


def half_squares(place, early, late, vec):
    return pl.pallas_call(
        squares_kernel,
        in_specs=[SMEM] + [VM] * 3,
        out_specs=VM,
        out_shape=sds((8, PAIR), F32),
        compiler_params=params(),
        cost_estimate=cost(1, 1),
        name="half_squares",
    )(place, early, late, vec)


def directly(value, axis, masks):
    return [swap(value, axis, mask) for mask in masks]


def four(value, others):
    return (value + others[0]) + (others[1] + others[2])


def join(held, arrived):
    return jnp.concatenate([held, arrived], 0)


def squares_of(value):
    value = value.astype(F32)
    return jnp.sum(value * value)


STAGES = (("narrow", 1), ("narrow", 2), ("wide", 1), ("wide", 2), ("wide", 4))


def body(
    tokens, cotangent, cells, present, generate,
    w_qkv, w_out, w_up, w_down, vectors,
    m_qkv, m_out, m_up, m_down, m_vec,
    v_qkv, v_out, v_up, v_down, v_vec,
):
    narrow, wide = lax.axis_size("narrow"), lax.axis_size("wide")
    quick = narrow == 4 and wide == 8
    stages = STAGES if quick else ()
    place = jnp.stack([lax.axis_index("narrow"), lax.axis_index("wide")]).astype(jnp.int32)
    shard = w_qkv.shape[0]

    low_a = pack_first(w_qkv, vectors)
    coded = jnp.where((present == 1) & (generate == 0), cells, cells + HIDDEN)
    tokens, tokens_t, cells, start = turn_tokens(tokens, after(coded, low_a))
    low_b, low_rest = pl.pallas_call(
        pack_second_kernel,
        in_specs=[VM] * 4 + [ANY],
        out_specs=[VM, VM],
        out_shape=[sds((shard, HW), BF), sds((shard, 3 * D), BF)],
        compiler_params=params(),
        name="pack_second",
    )(w_qkv, w_out, w_up, w_down, cells)
    if quick:
        y_a = after(swap(low_a, "narrow", 2), low_b)
        pieces_a = [low_a, swap(low_a, "narrow", 1), y_a, swap(y_a, "narrow", 1)]
        y_b = swap(after(low_b, y_a), "narrow", 2)
        c_b = swap(low_b, "narrow", 1)
        y_rest = swap(after(low_rest, y_a), "narrow", 2)
        c_rest = swap(low_rest, "narrow", 1)
        order = [(j, None, j) for j in range(4)]
        vec = jnp.zeros((8, PAIR), BF)
    else:
        pieces_a, pieces_b = [lax.all_gather(low_a, "narrow")], [lax.all_gather(low_b, "narrow")]
        pieces_rest = [lax.all_gather(low_rest, "narrow")]
        order = [(0, j, None) for j in range(narrow)]
        vec = lax.all_gather(vectors.astype(BF), "narrow", axis=1, tiled=True)
        vec = jnp.pad(vec, ((0, 7), (0, 0)))

    *saved_a, w_a, vec_full, tokens, mask = forward_attention(
        0, place, tokens, tokens_t, cells, vec, pieces_a, order
    )
    if quick:
        y_b, c_b = after(y_b, saved_a), after(c_b, saved_a)
        pieces_b = [low_b, c_b, y_b, swap(y_b, "narrow", 1)]
    *saved_b, w_b, vec_full, tokens = forward_attention(
        GROUP, place, tokens, tokens_t, mask, vec_full, pieces_b, order
    )
    if quick:
        y_rest, c_rest = after(y_rest, saved_b), after(c_rest, saved_b)
        d_rest = swap(y_rest, "narrow", 1)
        cotangent = turn_cotangent(start, cotangent, [y_rest])
        pieces_rest = [low_rest, c_rest, y_rest, after(d_rest, cotangent)]
    else:
        cotangent = turn_cotangent(start, cotangent, [])
    mixed, d_h1, d_t, vec_sums, *inner = middle(
        place, tokens, cotangent, (saved_a[0], saved_b[0]), vec_full, pieces_rest, order
    )
    sets = [saved_a, saved_b]
    plan = [(pair // GROUP, pair % GROUP, pair) for pair in range(PAIRS)]
    trio_a, vec_sums, *early = backward_attention(
        plan[:FIRST], False, place, mask, tokens_t, vec_sums, sets, d_t, inner, narrow, stages, []
    )
    later = []
    if quick:
        e_keep, e_send = early
        mixed = turn_back(start, mixed, [trio_a])
        e_keep, e_send = fold(e_keep, after(swap(e_send, "narrow", 1), mixed))
        e_arrived = swap(e_send, "narrow", 2)
        later = [e_send]
    trio_b, vec_sums, *late = backward_attention(
        plan[FIRST:], True, place, mask, tokens_t, vec_sums, sets, d_t, [], narrow, stages, later
    )
    weights, trios = (w_a, w_b), (trio_a, trio_b)

    if quick:
        b_keep, b_send = late
        b_arrived = swap(b_send, "narrow", 1)
        e_keep, e_send = fold(e_keep, after(e_arrived, trio_b))
        e_arrived = swap(e_send, "wide", 1)
        b_keep, b_send = fold(b_keep, after(b_arrived, e_send))
        b_arrived = swap(b_send, "narrow", 2)
        input_grad = input_gradient(start, weights, d_h1, trios, [b_send, e_send])
        e_keep, e_send = fold(e_keep, after(e_arrived, input_grad))
        e_arrived = swap(e_send, "wide", 2)
        b_keep, b_send = fold(b_keep, after(b_arrived, e_send))
        b_arrived = swap(b_send, "wide", 1)
        e_keep, e_send = fold(e_keep, after(e_arrived, b_send))
        e_arrived = swap(e_send, "wide", 4)
        b_keep, b_send = fold(b_keep, after(b_arrived, e_send))
        b_arrived = swap(b_send, "wide", 2)
        e_low = add_low(e_keep, after(e_arrived, b_send))
        e_arrived = swap(e_low, "wide", 4)
        b_keep, b_send = fold(b_keep, after(b_arrived, e_low))
        b_arrived = swap(b_send, "wide", 4)
        e_low = join(e_low, after(e_arrived, b_send))
        e_arrived = swap(e_low, "wide", 2)
        b_arrived = after(b_arrived, e_low)
        vec_total = b_keep[:, LATE:].astype(F32) + b_arrived[:, LATE:].astype(F32)
        b_low = add_low(b_keep[:, :LATE], b_arrived[:, :LATE])
        b_arrived = swap(b_low, "wide", 4)
        e_low = join(e_low, after(e_arrived, b_low))
        b_low = join(b_low, after(b_arrived, e_low))
        b_low = join(b_low, swap(b_low, "wide", 2))
        e_arrived, b_arrived = swap(e_low, "wide", 1), swap(b_low, "wide", 1)
        squares = half_squares(place, e_low, b_low, vec_total)
        squares = four(squares, directly(squares, "narrow", (1, 2, 3)))
        squares = squares + swap(squares, "wide", 1)
        grads = [e_low, after(e_arrived, squares), b_low, after(b_arrived, squares)]
    else:
        input_grad, mixed = input_gradient(start, weights, d_h1, trios, []), turn_back(start, mixed, [])
        vec_total = lax.psum_scatter(vec_sums, "narrow", scatter_dimension=1, tiled=True)
        vec_total = lax.psum(vec_total, "wide")
        grads = []
        for every in (early[0], late[0]):
            total = lax.psum_scatter(every, "narrow", scatter_dimension=0, tiled=True)
            grads.append(lax.psum(total.astype(F32), "wide"))
        squares = lax.psum(sum(squares_of(v) for v in grads + [vec_total]), "narrow")
        squares = jnp.full((8, PAIR), squares, F32)
    *updated, grad_norm = adam_step(
        place, squares, math.sqrt(TOK_DEV * wide * narrow), grads, vec_total,
        (w_qkv, w_out, w_up, w_down, vectors),
        (m_qkv, m_out, m_up, m_down, m_vec),
        (v_qkv, v_out, v_up, v_down, v_vec),
        quick,
    )
    return (mixed, input_grad, grad_norm[0, 0], *updated)


def solution(mesh):
    split = P(("wide", "narrow"), None)
    state = (P("narrow", None),) * 4 + (P(None, "narrow"),)
    return jax.shard_map(
        body,
        mesh=mesh,
        in_specs=(split,) * 5 + state * 3,
        out_specs=(split, split, P()) + state * 4,
        check_vma=False,
    )
```

```python
import functools
import math

import jax
import jax.numpy as jnp
from jax import lax
from jax.experimental import pallas as pl
from jax.experimental.pallas import tpu as pltpu
from jax.sharding import PartitionSpec as P

D = 512
HEADS = 8
HEAD_DIM = 64
PAIR = 2 * HEAD_DIM
PAIRS = HEADS // 2
TRIO = 3 * PAIR
TOK_DEV = 1024
QT = 256
HALF = TOK_DEV // 2
TILES = 1
MT = 512
STEP = 10
NORM_EPS = 1e-05
ADAM_EPS = 1e-08
MASKED = -1e30
HIDDEN = 16
BF = jnp.bfloat16
F32 = jnp.float32
MIB = 1024 * 1024
GROUP = 2
HW = GROUP * TRIO
FIRST = 1
LATE = (PAIRS - FIRST) * TRIO
FORWARD_MIB, MIDDLE_MIB, BACKWARD_MIB = 12, 18, 20

NN = (((1,), (0,)), ((), ()))
NT = (((1,), (1,)), ((), ()))
TN = (((0,), (0,)), ((), ()))


def dot(a, b, dims):
    return lax.dot_general(a, b, dims, preferred_element_type=F32)


def params(mib=8):
    return pltpu.CompilerParams(vmem_limit_bytes=mib * MIB)


def sds(shape, dtype):
    return jax.ShapeDtypeStruct(shape, dtype)


SMEM = pl.BlockSpec(memory_space=pltpu.SMEM)
VM = pl.BlockSpec(memory_space=pltpu.VMEM)
ANY = pl.BlockSpec(memory_space=pl.ANY)
HBM = pl.BlockSpec(memory_space=pltpu.HBM)


def whole(shape):
    return pl.BlockSpec(shape, lambda i: (0,) * len(shape))


def cost(flops, moved, exps=0):
    return pl.CostEstimate(flops=int(flops), bytes_accessed=int(moved), transcendentals=int(exps))


def fetch(pairs, sems):
    copies = [
        pltpu.make_async_copy(source, target, sems.at[number])
        for number, (source, target) in enumerate(pairs)
    ]
    for copy in copies:
        copy.start()
    return copies


def trio_columns(base):
    return [
        (local * TRIO + t * PAIR, t * D + (base + local) * PAIR)
        for local in range(GROUP)
        for t in range(3)
    ]


def pack_first_kernel(w_hbm, vec_hbm, out_ref, w_ref, vec_ref, sems):
    rows, vec_cols = w_hbm.shape[0], vec_hbm.shape[1]
    width = GROUP * PAIR
    copies = fetch(
        [(w_hbm.at[:, t * D : t * D + width], w_ref.at[t]) for t in range(3)] + [(vec_hbm, vec_ref)], sems
    )
    for copy in copies:
        copy.wait()
    for local in range(GROUP):
        for t in range(3):
            target = local * TRIO + t * PAIR
            out_ref[:rows, target : target + PAIR] = w_ref[t, :, local * PAIR : (local + 1) * PAIR].astype(BF)
    out_ref[rows:, :] = jnp.zeros((16, HW), BF)
    vec = jnp.concatenate([vec_ref[...], jnp.zeros((7, vec_cols), F32)], 0)
    out_ref[rows:, :vec_cols] = vec.astype(BF)


def pack_first(w_qkv, vectors):
    rows = w_qkv.shape[0]
    return pl.pallas_call(
        pack_first_kernel,
        in_specs=[HBM, HBM],
        out_specs=VM,
        out_shape=sds((rows + 16, HW), BF),
        scratch_shapes=[
            pltpu.VMEM((3, rows, GROUP * PAIR), F32),
            pltpu.VMEM(vectors.shape, F32),
            pltpu.SemaphoreType.DMA((4,)),
        ],
        compiler_params=params(60),
        name="pack_first",
    )(w_qkv, vectors)


def pack_second_kernel(w_ref, w_out_ref, w_up_ref, w_down_ref, *refs):
    second_ref, rest_ref = refs[-2:]
    for target, source in trio_columns(GROUP):
        second_ref[:, target : target + PAIR] = w_ref[:, source : source + PAIR].astype(BF)
    rest_ref[:, :D] = w_out_ref[...].astype(BF)
    rest_ref[:, D : 2 * D] = w_up_ref[...].astype(BF)
    rest_ref[:, 2 * D :] = w_down_ref[...].astype(BF)


def pick(piece, lead, rows):
    return piece[rows, :] if lead is None else piece[lead, rows, :]


def assemble(order, pieces, place, w_full):
    rows = D // len(order)
    for number, (piece, lead, mask) in enumerate(order):
        at = number if mask is None else jnp.bitwise_xor(place[0], mask)
        w_full[pl.ds(pl.multiple_of(at * rows, rows), rows), :] = pick(
            pieces[piece], lead, slice(0, rows)
        )


def turn_rows(source, start, write):
    blocks = source.shape[0] // 8
    whole_blocks, rest = start >> 3, start & 7
    inside = lax.broadcasted_iota(jnp.int32, (8, source.shape[1]), 0) < 8 - rest

    def rolled(block):
        at = pl.multiple_of(((block + whole_blocks) & (blocks - 1)) * 8, 8)
        return pltpu.roll(source[pl.ds(at, 8), :], (8 - rest) & 7, 0)

    def step(i, first):
        second, third = rolled(2 * i + 1), rolled(2 * i + 2)
        write(i, jnp.where(inside, first, second), jnp.where(inside, second, third))
        return third

    lax.fori_loop(0, blocks // 2, step, rolled(0), unroll=8)


def write_into(out):
    def write(i, upper, lower):
        at = pl.multiple_of(i * 16, 16)
        out[pl.ds(at, 16), :] = jnp.concatenate([upper, lower], 0).astype(out.dtype)

    return write


def turn_tokens_kernel(tokens, coded, *refs):
    tokens_out, turned_out, cells_out, start_out, wide_tokens = refs[-5:]
    seen = coded[...] < HIDDEN
    cell = jnp.where(seen, coded[...], coded[...] - HIDDEN)
    start = jnp.int32(TOK_DEV)
    for c in range(4):
        size = jnp.sum((cell == c).astype(jnp.int32))
        first = jnp.sum((cell < c).astype(jnp.int32))
        start = jnp.where(size == HALF, jnp.minimum(start, first), start)
    start_out[0] = start
    shift = jnp.where(start == 0, 0, TOK_DEV - start)
    row = lax.broadcasted_iota(jnp.int32, (8, TOK_DEV), 0)
    cells_out[...] = pltpu.roll(jnp.where((row == 0) | seen, cell, -1), shift, 1)
    wide_tokens[...] = tokens[...].astype(F32)
    turn_rows(wide_tokens, start, write_into(tokens_out))
    turned_out[...] = tokens_out[...].T


def turn_tokens(tokens, coded):
    return pl.pallas_call(
        turn_tokens_kernel,
        in_specs=[VM, VM],
        out_specs=[VM] * 3 + [SMEM],
        out_shape=[
            sds((TOK_DEV, D), BF),
            sds((D, TOK_DEV), BF),
            sds((8, TOK_DEV), jnp.int32),
            sds((1,), jnp.int32),
        ],
        scratch_shapes=[pltpu.VMEM((TOK_DEV, D), F32)],
        compiler_params=params(),
        cost_estimate=cost(1e7, 3e6),
        name="turn_tokens",
    )(tokens, coded)


def turn_cotangent_kernel(start, cot_ref, *refs):
    turn_rows(cot_ref, start[0], write_into(refs[-1]))


def turn_cotangent(start, cot, later):
    return pl.pallas_call(
        turn_cotangent_kernel,
        in_specs=[SMEM, VM] + [ANY] * len(later),
        out_specs=VM,
        out_shape=sds((TOK_DEV, D), F32),
        compiler_params=params(),
        cost_estimate=cost(1e7, 4e6),
        name="turn_cotangent",
    )(start, cot, *later)


def turn_back_kernel(start, source, *refs):
    turned, wide_source = refs[-2:]
    back = (TOK_DEV - start[0]) & (TOK_DEV - 1)
    if source.dtype == F32:
        turn_rows(source, back, write_into(turned))
    else:
        wide_source[...] = source[...].astype(F32)
        turn_rows(wide_source, back, write_into(turned))


def turn_back(start, value, later):
    scratch = (8, PAIR) if value.dtype == F32 else value.shape
    return pl.pallas_call(
        turn_back_kernel,
        in_specs=[SMEM, VM] + [ANY] * len(later),
        out_specs=VM,
        out_shape=sds(value.shape, value.dtype),
        scratch_shapes=[pltpu.VMEM(scratch, F32)],
        compiler_params=params(),
        cost_estimate=cost(1, 1),
        name="turn_back",
    )(start, value, *later)


def make_bias(cells_ref, bias):
    for half in range(2):
        mine = slice(half * HALF, (half + 1) * HALF)
        number = lax.broadcasted_iota(jnp.int32, (16, HALF), 0)
        of_key = jnp.where(cells_ref[1:2, mine] == number, 1.0, 0.0).astype(BF)
        of_query = jnp.where(cells_ref[0:1, mine] == number, 1.0, 0.0).astype(BF)
        keys = lax.broadcasted_iota(jnp.int32, (HALF, HALF), 0)
        queries = lax.broadcasted_iota(jnp.int32, (HALF, HALF), 1)
        seen = (dot(of_key, of_query, TN) > 0.5) | (keys == queries)
        bias[mine, :] = jnp.where(seen, 0.0, MASKED).astype(BF)


def column_of(row):
    eye = lax.broadcasted_iota(jnp.int32, (PAIR, PAIR), 0) == lax.broadcasted_iota(
        jnp.int32, (PAIR, PAIR), 1
    )
    return jnp.sum(jnp.where(eye, row, 0.0), 1, keepdims=True)


def both_heads(pair_t):
    zero = jnp.zeros((HEAD_DIM, pair_t.shape[1]), pair_t.dtype)
    return jnp.concatenate(
        [
            jnp.concatenate([pair_t[:HEAD_DIM], zero], 0),
            jnp.concatenate([zero, pair_t[HEAD_DIM:]], 0),
        ],
        1,
    )


def forward_kernel(order, n_pieces, base, *refs):
    place, tokens, tokens_t, bias, vec_in = refs[:5]
    pieces = refs[5 : 5 + n_pieces]
    att_out, lse_out, krow_out, vrow_out, qt_out, kt_out, w_full, vec_full, tokens_out = refs[
        5 + n_pieces : 14 + n_pieces
    ]
    if base == 0:
        make_bias(bias, refs[-1])
        bias = refs[-1]
    assemble(order, pieces, place, w_full)
    if vec_in.shape[1] == D:
        vec_full[...] = vec_in[...].astype(F32)
    else:
        rows = D // len(order)
        for piece, lead, mask in order:
            at = pl.multiple_of(jnp.bitwise_xor(place[0], mask) * rows, rows)
            vec_full[:, pl.ds(at, rows)] = pick(pieces[piece], lead, slice(rows, rows + 16))[
                :, :rows
            ].astype(F32)
    x = tokens[...]
    tokens_out[...] = x
    halves = [slice(0, HALF), slice(HALF, TOK_DEV)]
    chains = []
    for local in range(GROUP):
        lane = slice((base + local) * PAIR, (base + local + 1) * PAIR)
        w = w_full[:, local * TRIO : (local + 1) * TRIO]
        b_q = vec_full[0:1, lane]
        b_v = vec_full[1:2, lane]
        trio = dot(w, tokens_t[...], TN)
        rows = dot(x, w[:, PAIR:], NN)
        here = slice(local * PAIR, (local + 1) * PAIR)
        q_t = ((trio[:PAIR] + column_of(b_q)) * (HEAD_DIM**-0.5)).astype(BF)
        v_t = (trio[2 * PAIR :] + column_of(b_v)).astype(BF)
        k_row = rows[:, :PAIR].astype(BF)
        krow_out[local] = k_row
        vrow_out[local] = (rows[:, PAIR:] + b_v).astype(BF)
        qt_out[here, :] = q_t
        kt_out[here, :] = trio[PAIR : 2 * PAIR].astype(BF)
        chains += [(local, mine, q_t, v_t, k_row) for mine in halves]

    def scores(chain):
        local, mine, q_t, v_t, k_row = chain
        return dot(k_row[mine], both_heads(q_t[:, mine]), NN)

    ahead = scores(chains[0])
    for number, (local, mine, q_t, v_t, k_row) in enumerate(chains):
        s = ahead
        if number + 1 < len(chains):
            ahead = scores(chains[number + 1])
        mask = bias[mine, :].astype(F32)
        s = s + jnp.concatenate([mask, mask], 1)
        top = jnp.max(s, 0, keepdims=True)
        e = jnp.exp(s - top)
        total = jnp.sum(e, 0, keepdims=True)
        lse = top + jnp.log(total)
        e_low = e.astype(BF)
        for h in range(2):
            cols = slice(h * HALF, (h + 1) * HALF)
            head = slice(h * HEAD_DIM, (h + 1) * HEAD_DIM)
            o = dot(v_t[head, mine], e_low[:, cols], NN)
            at = local * PAIR + h * HEAD_DIM
            att_out[at : at + HEAD_DIM, mine] = (o / total[:, cols]).astype(BF)
            lse_out[local, h : h + 1, mine] = lse[:, cols]


def forward_attention(base, place, tokens, tokens_t, cells, vec, pieces, order):
    mask = [] if base else [sds((TOK_DEV, HALF), BF)]
    wide_t, tall = sds((GROUP * PAIR, TOK_DEV), BF), sds((GROUP, TOK_DEV, PAIR), BF)
    return pl.pallas_call(
        functools.partial(forward_kernel, order, len(pieces), base),
        in_specs=[SMEM] + [VM] * (4 + len(pieces)),
        out_specs=[VM] * (9 + len(mask)),
        out_shape=[
            wide_t, sds((GROUP, 8, TOK_DEV), F32), tall, tall, wide_t, wide_t, sds((D, HW), BF), sds((16, D), F32),
            sds((TOK_DEV, D), BF),
        ]
        + mask,
        compiler_params=params(FORWARD_MIB),
        cost_estimate=cost(1, 1),
        name="forward_attention",
    )(place, tokens, tokens_t, cells, vec, *pieces)


def normalize(value):
    center = value - jnp.mean(value, -1, keepdims=True)
    inverse = lax.rsqrt(jnp.mean(center * center, -1, keepdims=True) + NORM_EPS)
    return center * inverse, inverse


def normalize_back(grad, normal, inverse):
    return inverse * (
        grad
        - jnp.mean(grad, -1, keepdims=True)
        - normal * jnp.mean(grad * normal, -1, keepdims=True)
    )


def column_sum(value):
    return jnp.sum(value, 0, keepdims=True)


def row_sources(place, n_shards, stages):
    if not stages:
        return [(0, 0, D)]
    rows = D // n_shards
    piece = D >> len(stages)
    found = []
    for block in range(1 << len(stages)):
        masks = {"narrow": 0, "wide": 0}
        for number, (axis, mask) in enumerate(stages):
            if block >> (len(stages) - 1 - number) & 1:
                masks[axis] |= mask
        source = jnp.bitwise_xor(place[0], masks["narrow"]) * rows
        if piece < rows:
            source = source + jnp.bitwise_xor(place[1], masks["wide"]) * piece
        found.append((block * piece, pl.multiple_of(source, piece), piece))
    return found


def store_rows(outs, place, n_shards, stages, matrix, cols):
    height = outs[0].shape[0]
    for target, source, rows in row_sources(place, n_shards, stages):
        out = outs[target // height]
        at = target % height
        out[at : at + rows, cols] = matrix[pl.ds(source, rows), :].astype(BF)


def gelu_parts(value):
    density = jnp.exp(-0.5 * value * value)
    t = 1.0 / (1.0 + (0.3275911 / math.sqrt(2.0)) * jnp.abs(value))
    poly = 1.061405429
    for factor in (-1.453152027, 1.421413741, -0.284496736, 0.254829592):
        poly = poly * t + factor
    tail = 0.5 * poly * t * density
    return jnp.where(value >= 0.0, 1.0 - tail, tail), value * density * (1.0 / math.sqrt(2.0 * math.pi))


def middle_kernel(order, n_pieces, *refs):
    place, tokens, cot_ref, att_a, att_b, vec_ref = refs[:6]
    pieces = refs[6 : 6 + n_pieces]
    mixed_out, dh1_out, datt_out, vec_out = refs[6 + n_pieces : 10 + n_pieces]
    first_all, hidden_all, branch_all, pre_all, down_all = refs[10 + n_pieces : 15 + n_pieces]
    w_full, sums = refs[15 + n_pieces :]
    step = pl.program_id(0)

    @pl.when(step == 0)
    def _():
        assemble(order, pieces, place, w_full)
        sums[...] = jnp.zeros_like(sums)

    w_out, w_up, w_down = w_full[:, :D], w_full[:, D : 2 * D], w_full[:, 2 * D :]

    def vec(row):
        return vec_ref[row : row + 1, :]

    def tile(number):
        at = pl.ds(pl.multiple_of(step * (TILES * MT) + number * MT, MT), MT)
        att_t = jnp.concatenate([att_a[:, at], att_b[:, at]], 0)
        branch = dot(att_t, w_out, TN)
        yield
        normal_1, inverse_1 = normalize(tokens[at, :].astype(F32) + (branch + vec(2)))
        first = normal_1 * vec(5) + vec(6)
        first_low = first.astype(BF)
        first_all[at, :] = first_low
        pre = dot(first_low, w_up, NN)
        yield
        pre = pre + vec(3)
        cdf, bump = gelu_parts(pre)
        hidden = (pre * cdf).astype(BF)
        hidden_all[at, :] = hidden
        slope = cdf + bump
        down = dot(hidden, w_down, NN)
        yield
        normal_2, inverse_2 = normalize(first + (down + vec(4)))
        mixed_out[at, :] = (normal_2 * vec(7) + vec(8)).astype(BF)
        cot = cot_ref[at, :]
        d_h2 = normalize_back(cot * vec(7), normal_2, inverse_2)
        d_down = d_h2.astype(BF)
        down_all[at, :] = d_down
        d_hidden = dot(d_down, w_down, NT)
        yield
        sums[7:8, :] += column_sum(cot * normal_2)
        sums[8:9, :] += column_sum(cot)
        d_pre = (d_hidden * slope).astype(BF)
        pre_all[at, :] = d_pre
        d_up = dot(d_pre, w_up, NT)
        yield
        d_first = d_h2 + d_up
        d_h1 = normalize_back(d_first * vec(5), normal_1, inverse_1)
        dh1_out[at, :] = d_h1
        d_branch = d_h1.astype(BF)
        branch_all[at, :] = d_branch
        datt_out[:, at] = dot(w_out, d_branch, NT).astype(BF)
        yield
        sums[5:6, :] += column_sum(d_first * normal_1)
        sums[6:7, :] += column_sum(d_first)

    tiles = [tile(number) for number in range(TILES)]
    while tiles:
        tiles = [one for one in tiles if next(one, True) is None]

    @pl.when(step == pl.num_programs(0) - 1)
    def _():
        ones = jnp.ones((16, TOK_DEV), BF)
        sums[2:3, :] = dot(ones, branch_all[...], NN)[:1]
        sums[3:4, :] = dot(ones, pre_all[...], NN)[:1]
        sums[4:5, :] = dot(ones, down_all[...], NN)[:1]
        vec_out[...] = sums[...]


def middle(place, tokens, cot, atts, vec, pieces, order):
    height = TILES * MT
    return pl.pallas_call(
        functools.partial(middle_kernel, order, len(pieces)),
        grid=(TOK_DEV // height,),
        in_specs=[SMEM] + [VM] * (5 + len(pieces)),
        out_specs=[VM] * 9,
        out_shape=[
            sds((TOK_DEV, D), BF),
            sds((TOK_DEV, D), F32),
            sds((D, TOK_DEV), BF),
            sds((16, D), F32),
        ]
        + [sds((TOK_DEV, D), BF)] * 5,
        scratch_shapes=[pltpu.VMEM((D, 3 * D), BF), pltpu.VMEM((16, D), F32)],
        compiler_params=params(MIDDLE_MIB),
        cost_estimate=cost(1e10, 1.2e7, 2**20),
        name="middle",
    )(place, tokens, cot, *atts, vec, *pieces)


def backward_kernel(n_shards, stages, plan, n_sets, n_inner, last, place, bias, tokens_t, vec_ref,
                    datt_ref, *refs):
    sets = [refs[6 * number : 6 * (number + 1)] for number in range(n_sets)]
    inner = refs[6 * n_sets : 6 * n_sets + n_inner]
    dw = refs[-1]
    n_g = 2 if stages else 1
    d_out, vec = refs[-3 - n_g : -1 - n_g]
    g_outs = refs[-1 - n_g : -1]
    vec[...] = vec_ref[...]
    halves = [slice(0, HALF), slice(HALF, TOK_DEV)]
    chains = [(place_out, *entry, mine) for place_out, entry in enumerate(plan) for mine in halves]

    def scores(chain):
        _, number, local, pair, mine = chain
        att_ref, lse_ref, krow_ref, vrow_ref, qt_ref, kt_ref = sets[number]
        here = slice(local * PAIR, (local + 1) * PAIR)
        q_t, d_t = qt_ref[here, mine], datt_ref[pair * PAIR : (pair + 1) * PAIR, mine]
        s = dot(krow_ref[local, mine, :], both_heads(q_t), NN)
        return q_t, d_t, s, dot(vrow_ref[local, mine, :], both_heads(d_t), NN)

    first = 0
    if inner:
        first = 3 * D
        first_all, hidden_all, branch_all, pre_all, down_all = inner
        attended = jnp.concatenate([sets[0][0][...], sets[1][0][...]], 0)
        products = [
            dot(attended, branch_all[...], NN),
            dot(first_all[...], pre_all[...], TN),
            dot(hidden_all[...], down_all[...], TN),
        ]
        for number, product in enumerate(products):
            dw[number % 2] = product
            cols = slice(number * D, (number + 1) * D)
            store_rows(g_outs, place, n_shards, stages, dw.at[number % 2], cols)
    ahead = scores(chains[0])
    for step, (place_out, number, local, pair, mine) in enumerate(chains):
        q_t, d_t, s, d_prob = ahead
        if step + 1 < len(chains):
            ahead = scores(chains[step + 1])
        att_ref, lse_ref, krow_ref, vrow_ref, qt_ref, kt_ref = sets[number]
        mask = bias[mine, :].astype(F32)
        lse = jnp.concatenate([lse_ref[local, 0:1, mine], lse_ref[local, 1:2, mine]], 1)
        here = slice(local * PAIR, (local + 1) * PAIR)
        product = d_t.astype(F32) * att_ref[here, mine].astype(F32)
        delta = jnp.concatenate([column_sum(product[:HEAD_DIM]), column_sum(product[HEAD_DIM:])], 1)
        prob = jnp.exp(s + jnp.concatenate([mask, mask], 1) - lse)
        d_s = (prob * (d_prob - delta)).astype(BF)
        prob_low = prob.astype(BF)
        for h in range(2):
            cols = slice(h * HALF, (h + 1) * HALF)
            head = slice(h * HEAD_DIM, (h + 1) * HEAD_DIM)
            k_t = kt_ref[local * PAIR + h * HEAD_DIM : local * PAIR + (h + 1) * HEAD_DIM, mine]
            d_q = dot(k_t, d_s[:, cols], NN) * (HEAD_DIM**-0.5)
            d_k = dot(q_t[head], d_s[:, cols], NT)
            d_v = dot(d_t[head], prob_low[:, cols], NT)
            for t, value in enumerate((d_q, d_k, d_v)):
                at = t * PAIR + h * HEAD_DIM
                d_out[place_out, at : at + HEAD_DIM, mine] = value.astype(BF)
        if mine.start == 0:
            continue
        trio = d_out[place_out]
        dw[place_out % 2, :, :TRIO] = dot(tokens_t[...], trio, NT)
        at = first + place_out * TRIO
        store_rows(
            g_outs, place, n_shards, stages, dw.at[place_out % 2, :, :TRIO], slice(at, at + TRIO)
        )
        total = dot(jnp.ones((16, TOK_DEV), BF), trio, NT)
        lanes = slice(pair * PAIR, (pair + 1) * PAIR)
        vec[0:1, lanes] = total[:1, :PAIR]
        vec[1:2, lanes] = total[:1, 2 * PAIR :]
    if stages and last:
        height = g_outs[0].shape[0]
        rows = D // n_shards
        for target, source, count in row_sources(place, n_shards, stages):
            at = pl.multiple_of(source // rows * rows, rows)
            g_outs[target // height][target % height : target % height + count, LATE:] = vec[
                :, pl.ds(at, rows)
            ].astype(BF)


def backward_attention(plan, last, place, mask, tokens_t, vec_sums, sets, d_t, inner, n_shards, stages, later):
    width = len(plan) * TRIO + (3 * D if inner else 0)
    if stages:
        shapes = [sds((D // 2, width + (PAIR if last else 0)), BF)] * 2
    else:
        shapes = [sds((D, width), BF)]
    flat = [value for saved in sets for value in saved]
    return pl.pallas_call(
        functools.partial(backward_kernel, n_shards, stages, plan, len(sets), len(inner), last),
        in_specs=[SMEM] + [VM] * (4 + len(flat) + len(inner)) + [ANY] * len(later),
        out_specs=[VM] * (2 + len(shapes)),
        out_shape=[sds((len(plan), TRIO, TOK_DEV), BF), sds((16, D), F32)] + shapes,
        scratch_shapes=[pltpu.VMEM((2, D, D), F32)],
        compiler_params=params(BACKWARD_MIB),
        cost_estimate=cost(5e9 * len(plan), 8e6, 2**21),
        name="backward_attention",
    )(place, mask, tokens_t, vec_sums, d_t, *flat, *inner, *later)


def input_grad_kernel(start, w_a, w_b, dh1_ref, trio_a, trio_b, *refs):
    out, turned = refs[-2:]
    trios = [ref.at[number] for ref in (trio_a, trio_b) for number in range(ref.shape[0])]
    for tile in range(TOK_DEV // QT):
        here = slice(tile * QT, (tile + 1) * QT)
        total = None
        for w_ref, parts in ((w_a, trios[:GROUP]), (w_b, trios[GROUP:])):
            term = dot(w_ref[...], jnp.concatenate([part[:, here] for part in parts], 0), NN)
            total = term if total is None else total + term
        turned[here, :] = dh1_ref[here, :] + total.T
    turn_rows(turned, (TOK_DEV - start[0]) & (TOK_DEV - 1), write_into(out))


def input_gradient(start, weights, d_h1, trios, later):
    return pl.pallas_call(
        input_grad_kernel,
        in_specs=[SMEM] + [VM] * 5 + [ANY] * len(later),
        out_specs=VM,
        out_shape=sds((TOK_DEV, D), F32),
        scratch_shapes=[pltpu.VMEM((TOK_DEV, D), F32)],
        compiler_params=params(),
        cost_estimate=cost(1, 1),
        name="input_gradient",
    )(start, *weights, d_h1, *trios, *later)


def adam(weight, grad, first, second, rate, decay):
    first = 0.5 * first + 0.5 * grad
    second = 0.5 * second + 0.5 * grad * grad
    fix = 1.0 - 0.5**STEP
    fixed = second * (1.0 / fix)
    update = first * (1.0 / fix) / (fixed * lax.rsqrt(fixed) + ADAM_EPS)
    return weight - rate * (update + decay * weight), first, second


def pair_parts(first, pairs):
    return [
        (slice(at, at + PAIR), 0, t * D + pair * PAIR)
        for number, pair in enumerate(pairs)
        for t in range(3)
        for at in [first + number * TRIO + t * PAIR]
    ]


EARLY_PARTS = [(slice(i * D, (i + 1) * D), i + 1, 0) for i in range(3)] + pair_parts(3 * D, range(FIRST))
LATE_PARTS = pair_parts(0, range(FIRST, PAIRS))


def adam_kernel(quick, limit, place, square_ref, *refs):
    n_grads = 4 if quick else 2
    grads = refs[:n_grads]
    vec_ref = refs[n_grads]
    states = refs[n_grads + 1 : n_grads + 16]
    outs = refs[n_grads + 16 : n_grads + 36]
    norm_out = refs[-1]
    step = pl.program_id(0)
    norm = jnp.sqrt(square_ref[0:1, 0:1])
    factor = limit / jnp.maximum(norm, limit)

    def write(number, where, target, grad, rate, decay):
        new, first, second = adam(
            states[number][where], grad * factor, states[5 + number][where],
            states[10 + number][where], rate, decay,
        )
        outs[number][target] = new
        outs[5 + number][target] = first
        outs[10 + number][target] = second
        outs[15 + number][target] = new.astype(BF)

    height = outs[0].shape[0]
    pieces = height // 16 if quick else 1
    rows = height // pieces
    for piece in range(pieces):
        here = pl.multiple_of(step * height + piece * rows, rows)
        if quick:
            mask = jnp.bitwise_xor(place[1], step * pieces + piece)
            at = pl.multiple_of(((mask >> 2) & 1) * 16 + ((mask >> 1) & 1) * 32, 16)
            odd = (mask & 1) == 1
        else:
            at = here
        for group, parts in enumerate((EARLY_PARTS, LATE_PARTS)):
            for cols, number, first in parts:
                if quick:
                    low, high = grads[2 * group], grads[2 * group + 1]
                    grad = jnp.where(odd, high[pl.ds(at, rows), cols], low[pl.ds(at, rows), cols])
                else:
                    grad = grads[group][pl.ds(at, rows), cols]
                there = slice(first, first + cols.stop - cols.start)
                write(
                    number, (pl.ds(here, rows), there), (slice(piece * rows, (piece + 1) * rows), there),
                    grad.astype(F32), 0.1, 0.01,
                )

    @pl.when(step == 0)
    def _():
        norm_out[0, 0] = norm[0, 0]
        vec_cols = states[4].shape[1]
        where = (slice(0, 9), slice(0, vec_cols))
        write(4, where, where, vec_ref[0:9, :vec_cols].astype(F32), 0.5, 0.0)


def adam_step(place, squares, limit, grads, vec_grad, weights, firsts, seconds, quick):
    steps = 2

    def spec(value):
        if value.shape[0] == 9:
            return whole(value.shape)
        return pl.BlockSpec((value.shape[0] // steps, value.shape[1]), lambda i: (i, 0))

    state = [spec(w) for w in weights]
    shapes = [sds(w.shape, F32) for w in weights]
    return pl.pallas_call(
        functools.partial(adam_kernel, quick, limit),
        grid=(steps,),
        in_specs=[SMEM] + [VM] * (17 + len(grads)),
        out_specs=state * 4 + [SMEM],
        out_shape=shapes * 3 + [sds(w.shape, BF) for w in weights] + [sds((1, 1), F32)],
        compiler_params=params(),
        name="adam",
    )(place, squares, *grads, vec_grad, *weights, *firsts, *seconds)


def swap(value, axis, mask):
    size = lax.axis_size(axis)
    return lax.ppermute(value, axis, [(i, i ^ mask) for i in range(size)])


def add_low(a, b):
    return (a.astype(F32) + b.astype(F32)).astype(BF)


def after(value, *others):
    return lax.optimization_barrier((value, others))[0]


def fold(keep, arrived):
    rows = keep.shape[0] // 2
    send = add_low(keep[rows:], arrived[rows:])
    return add_low(keep[:rows], arrived[:rows]), send


def squares_kernel(place, early, late, vec, out):
    total = []
    for piece in range(4):
        rows = slice(16 * piece, 16 * (piece + 1))
        first, second = early[rows, :].astype(F32), late[rows, :].astype(F32)
        total.append(jnp.sum(first * first) + jnp.sum(second * second))
    total = (total[0] + total[1]) + (total[2] + total[3])
    total = total + jnp.where((place[1] & 1) == 0, jnp.sum(vec[...] * vec[...]), 0.0)
    out[...] = jnp.full(out.shape, total, F32)


def half_squares(place, early, late, vec):
    return pl.pallas_call(
        squares_kernel,
        in_specs=[SMEM] + [VM] * 3,
        out_specs=VM,
        out_shape=sds((8, PAIR), F32),
        compiler_params=params(),
        cost_estimate=cost(1, 1),
        name="half_squares",
    )(place, early, late, vec)


def directly(value, axis, masks):
    return [swap(value, axis, mask) for mask in masks]


def four(value, others):
    return (value + others[0]) + (others[1] + others[2])


def join(held, arrived):
    return jnp.concatenate([held, arrived], 0)


def squares_of(value):
    value = value.astype(F32)
    return jnp.sum(value * value)


STAGES = (("narrow", 1), ("narrow", 2), ("wide", 1), ("wide", 2), ("wide", 4))


def body(
    tokens, cotangent, cells, present, generate,
    w_qkv, w_out, w_up, w_down, vectors,
    m_qkv, m_out, m_up, m_down, m_vec,
    v_qkv, v_out, v_up, v_down, v_vec,
):
    narrow, wide = lax.axis_size("narrow"), lax.axis_size("wide")
    quick = narrow == 4 and wide == 8
    stages = STAGES if quick else ()
    place = jnp.stack([lax.axis_index("narrow"), lax.axis_index("wide")]).astype(jnp.int32)
    shard = w_qkv.shape[0]

    low_a = pack_first(w_qkv, vectors)
    coded = jnp.where((present == 1) & (generate == 0), cells, cells + HIDDEN)
    tokens, tokens_t, cells, start = turn_tokens(tokens, after(coded, low_a))
    low_b, low_rest = pl.pallas_call(
        pack_second_kernel,
        in_specs=[VM] * 4 + [ANY],
        out_specs=[VM, VM],
        out_shape=[sds((shard, HW), BF), sds((shard, 3 * D), BF)],
        compiler_params=params(),
        name="pack_second",
    )(w_qkv, w_out, w_up, w_down, cells)
    if quick:
        y_a = after(swap(low_a, "narrow", 2), low_b)
        pieces_a = [low_a, swap(low_a, "narrow", 1), y_a, swap(y_a, "narrow", 1)]
        y_b = swap(after(low_b, y_a), "narrow", 2)
        c_b = swap(low_b, "narrow", 1)
        y_rest = swap(after(low_rest, y_a), "narrow", 2)
        c_rest = swap(low_rest, "narrow", 1)
        order = [(j, None, j) for j in range(4)]
        vec = jnp.zeros((8, PAIR), BF)
    else:
        pieces_a, pieces_b = [lax.all_gather(low_a, "narrow")], [lax.all_gather(low_b, "narrow")]
        pieces_rest = [lax.all_gather(low_rest, "narrow")]
        order = [(0, j, None) for j in range(narrow)]
        vec = lax.all_gather(vectors.astype(BF), "narrow", axis=1, tiled=True)
        vec = jnp.pad(vec, ((0, 7), (0, 0)))

    *saved_a, w_a, vec_full, tokens, mask = forward_attention(
        0, place, tokens, tokens_t, cells, vec, pieces_a, order
    )
    if quick:
        y_b, c_b = after(y_b, saved_a), after(c_b, saved_a)
        pieces_b = [low_b, c_b, y_b, swap(y_b, "narrow", 1)]
    *saved_b, w_b, vec_full, tokens = forward_attention(
        GROUP, place, tokens, tokens_t, mask, vec_full, pieces_b, order
    )
    if quick:
        y_rest, c_rest = after(y_rest, saved_b), after(c_rest, saved_b)
        d_rest = swap(y_rest, "narrow", 1)
        cotangent = turn_cotangent(start, cotangent, [y_rest])
        pieces_rest = [low_rest, c_rest, y_rest, after(d_rest, cotangent)]
    else:
        cotangent = turn_cotangent(start, cotangent, [])
    mixed, d_h1, d_t, vec_sums, *inner = middle(
        place, tokens, cotangent, (saved_a[0], saved_b[0]), vec_full, pieces_rest, order
    )
    sets = [saved_a, saved_b]
    plan = [(pair // GROUP, pair % GROUP, pair) for pair in range(PAIRS)]
    trio_a, vec_sums, *early = backward_attention(
        plan[:FIRST], False, place, mask, tokens_t, vec_sums, sets, d_t, inner, narrow, stages, []
    )
    later = []
    if quick:
        e_keep, e_send = early
        mixed = turn_back(start, mixed, [trio_a])
        e_keep, e_send = fold(e_keep, after(swap(e_send, "narrow", 1), mixed))
        e_arrived = swap(e_send, "narrow", 2)
        later = [e_send]
    trio_b, vec_sums, *late = backward_attention(
        plan[FIRST:], True, place, mask, tokens_t, vec_sums, sets, d_t, [], narrow, stages, later
    )
    weights, trios = (w_a, w_b), (trio_a, trio_b)

    if quick:
        b_keep, b_send = late
        b_arrived = swap(b_send, "narrow", 1)
        e_keep, e_send = fold(e_keep, after(e_arrived, trio_b))
        e_arrived = swap(e_send, "wide", 1)
        b_keep, b_send = fold(b_keep, after(b_arrived, e_send))
        b_arrived = swap(b_send, "narrow", 2)
        input_grad = input_gradient(start, weights, d_h1, trios, [b_send, e_send])
        e_keep, e_send = fold(e_keep, after(e_arrived, input_grad))
        e_arrived = swap(e_send, "wide", 2)
        b_keep, b_send = fold(b_keep, after(b_arrived, e_send))
        b_arrived = swap(b_send, "wide", 1)
        e_keep, e_send = fold(e_keep, after(e_arrived, b_send))
        e_arrived = swap(e_send, "wide", 4)
        b_keep, b_send = fold(b_keep, after(b_arrived, e_send))
        b_arrived = swap(b_send, "wide", 2)
        e_low = add_low(e_keep, after(e_arrived, b_send))
        e_arrived = swap(e_low, "wide", 4)
        b_keep, b_send = fold(b_keep, after(b_arrived, e_low))
        b_arrived = swap(b_send, "wide", 4)
        e_low = join(e_low, after(e_arrived, b_send))
        e_arrived = swap(e_low, "wide", 2)
        b_arrived = after(b_arrived, e_low)
        vec_total = b_keep[:, LATE:].astype(F32) + b_arrived[:, LATE:].astype(F32)
        b_low = add_low(b_keep[:, :LATE], b_arrived[:, :LATE])
        b_arrived = swap(b_low, "wide", 4)
        e_low = join(e_low, after(e_arrived, b_low))
        b_low = join(b_low, after(b_arrived, e_low))
        b_low = join(b_low, swap(b_low, "wide", 2))
        e_arrived, b_arrived = swap(e_low, "wide", 1), swap(b_low, "wide", 1)
        squares = half_squares(place, e_low, b_low, vec_total)
        squares = four(squares, directly(squares, "narrow", (1, 2, 3)))
        squares = squares + swap(squares, "wide", 1)
        grads = [e_low, after(e_arrived, squares), b_low, after(b_arrived, squares)]
    else:
        input_grad, mixed = input_gradient(start, weights, d_h1, trios, []), turn_back(start, mixed, [])
        vec_total = lax.psum_scatter(vec_sums, "narrow", scatter_dimension=1, tiled=True)
        vec_total = lax.psum(vec_total, "wide")
        grads = []
        for every in (early[0], late[0]):
            total = lax.psum_scatter(every, "narrow", scatter_dimension=0, tiled=True)
            grads.append(lax.psum(total.astype(F32), "wide"))
        squares = lax.psum(sum(squares_of(v) for v in grads + [vec_total]), "narrow")
        squares = jnp.full((8, PAIR), squares, F32)
    *updated, grad_norm = adam_step(
        place, squares, math.sqrt(TOK_DEV * wide * narrow), grads, vec_total,
        (w_qkv, w_out, w_up, w_down, vectors),
        (m_qkv, m_out, m_up, m_down, m_vec),
        (v_qkv, v_out, v_up, v_down, v_vec),
        quick,
    )
    return (mixed, input_grad, grad_norm[0, 0], *updated)


def solution(mesh):
    split = P(("wide", "narrow"), None)
    state = (P("narrow", None),) * 4 + (P(None, "narrow"),)
    return jax.shard_map(
        body,
        mesh=mesh,
        in_specs=(split,) * 5 + state * 3,
        out_specs=(split, split, P()) + state * 4,
        check_vma=False,
    )
```
